32 devices in a mesh: dp: 4 (over z), section: 2 (over core), mp: 4 (over y, x).
Axes of the slice: x: 2, y: 2, z: 4, core: 2. Of those that a mesh axis runs over, the one named last changes fastest.
Arguments:
- frames: bfloat16 [4, 128, 512], P('dp'), may hold values from -6 to 6
- lengths: int32 [4], P('dp'), may hold values from 32 to 128
- feature_proj: bfloat16 [512, 1920], P(None, 'mp'), may hold values from -0.25 to 0.25
- norm_gain: float32 [2, 1920], P('section'), may hold values from 0.25 to 1.75
- qkv_weight: bfloat16 [2, 1920, 5760], P('section', 'dp', 'mp'), may hold values from -0.125 to 0.125
- out_weight: bfloat16 [2, 1920, 1920], P('section', 'mp', 'dp'), may hold values from -0.125 to 0.125
- center: float32 [1920], replicated, may hold values from -4 to 4
- whitening: float32 [1920, 1024], P(None, 'dp'), may hold values from -0.125 to 0.125
Outputs:
- embeddings: float32 [4, 1024], P(None, 'dp')
The draws below stay inside these ranges and needn't reach their ends.
All inputs are finite; a program needn't handle non-finite values.
Results may differ from the reference program's by a relative error of at most 0.0095.
Values may be sent and summed in bfloat16 or wider, within the bound.
A program may use at most 64 MiB of HBM per device.

```python
import jax
import jax.numpy as jnp
from jax import lax

D = 1920
H = 16
HD = 120
CIN = 512
OUT = 1024
F = 128
UTTS = 4
N_MP = 4


def with_ends(array, rng, smallest, largest):
    longest = array.shape.index(max(array.shape))
    spots = []
    for shift in (0, 1):
        where = [jax.random.randint(jax.random.fold_in(rng, axis), (), 0, length) for axis, length in enumerate(array.shape)]
        where[longest] = (where[longest] + shift) % array.shape[longest]
        spots.append(tuple(where))
    return array.at[spots[0]].set(smallest).at[spots[1]].set(largest)


def levels(key, shape, cuts, smallest, top_value):
    level, own = 1.0, jax.random.fold_in(key, 6)
    for position, blocks in cuts:
        heights = jnp.exp(jax.random.uniform(jax.random.fold_in(own, position), (blocks,), jnp.float32, smallest / len(cuts), top_value / len(cuts)))
        level = level * jnp.repeat(heights, shape[position] // blocks).reshape([-1 if axis == position else 1 for axis in range(len(shape))])
    return level


def noise(rng, extent, deviation, reach, pieces=(), kind=jnp.bfloat16):
    level = levels(rng, extent, pieces, -0.22, 0.18) if pieces else 1.0
    drawn = jax.random.normal(rng, extent, jnp.float32) * deviation * level
    return jnp.minimum(jnp.maximum(drawn, -reach), reach).astype(kind)


def setup_inputs(seed: int = 0) -> dict:
    splits = jax.random.split(jax.random.key(seed), 9)
    return {
        "frames": noise(splits[0], (UTTS, F, CIN), 1.0, 6.0, ((0, 4),)),
        "lengths": with_ends(jax.random.randint(splits[1], (UTTS,), F // 4, F + 1), jax.random.fold_in(splits[1], 1), F // 4, F).astype(jnp.int32),
        "feature_proj": noise(splits[2], (CIN, D), CIN ** -0.5, 0.25, ((1, 4),)),
        "norm_gain": jnp.clip(1.0 + 0.15 * jax.random.normal(splits[3], (2, D), jnp.float32), 0.25, 1.75),
        "qkv_weight": noise(splits[4], (2, D, 3 * D), D ** -0.5, 0.125, ((0, 2), (1, 4), (2, 4))),
        "out_weight": noise(splits[5], (2, D, D), D ** -0.5, 0.125, ((0, 2), (1, 4), (2, 4))),
        "center": noise(splits[6], (D,), 1.0, 4.0, (), jnp.float32),
        "whitening": noise(splits[7], (D, OUT), D ** -0.5, 0.125, ((1, 4),), jnp.float32),
    }


def layer_norm(values, gain):
    mean = lax.optimization_barrier(jnp.mean(values, axis=-1, keepdims=True))
    centered = values - mean
    var = lax.optimization_barrier(jnp.mean(centered * centered, axis=-1, keepdims=True))
    return centered * lax.rsqrt(var + 1e-05) * gain

def attention_layer(x, length, gain, qkv_weight, out_weight):
    frames_count = x.shape[0]
    heads_local = H // N_MP
    normed = layer_norm(x.astype(jnp.float32), gain).astype(jnp.bfloat16)
    qkv = jnp.dot(normed, qkv_weight, preferred_element_type=jnp.float32).astype(jnp.bfloat16)
    qkv = qkv.reshape(frames_count, N_MP, 3, heads_local, HD).astype(jnp.float32)
    query = qkv[:, :, 0]
    keys = qkv[:, :, 1]
    values = qkv[:, :, 2]
    scores = jnp.einsum('qghd,kghd->ghqk', query, keys) / jnp.sqrt(jnp.float32(HD))
    valid = jnp.arange(frames_count, dtype=jnp.int32) < length
    scores = jnp.where(valid[None, None, None, :], scores, jnp.float32(-1e+30))
    probs = jax.nn.softmax(scores, axis=-1).astype(jnp.bfloat16).astype(jnp.float32)
    context = jnp.einsum('ghqk,kghd->qghd', probs, values).astype(jnp.bfloat16)
    context = context.reshape(frames_count, N_MP, heads_local * HD).astype(jnp.float32)
    grouped_out = out_weight.reshape(N_MP, heads_local * HD, D).astype(jnp.float32)
    partials = jnp.einsum('qgc,gcd->gqd', context, grouped_out).astype(jnp.bfloat16)
    attended = lax.optimization_barrier(jnp.sum(partials.astype(jnp.float32), axis=0))
    return (x.astype(jnp.float32) + attended).astype(jnp.bfloat16)

def reference(frames, lengths, feature_proj, norm_gain, qkv_weight, out_weight, center, whitening):

    def one_utterance(item):
        feats, length = item
        hidden = jnp.dot(feats, feature_proj, preferred_element_type=jnp.float32).astype(jnp.bfloat16)
        for layer_index in range(2):
            hidden = attention_layer(hidden, length, norm_gain[layer_index], qkv_weight[layer_index], out_weight[layer_index])
        valid = jnp.arange(hidden.shape[0], dtype=jnp.int32) < length
        summed = lax.optimization_barrier(jnp.sum(jnp.where(valid[:, None], hidden.astype(jnp.float32), jnp.float32(0.0)), axis=0))
        return summed / length.astype(jnp.float32)
    pooled = lax.map(one_utterance, (frames, lengths))
    return jnp.dot(pooled - center, whitening, precision=lax.Precision.HIGHEST, preferred_element_type=jnp.float32)
```

```python
import functools

import jax
import jax.numpy as jnp
from jax import lax
from jax.experimental import pallas as pl
from jax.experimental.pallas import tpu as pltpu
from jax.sharding import PartitionSpec as P

MESH = pl.DeviceIdType.MESH
BF16 = jnp.bfloat16
F32 = jnp.float32

HD = 120


def passed_along(x, axis, by):
    count = lax.axis_size(axis)
    pairs = [(i, i + by) for i in range(count) if 0 <= i + by < count]
    return lax.ppermute(x, axis, pairs)


def broadcast(value, axis, source):
    kept = jnp.where(lax.axis_index(axis) == source, value, 0).astype(value.dtype)
    return lax.psum(kept, axis)


def layer_norm(values, gain):
    mean = jnp.mean(values, axis=-1, keepdims=True)
    centered = values - mean
    var = jnp.mean(centered * centered, axis=-1, keepdims=True)
    return centered * lax.rsqrt(var + 1e-05) * gain


def body(frames, lengths, feature_proj, norm_gain, qkv_weight, out_weight, center, whitening):
    section_index = lax.axis_index("section")
    gain = norm_gain[0]
    qkv_local = qkv_weight[0]
    out_local = out_weight[0]
    count_utt = frames.shape[0]
    frames_count = frames.shape[1]
    width = gain.shape[0]
    qkv_cols = qkv_local.shape[1]
    heads_local = qkv_cols // (3 * HD)
    full_qkv, full_out = (
        lax.all_gather(qkv_local, "dp", axis=0, tiled=True),
        lax.all_gather(out_local, "dp", axis=1, tiled=True),
    )
    received = jnp.zeros((frames_count, width), jnp.bfloat16)
    pooled_rows = []
    frame_ids = jnp.arange(frames_count, dtype=jnp.int32)
    for step in range(count_utt + 1):
        first_mb = min(step, count_utt - 1)
        second_mb = max(step - 1, 0)
        projected_part = jnp.dot(
            frames[first_mb], feature_proj, preferred_element_type=jnp.float32
        ).astype(jnp.bfloat16)
        projected = lax.all_gather(projected_part, "mp", axis=1, tiled=True)
        first_section = section_index == 0
        layer_input = jnp.where(first_section, projected, received)
        length = jnp.where(first_section, lengths[first_mb], lengths[second_mb])
        normed = layer_norm(layer_input.astype(jnp.float32), gain).astype(jnp.bfloat16)
        qkv_sum = jnp.dot(normed, full_qkv, preferred_element_type=jnp.float32)
        qkv = qkv_sum.astype(jnp.bfloat16).reshape(frames_count, 3, heads_local, HD)
        query = qkv[:, 0]
        keys = qkv[:, 1]
        values = qkv[:, 2]
        scores = jnp.einsum(
            "qhd,khd->hqk", query, keys, preferred_element_type=jnp.float32
        ) / jnp.sqrt(jnp.float32(HD))
        attention_valid = jnp.arange(frames_count, dtype=jnp.int32) < length
        scores = jnp.where(attention_valid[None, None, :], scores, jnp.float32(-1e30))
        probs = jax.nn.softmax(scores, axis=-1).astype(jnp.bfloat16)
        context = jnp.einsum(
            "hqk,khd->qhd", probs, values, preferred_element_type=jnp.float32
        ).astype(jnp.bfloat16)
        context = context.reshape(frames_count, heads_local * HD)
        partial_out = jnp.dot(context, full_out, preferred_element_type=jnp.float32)
        attended = lax.psum(partial_out.astype(jnp.bfloat16), "mp").astype(jnp.float32)
        result = (layer_input.astype(jnp.float32) + attended).astype(jnp.bfloat16)
        if step >= 1:
            valid = frame_ids < lengths[step - 1]
            summed = jnp.sum(
                jnp.where(valid[:, None], result.astype(jnp.float32), jnp.float32(0.0)), axis=0
            )
            pooled_rows.append(summed / lengths[step - 1].astype(jnp.float32))
        if step < count_utt:
            received = passed_along(result, "section", 1)
    pooled = jnp.stack(pooled_rows, axis=0)
    pooled = broadcast(pooled, "section", 1)
    return jnp.dot(
        lax.all_gather(pooled, "dp", axis=0, tiled=True) - center,
        whitening,
        precision=lax.Precision.HIGHEST,
        preferred_element_type=jnp.float32,
    )


def slice_of(ref, index, count, size):
    value = jnp.zeros((1, size), F32)
    for part in range(count):
        value += jnp.where(index == part, ref[:, part * size : (part + 1) * size], 0.0)
    return value


def kernel(
    n,
    lengths_ref,
    frames_ref,
    proj_ref,
    gain_ref,
    center_ref,
    qkv_hbm,
    out_hbm,
    white_hbm,
    emb_ref,
    wq,
    wo,
    wh,
    x0buf,
    xbuf,
    stat,
    qsend,
    qrecv,
    own,
    ctx,
    psend,
    precv,
    xnew,
    pool,
    rows,
    load_sem,
    x_send,
    x_recv,
    stat_send,
    stat_recv,
    q_send,
    q_recv,
    c_send,
    c_recv,
    p_send,
    p_recv,
    n_send,
    pool_send,
    pool_recv,
    row_send,
    row_recv,
):
    d = lax.axis_index("dp")
    s = lax.axis_index("section")
    m = lax.axis_index("mp")
    frames_count, wide = x0buf.shape
    full = n * wide

    barrier = pltpu.get_barrier_semaphore()
    for dz in range(n):
        for dm in range(n):
            if dz or dm:
                pl.semaphore_signal(
                    barrier, inc=1, device_id=(lax.rem(d + dz, n), s, lax.rem(m + dm, n)), device_id_type=MESH
                )
    for dm in range(n):
        pl.semaphore_signal(barrier, inc=1, device_id=(d, 1 - s, lax.rem(m + dm, n)), device_id_type=MESH)

    loads = [
        pltpu.make_async_copy(qkv_hbm, wq, load_sem.at[0]),
        pltpu.make_async_copy(out_hbm, wo, load_sem.at[1]),
        pltpu.make_async_copy(white_hbm, wh, load_sem.at[2]),
    ]
    for load in loads:
        load.start()

    @pl.when(s == 0)
    def _():
        x0buf[...] = jnp.dot(frames_ref[0], proj_ref[...], preferred_element_type=F32).astype(BF16)

    pl.semaphore_wait(barrier, n * n - 1 + n)

    def remote(src, dst, send, recv, target):
        return pltpu.make_async_remote_copy(
            src_ref=src, dst_ref=dst, send_sem=send, recv_sem=recv, device_id=target, device_id_type=MESH
        )

    def x0_copy(dm):
        return remote(
            x0buf, xbuf.at[d], x_send.at[dm], x_recv.at[d], (m, s, lax.rem(m + dm, n))
        )

    @pl.when(s == 0)
    def _():
        for dm in range(1, n):
            x0_copy(dm).start()

        @pl.when(d != m)
        def _():
            x0_copy(0).start()

        @pl.when(d == m)
        def _():
            xbuf[d] = x0buf[...]

    gain = slice_of(gain_ref, d, n, wide)
    lanes = lax.broadcasted_iota(jnp.int32, (frames_count, 128), 1)

    for u in range(n):
        @pl.when(jnp.logical_or(s == 1, jnp.logical_or(d != u, m != d)))
        def _():
            remote(x0buf, xbuf.at[u], x_send.at[0], x_recv.at[u], (d, s, m)).wait_recv()

    table = jnp.zeros((frames_count, 128), F32)
    for u in range(n):
        x = xbuf[u].astype(F32)
        total = jnp.sum(x, axis=1, keepdims=True)
        centered = x - total * (1.0 / wide)
        spread = jnp.sum(centered * centered, axis=1, keepdims=True)
        table = jnp.where(lanes == 2 * u, total, table)
        table = jnp.where(lanes == 2 * u + 1, spread, table)
    table = jnp.where(lanes == 2 * n, lengths_ref[0].astype(F32), table)
    stat[0] = table.T[0:16]
    stat_copies = []
    for k in range(1, n):
        copy = remote(stat.at[0], stat.at[k], stat_send.at[k], stat_recv.at[k], (lax.rem(d + k, n), s, m))
        copy.start()
        stat_copies.append(copy)
    for copy in stat_copies:
        copy.wait_recv()
    sums = stat[0]
    for k in range(1, n):
        sums = sums + stat[k]
    mean_rows = sums * (1.0 / full)
    moved = jnp.zeros_like(mean_rows)
    for k in range(n):
        delta = stat[k] * (1.0 / wide) - mean_rows
        moved += delta * delta
    spread_rows = jnp.concatenate([sums[1:], sums[:1]], axis=0) + moved * wide
    rstd_rows = lax.rsqrt(spread_rows * (1.0 / full) + 1e-05)
    filler = jnp.zeros((128 - 16, 128), F32)
    mean_table = jnp.concatenate([mean_rows, filler], axis=0).T
    rstd_table = jnp.concatenate([rstd_rows, filler], axis=0).T

    def partial_qkv(u):
        here = lanes == 2 * u
        mean = jnp.sum(jnp.where(here, mean_table, 0.0), axis=1, keepdims=True)
        rstd = jnp.sum(jnp.where(here, rstd_table, 0.0), axis=1, keepdims=True)
        normed = ((xbuf[u].astype(F32) - mean) * rstd * gain).astype(BF16)
        return jnp.dot(normed, wq[...], preferred_element_type=F32)

    loads[0].wait()
    q_copies = []
    for k in (2, 1, 3):
        u = lax.rem(d + k, n)
        qsend[k] = partial_qkv(u).astype(BF16)
        copy = remote(qsend.at[k], qrecv.at[k], q_send.at[k], q_recv.at[k], (u, s, m))
        copy.start()
        q_copies.append(copy)
    own[...] = partial_qkv(d)
    for copy in q_copies:
        copy.wait_recv()
    third = n * HD
    summed = own[...]
    for k in range(1, n):
        summed = summed + qrecv[k].astype(F32)
    qkv = summed.astype(BF16)
    query = qkv[:, 0:third]
    keys = qkv[:, third : 2 * third]
    values = qkv[:, 2 * third : 3 * third]
    columns = lax.broadcasted_iota(jnp.int32, (frames_count, third), 1)
    valid = lax.broadcasted_iota(jnp.int32, (frames_count, frames_count), 1) < lengths_ref[0]
    context = jnp.zeros((frames_count, third), F32)
    for h in range(n):
        in_head = jnp.logical_and(columns >= h * HD, columns < (h + 1) * HD)
        head_query = jnp.where(in_head, query, jnp.zeros_like(query))
        head_values = jnp.where(in_head, values, jnp.zeros_like(values))
        scores = lax.dot_general(
            head_query, keys, (((1,), (1,)), ((), ())), preferred_element_type=F32
        ) / jnp.sqrt(F32(HD))
        scores = jnp.where(valid, scores, F32(-1e30))
        weights = jnp.exp(scores - jnp.max(scores, axis=1, keepdims=True))
        probs = (weights / jnp.sum(weights, axis=1, keepdims=True)).astype(BF16)
        context += jnp.dot(probs, head_values, preferred_element_type=F32)
    ctx[0] = context.astype(BF16)
    c_copies = []
    for k in (2, 1, 3):
        copy = remote(ctx.at[0], ctx.at[k], c_send.at[k], c_recv.at[k], (lax.rem(d + k, n), s, m))
        copy.start()
        c_copies.append(copy)
    loads[1].wait()
    for copy in c_copies:
        copy.wait_recv()

    def partial_out(u):
        return jnp.dot(ctx[lax.rem(d - u + n, n)], wo[...], preferred_element_type=F32).astype(BF16)

    p_copies = []
    for j in (3, 1, 2):
        u = lax.rem(m + j, n)
        psend[j] = partial_out(u)
        copy = remote(psend.at[j], precv.at[j], p_send.at[j], p_recv.at[j], (d, s, u))
        copy.start()
        p_copies.append(copy)
    attended = partial_out(m).astype(F32)
    for copy in p_copies:
        copy.wait_recv()
    for j in range(1, n):
        attended = attended + precv[j].astype(F32)
    xnew[...] = (xbuf[m].astype(F32) + attended).astype(BF16)

    def next_copy(dm):
        return remote(xnew, xbuf.at[m], n_send.at[dm], x_recv.at[m], (d, 1, lax.rem(m + dm, n)))

    @pl.when(s == 0)
    def _():
        for dm in range(n):
            next_copy(dm).start()

    def pool_copy(ds, dm):
        return remote(
            pool.at[m],
            pool.at[m],
            pool_send.at[ds, dm],
            pool_recv.at[m],
            (d, lax.rem(s + ds, 2), lax.rem(m + dm, n)),
        )

    hops = [(ds, dm) for ds in range(2) for dm in range(n) if ds or dm]

    @pl.when(s == 1)
    def _():
        length = stat[lax.rem(d - m + n, n), 2 * n : 2 * n + 1, :]
        inside = lax.broadcasted_iota(jnp.int32, (8, frames_count), 1).astype(F32) < length
        weights = jnp.where(inside, 1.0, 0.0).astype(BF16)
        total = jnp.dot(weights, xnew[...], preferred_element_type=F32)
        pool[m] = total / length[:, 0:1]
        for ds, dm in hops:
            pool_copy(ds, dm).start()

    for u in range(n):
        @pl.when(jnp.logical_or(s == 0, m != u))
        def _():
            remote(pool.at[u], pool.at[u], pool_send.at[0, 0], pool_recv.at[u], (d, s, m)).wait_recv()

    row_ids = lax.broadcasted_iota(jnp.int32, (8, wide), 0)
    gathered = jnp.zeros((8, wide), F32)
    for u in range(n):
        gathered = jnp.where(row_ids == u, pool[u], gathered)
    rows[d] = gathered - slice_of(center_ref, d, n, wide)
    row_copies = []
    for k in range(1, n):
        copy = remote(rows.at[d], rows.at[d], row_send.at[k], row_recv.at[k], (lax.rem(d + k, n), s, m))
        copy.start()
        row_copies.append(copy)
    loads[2].wait()
    for k in range(1, n):
        source = lax.rem(d - k + n, n)
        remote(rows.at[source], rows.at[source], row_send.at[k], row_recv.at[k], (source, s, m)).wait_recv()
    result = jnp.zeros((8, emb_ref.shape[1]), F32)
    for part in range(n):
        result += jnp.dot(
            rows[part],
            wh[part * wide : (part + 1) * wide, :],
            precision=lax.Precision.HIGHEST,
            preferred_element_type=F32,
        )
    emb_ref[...] = result[0:n]

    for copy in stat_copies + q_copies + c_copies + p_copies + row_copies:
        copy.wait_send()

    @pl.when(s == 0)
    def _():
        for dm in range(1, n):
            x0_copy(dm).wait_send()

        @pl.when(d != m)
        def _():
            x0_copy(0).wait_send()

        for dm in range(n):
            next_copy(dm).wait_send()

    @pl.when(s == 1)
    def _():
        for ds, dm in hops:
            pool_copy(ds, dm).wait_send()


def fused(n, frames, lengths, feature_proj, norm_gain, qkv_weight, out_weight, center, whitening):
    frames_count = frames.shape[1]
    wide = feature_proj.shape[1]
    qkv_cols = qkv_weight.shape[2]
    head_rows = out_weight.shape[1]
    out_cols = whitening.shape[1]
    vmem = pl.BlockSpec(memory_space=pltpu.VMEM)
    anywhere = pl.BlockSpec(memory_space=pl.ANY)
    dma = pltpu.SemaphoreType.DMA
    return pl.pallas_call(
        functools.partial(kernel, n),
        out_shape=jax.ShapeDtypeStruct((n, out_cols), F32),
        in_specs=[pl.BlockSpec(memory_space=pltpu.SMEM)] + [vmem] * 4 + [anywhere] * 3,
        out_specs=vmem,
        scratch_shapes=[
            pltpu.VMEM((wide, qkv_cols), BF16),
            pltpu.VMEM((head_rows, wide), BF16),
            pltpu.VMEM((n * wide, out_cols), F32),
            pltpu.VMEM((frames_count, wide), BF16),
            pltpu.VMEM((n, frames_count, wide), BF16),
            pltpu.VMEM((n, 16, 128), F32),
            pltpu.VMEM((n, frames_count, qkv_cols), BF16),
            pltpu.VMEM((n, frames_count, qkv_cols), BF16),
            pltpu.VMEM((frames_count, qkv_cols), F32),
            pltpu.VMEM((n, frames_count, head_rows), BF16),
            pltpu.VMEM((n, frames_count, wide), BF16),
            pltpu.VMEM((n, frames_count, wide), BF16),
            pltpu.VMEM((frames_count, wide), BF16),
            pltpu.VMEM((n, 8, wide), F32),
            pltpu.VMEM((n, 8, wide), F32),
            dma((3,)),
            dma((n,)), dma((n,)),
            dma((n,)), dma((n,)),
            dma((n,)), dma((n,)),
            dma((n,)), dma((n,)),
            dma((n,)), dma((n,)),
            dma((n,)),
            dma((2, n)), dma((n,)),
            dma((n,)), dma((n,)),
        ],
        compiler_params=pltpu.CompilerParams(
            collective_id=0, has_side_effects=True, vmem_limit_bytes=40 * 1024 * 1024
        ),
    )(
        lengths,
        frames,
        feature_proj,
        norm_gain,
        center.reshape(1, -1),
        qkv_weight.reshape(qkv_weight.shape[1:]),
        out_weight.reshape(out_weight.shape[1:]),
        whitening,
    )


def solution(mesh):
    in_specs = (
        P("dp", None, None),
        P("dp"),
        P(None, "mp"),
        P("section", None),
        P("section", "dp", "mp"),
        P("section", "mp", "dp"),
        P(),
        P(None, "dp"),
    )
    out_specs = P(None, "dp")

    def step(frames, lengths, feature_proj, norm_gain, qkv_weight, out_weight, center, whitening):
        n = mesh.shape["mp"]
        square = mesh.shape["dp"] == n and mesh.shape["section"] == 2
        square = square and frames.shape[0] == 1 and frames.shape[1] == 128 and 2 * n < 16
        square = square and qkv_weight.shape[2] == 3 * n * HD and qkv_weight.shape[1] == feature_proj.shape[1]
        if square:
            return fused(
                n, frames, lengths, feature_proj, norm_gain, qkv_weight, out_weight, center, whitening
            )
        return body(frames, lengths, feature_proj, norm_gain, qkv_weight, out_weight, center, whitening)

    return jax.shard_map(step, mesh=mesh, in_specs=in_specs, out_specs=out_specs, check_vma=False)
```

```python
import functools

import jax
import jax.numpy as jnp
from jax import lax
from jax.experimental import pallas as pl
from jax.experimental.pallas import tpu as pltpu
from jax.sharding import PartitionSpec as P

MESH = pl.DeviceIdType.MESH
BF16 = jnp.bfloat16
F32 = jnp.float32

HD = 120


def passed_along(x, axis, by):
    count = lax.axis_size(axis)
    pairs = [(i, i + by) for i in range(count) if 0 <= i + by < count]
    return lax.ppermute(x, axis, pairs)


def broadcast(value, axis, source):
    kept = jnp.where(lax.axis_index(axis) == source, value, 0).astype(value.dtype)
    return lax.psum(kept, axis)


def layer_norm(values, gain):
    mean = jnp.mean(values, axis=-1, keepdims=True)
    centered = values - mean
    var = jnp.mean(centered * centered, axis=-1, keepdims=True)
    return centered * lax.rsqrt(var + 1e-05) * gain


def body(frames, lengths, feature_proj, norm_gain, qkv_weight, out_weight, center, whitening):
    section_index = lax.axis_index("section")
    gain = norm_gain[0]
    qkv_local = qkv_weight[0]
    out_local = out_weight[0]
    count_utt = frames.shape[0]
    frames_count = frames.shape[1]
    width = gain.shape[0]
    qkv_cols = qkv_local.shape[1]
    heads_local = qkv_cols // (3 * HD)
    full_qkv, full_out = (
        lax.all_gather(qkv_local, "dp", axis=0, tiled=True),
        lax.all_gather(out_local, "dp", axis=1, tiled=True),
    )
    received = jnp.zeros((frames_count, width), jnp.bfloat16)
    pooled_rows = []
    frame_ids = jnp.arange(frames_count, dtype=jnp.int32)
    for step in range(count_utt + 1):
        first_mb = min(step, count_utt - 1)
        second_mb = max(step - 1, 0)
        projected_part = jnp.dot(
            frames[first_mb], feature_proj, preferred_element_type=jnp.float32
        ).astype(jnp.bfloat16)
        projected = lax.all_gather(projected_part, "mp", axis=1, tiled=True)
        first_section = section_index == 0
        layer_input = jnp.where(first_section, projected, received)
        length = jnp.where(first_section, lengths[first_mb], lengths[second_mb])
        normed = layer_norm(layer_input.astype(jnp.float32), gain).astype(jnp.bfloat16)
        qkv_sum = jnp.dot(normed, full_qkv, preferred_element_type=jnp.float32)
        qkv = qkv_sum.astype(jnp.bfloat16).reshape(frames_count, 3, heads_local, HD)
        query = qkv[:, 0]
        keys = qkv[:, 1]
        values = qkv[:, 2]
        scores = jnp.einsum(
            "qhd,khd->hqk", query, keys, preferred_element_type=jnp.float32
        ) / jnp.sqrt(jnp.float32(HD))
        attention_valid = jnp.arange(frames_count, dtype=jnp.int32) < length
        scores = jnp.where(attention_valid[None, None, :], scores, jnp.float32(-1e30))
        probs = jax.nn.softmax(scores, axis=-1).astype(jnp.bfloat16)
        context = jnp.einsum(
            "hqk,khd->qhd", probs, values, preferred_element_type=jnp.float32
        ).astype(jnp.bfloat16)
        context = context.reshape(frames_count, heads_local * HD)
        partial_out = jnp.dot(context, full_out, preferred_element_type=jnp.float32)
        attended = lax.psum(partial_out.astype(jnp.bfloat16), "mp").astype(jnp.float32)
        result = (layer_input.astype(jnp.float32) + attended).astype(jnp.bfloat16)
        if step >= 1:
            valid = frame_ids < lengths[step - 1]
            summed = jnp.sum(
                jnp.where(valid[:, None], result.astype(jnp.float32), jnp.float32(0.0)), axis=0
            )
            pooled_rows.append(summed / lengths[step - 1].astype(jnp.float32))
        if step < count_utt:
            received = passed_along(result, "section", 1)
    pooled = jnp.stack(pooled_rows, axis=0)
    pooled = broadcast(pooled, "section", 1)
    return jnp.dot(
        lax.all_gather(pooled, "dp", axis=0, tiled=True) - center,
        whitening,
        precision=lax.Precision.HIGHEST,
        preferred_element_type=jnp.float32,
    )


def slice_of(row, index, count, size):
    value = jnp.zeros((1, size), F32)
    for part in range(count):
        value += jnp.where(index == part, row[:, part * size : (part + 1) * size], 0.0)
    return value


def chunk_bounds(columns):
    size = -(-columns // (3 * 128)) * 128
    return [(start, min(start + size, columns)) for start in range(0, columns, size)]


def kernel(
    n,
    lengths_ref,
    frames_hbm,
    proj_hbm,
    gain_hbm,
    center_hbm,
    qkv_hbm,
    out_hbm,
    white_hbm,
    emb_ref,
    frames_ref,
    proj_ref,
    gain_ref,
    center_ref,
    wq,
    wo,
    wh,
    x0buf,
    xbuf,
    stat,
    normed,
    own,
    qkv,
    qsend0,
    qsend1,
    qsend2,
    qrecv0,
    qrecv1,
    qrecv2,
    ctx,
    psend,
    precv,
    xnew,
    pool,
    rows,
    load_sem,
    x_send,
    x_recv,
    stat_send,
    stat_recv,
    q_send,
    q_recv,
    c_send,
    c_recv,
    p_send,
    p_recv,
    n_send,
    pool_send,
    pool_recv,
    row_send,
    row_recv,
):
    d = lax.axis_index("dp")
    s = lax.axis_index("section")
    m = lax.axis_index("mp")
    frames_count, wide = x0buf.shape
    full = n * wide

    pairs = (
        (frames_hbm, frames_ref),
        (proj_hbm, proj_ref),
        (gain_hbm, gain_ref),
        (qkv_hbm, wq),
        (out_hbm, wo),
        (center_hbm, center_ref),
        (white_hbm, wh),
    )
    loads = [pltpu.make_async_copy(src, dst, load_sem.at[i]) for i, (src, dst) in enumerate(pairs)]
    for load in loads:
        load.start()

    barrier = pltpu.get_barrier_semaphore()
    for dz in range(n):
        for dm in range(n):
            if dz or dm:
                pl.semaphore_signal(
                    barrier, inc=1, device_id=(lax.rem(d + dz, n), s, lax.rem(m + dm, n)), device_id_type=MESH
                )
    for dm in range(n):
        pl.semaphore_signal(barrier, inc=1, device_id=(d, 1 - s, lax.rem(m + dm, n)), device_id_type=MESH)

    loads[0].wait()
    loads[1].wait()

    @pl.when(s == 0)
    def _():
        x0buf[...] = lax.dot_general(
            frames_ref[0], proj_ref[...], (((1,), (1,)), ((), ())), preferred_element_type=F32
        ).astype(BF16)

    pl.semaphore_wait(barrier, n * n - 1 + n)

    def remote(src, dst, send, recv, target):
        return pltpu.make_async_remote_copy(
            src_ref=src, dst_ref=dst, send_sem=send, recv_sem=recv, device_id=target, device_id_type=MESH
        )

    def x0_copy(dm):
        return remote(
            x0buf, xbuf.at[d], x_send.at[dm], x_recv.at[d], (m, s, lax.rem(m + dm, n))
        )

    @pl.when(s == 0)
    def _():
        for dm in range(1, n):
            x0_copy(dm).start()

        @pl.when(d != m)
        def _():
            x0_copy(0).start()

        @pl.when(d == m)
        def _():
            xbuf[d] = x0buf[...]

    loads[2].wait()
    gain = slice_of(gain_ref, d, n, wide)
    lanes = lax.broadcasted_iota(jnp.int32, (frames_count, 128), 1)

    for u in range(n):
        @pl.when(jnp.logical_or(s == 1, jnp.logical_or(d != u, m != d)))
        def _():
            remote(x0buf, xbuf.at[u], x_send.at[0], x_recv.at[u], (d, s, m)).wait_recv()

    table = jnp.zeros((frames_count, 128), F32)
    for u in range(n):
        x = xbuf[u].astype(F32)
        total = jnp.sum(x, axis=1, keepdims=True)
        centered = x - total * (1.0 / wide)
        spread = jnp.sum(centered * centered, axis=1, keepdims=True)
        table = jnp.where(lanes == 2 * u, total, table)
        table = jnp.where(lanes == 2 * u + 1, spread, table)
    table = jnp.where(lanes == 2 * n, lengths_ref[0].astype(F32), table)
    stat[0] = table.T[0:16]
    stat_copies = []
    for k in range(1, n):
        copy = remote(stat.at[0], stat.at[k], stat_send.at[k], stat_recv.at[k], (lax.rem(d + k, n), s, m))
        copy.start()
        stat_copies.append(copy)
    for copy in stat_copies:
        copy.wait_recv()
    sums = stat[0]
    for k in range(1, n):
        sums = sums + stat[k]
    mean_rows = sums * (1.0 / full)
    moved = jnp.zeros_like(mean_rows)
    for k in range(n):
        delta = stat[k] * (1.0 / wide) - mean_rows
        moved += delta * delta
    spread_rows = jnp.concatenate([sums[1:], sums[:1]], axis=0) + moved * wide
    rstd_rows = lax.rsqrt(spread_rows * (1.0 / full) + 1e-05)
    filler = jnp.zeros((128 - 16, 128), F32)
    mean_table = jnp.concatenate([mean_rows, filler], axis=0).T
    rstd_table = jnp.concatenate([rstd_rows, filler], axis=0).T

    for u in range(n):
        mean = mean_table[:, 2 * u : 2 * u + 1]
        rstd = rstd_table[:, 2 * u : 2 * u + 1]
        normed[u * frames_count : (u + 1) * frames_count] = (
            (xbuf[u].astype(F32) - mean) * rstd * gain
        ).astype(BF16)

    loads[3].wait()
    third = n * HD
    bounds = chunk_bounds(3 * third)
    qsend, qrecv = (qsend0, qsend1, qsend2), (qrecv0, qrecv1, qrecv2)
    q_copies = []
    for c, (start, stop) in enumerate(bounds):
        partial = jnp.dot(normed[...], wq[:, start:stop], preferred_element_type=F32)
        for u in range(n):
            piece = partial[u * frames_count : (u + 1) * frames_count]
            qsend[c][u] = piece.astype(BF16)
            own[u, :, start:stop] = piece
        for k in (2, 1, 3):
            u = lax.rem(d + k, n)
            copy = remote(qsend[c].at[u], qrecv[c].at[k], q_send.at[c, k], q_recv.at[c, k], (u, s, m))
            copy.start()
            q_copies.append(copy)

    def collect(c):
        start, stop = bounds[c]
        for copy in q_copies[c * (n - 1) : (c + 1) * (n - 1)]:
            copy.wait_recv()
        summed = own[d, :, start:stop]
        for k in range(1, n):
            summed = summed + qrecv[c][k].astype(F32)
        qkv[:, start:stop] = summed.astype(BF16)

    collect(0)
    collect(1)
    query = qkv[:, 0:third]
    keys = qkv[:, third : 2 * third]
    columns = lax.broadcasted_iota(jnp.int32, (frames_count, third), 1)
    valid = lax.broadcasted_iota(jnp.int32, (frames_count, frames_count), 1) < lengths_ref[0]
    heads = []
    for h in range(n):
        in_head = jnp.logical_and(columns >= h * HD, columns < (h + 1) * HD)
        head_query = jnp.where(in_head, query, jnp.zeros_like(query))
        scores = lax.dot_general(
            head_query, keys, (((1,), (1,)), ((), ())), preferred_element_type=F32
        ) / jnp.sqrt(F32(HD))
        scores = jnp.where(valid, scores, F32(-1e30))
        weights = jnp.exp(scores - jnp.max(scores, axis=1, keepdims=True))
        heads.append((in_head, (weights / jnp.sum(weights, axis=1, keepdims=True)).astype(BF16)))
    collect(2)
    values = qkv[:, 2 * third : 3 * third]
    context = jnp.zeros((frames_count, third), F32)
    for in_head, probs in heads:
        head_values = jnp.where(in_head, values, jnp.zeros_like(values))
        context += jnp.dot(probs, head_values, preferred_element_type=F32)
    ctx[0] = context.astype(BF16)
    c_copies = []
    for k in (2, 1, 3):
        copy = remote(ctx.at[0], ctx.at[k], c_send.at[k], c_recv.at[k], (lax.rem(d + k, n), s, m))
        copy.start()
        c_copies.append(copy)
    loads[4].wait()
    for copy in c_copies:
        copy.wait_recv()

    def partial_out(u):
        return jnp.dot(ctx[lax.rem(d - u + n, n)], wo[...], preferred_element_type=F32).astype(BF16)

    p_copies = []
    for j in (3, 1, 2):
        u = lax.rem(m + j, n)
        psend[j] = partial_out(u)
        copy = remote(psend.at[j], precv.at[j], p_send.at[j], p_recv.at[j], (d, s, u))
        copy.start()
        p_copies.append(copy)
    attended = partial_out(m).astype(F32)
    for copy in p_copies:
        copy.wait_recv()
    for j in range(1, n):
        attended = attended + precv[j].astype(F32)
    xnew[...] = (xbuf[m].astype(F32) + attended).astype(BF16)

    def next_copy(dm):
        return remote(xnew, xbuf.at[m], n_send.at[dm], x_recv.at[m], (d, 1, lax.rem(m + dm, n)))

    @pl.when(s == 0)
    def _():
        for dm in range(n):
            next_copy(dm).start()

    def pool_copy(ds, dm):
        return remote(
            pool.at[m],
            pool.at[m],
            pool_send.at[ds, dm],
            pool_recv.at[m],
            (d, lax.rem(s + ds, 2), lax.rem(m + dm, n)),
        )

    hops = [(ds, dm) for ds in range(2) for dm in range(n) if ds or dm]

    @pl.when(s == 1)
    def _():
        length = stat[lax.rem(d - m + n, n), 2 * n : 2 * n + 1, :]
        inside = lax.broadcasted_iota(jnp.int32, (8, frames_count), 1).astype(F32) < length
        weights = jnp.where(inside, 1.0, 0.0).astype(BF16)
        total = jnp.dot(weights, xnew[...], preferred_element_type=F32)
        pool[m] = total / length[:, 0:1]
        for ds, dm in hops:
            pool_copy(ds, dm).start()

    for u in range(n):
        @pl.when(jnp.logical_or(s == 0, m != u))
        def _():
            remote(pool.at[u], pool.at[u], pool_send.at[0, 0], pool_recv.at[u], (d, s, m)).wait_recv()

    loads[5].wait()
    row_ids = lax.broadcasted_iota(jnp.int32, (8, wide), 0)
    gathered = jnp.zeros((8, wide), F32)
    for u in range(n):
        gathered = jnp.where(row_ids == u, pool[u], gathered)
    rows[d] = gathered - slice_of(center_ref[...].reshape(1, full), d, n, wide)
    row_copies = []
    for k in range(1, n):
        copy = remote(rows.at[d], rows.at[d], row_send.at[k], row_recv.at[k], (lax.rem(d + k, n), s, m))
        copy.start()
        row_copies.append(copy)
    loads[6].wait()
    for k in range(1, n):
        source = lax.rem(d - k + n, n)
        remote(rows.at[source], rows.at[source], row_send.at[k], row_recv.at[k], (source, s, m)).wait_recv()
    result = jnp.zeros((8, emb_ref.shape[1]), F32)
    for part in range(n):
        result += jnp.dot(
            rows[part],
            wh[part * wide : (part + 1) * wide, :],
            precision=lax.Precision.HIGHEST,
            preferred_element_type=F32,
        )
    emb_ref[...] = result[0:n]

    for copy in stat_copies + q_copies + c_copies + p_copies + row_copies:
        copy.wait_send()

    @pl.when(s == 0)
    def _():
        for dm in range(1, n):
            x0_copy(dm).wait_send()

        @pl.when(d != m)
        def _():
            x0_copy(0).wait_send()

        for dm in range(n):
            next_copy(dm).wait_send()

    @pl.when(s == 1)
    def _():
        for ds, dm in hops:
            pool_copy(ds, dm).wait_send()


def fused(n, frames, lengths, feature_proj, norm_gain, qkv_weight, out_weight, center, whitening):
    frames_count = frames.shape[1]
    wide = feature_proj.shape[1]
    qkv_cols = qkv_weight.shape[2]
    head_rows = out_weight.shape[1]
    out_cols = whitening.shape[1]
    vmem = pl.BlockSpec(memory_space=pltpu.VMEM)
    anywhere = pl.BlockSpec(memory_space=pl.ANY)
    dma = pltpu.SemaphoreType.DMA
    return pl.pallas_call(
        functools.partial(kernel, n),
        out_shape=jax.ShapeDtypeStruct((n, out_cols), F32),
        in_specs=[pl.BlockSpec(memory_space=pltpu.SMEM)] + [anywhere] * 7,
        out_specs=vmem,
        scratch_shapes=[
            pltpu.VMEM(frames.shape, BF16),
            pltpu.VMEM(feature_proj.shape[::-1], BF16),
            pltpu.VMEM(norm_gain.shape, F32),
            pltpu.VMEM(center.shape, F32),
            pltpu.VMEM((wide, qkv_cols), BF16),
            pltpu.VMEM((head_rows, wide), BF16),
            pltpu.VMEM((n * wide, out_cols), F32),
            pltpu.VMEM((frames_count, wide), BF16),
            pltpu.VMEM((n, frames_count, wide), BF16),
            pltpu.VMEM((n, 16, 128), F32),
            pltpu.VMEM((n * frames_count, wide), BF16),
            pltpu.VMEM((n, frames_count, qkv_cols), F32),
            pltpu.VMEM((frames_count, qkv_cols), BF16),
        ]
        + [pltpu.VMEM((n, frames_count, stop - start), BF16) for start, stop in chunk_bounds(qkv_cols)] * 2
        + [
            pltpu.VMEM((n, frames_count, head_rows), BF16),
            pltpu.VMEM((n, frames_count, wide), BF16),
            pltpu.VMEM((n, frames_count, wide), BF16),
            pltpu.VMEM((frames_count, wide), BF16),
            pltpu.VMEM((n, 8, wide), F32),
            pltpu.VMEM((n, 8, wide), F32),
            dma((7,)),
            dma((n,)), dma((n,)),
            dma((n,)), dma((n,)),
            dma((3, n)), dma((3, n)),
            dma((n,)), dma((n,)),
            dma((n,)), dma((n,)),
            dma((n,)),
            dma((2, n)), dma((n,)),
            dma((n,)), dma((n,)),
        ],
        compiler_params=pltpu.CompilerParams(
            collective_id=0, has_side_effects=True, vmem_limit_bytes=60 * 1024 * 1024
        ),
    )(
        lengths,
        frames,
        feature_proj.T,
        norm_gain,
        center,
        qkv_weight.reshape(qkv_weight.shape[1:]),
        out_weight.reshape(out_weight.shape[1:]),
        whitening,
    )


def solution(mesh):
    in_specs = (
        P("dp", None, None),
        P("dp"),
        P(None, "mp"),
        P("section", None),
        P("section", "dp", "mp"),
        P("section", "mp", "dp"),
        P(),
        P(None, "dp"),
    )
    out_specs = P(None, "dp")

    def step(frames, lengths, feature_proj, norm_gain, qkv_weight, out_weight, center, whitening):
        n = mesh.shape["mp"]
        square = mesh.shape["dp"] == n and mesh.shape["section"] == 2
        square = square and frames.shape[0] == 1 and frames.shape[1] == 128 and 2 * n < 16
        square = square and qkv_weight.shape[2] == 3 * n * HD and qkv_weight.shape[1] == feature_proj.shape[1]
        if square:
            return fused(
                n, frames, lengths, feature_proj, norm_gain, qkv_weight, out_weight, center, whitening
            )
        return body(frames, lengths, feature_proj, norm_gain, qkv_weight, out_weight, center, whitening)

    return jax.shard_map(step, mesh=mesh, in_specs=in_specs, out_specs=out_specs, check_vma=False)
```

```python
import functools

import jax
import jax.numpy as jnp
from jax import lax
from jax.experimental import pallas as pl
from jax.experimental.pallas import tpu as pltpu
from jax.sharding import PartitionSpec as P

MESH = pl.DeviceIdType.MESH
BF16 = jnp.bfloat16
F32 = jnp.float32

HD = 120


def passed_along(x, axis, by):
    count = lax.axis_size(axis)
    pairs = [(i, i + by) for i in range(count) if 0 <= i + by < count]
    return lax.ppermute(x, axis, pairs)


def broadcast(value, axis, source):
    kept = jnp.where(lax.axis_index(axis) == source, value, 0).astype(value.dtype)
    return lax.psum(kept, axis)


def layer_norm(values, gain):
    mean = jnp.mean(values, axis=-1, keepdims=True)
    centered = values - mean
    var = jnp.mean(centered * centered, axis=-1, keepdims=True)
    return centered * lax.rsqrt(var + 1e-05) * gain


def body(frames, lengths, feature_proj, norm_gain, qkv_weight, out_weight, center, whitening):
    section_index = lax.axis_index("section")
    gain = norm_gain[0]
    qkv_local = qkv_weight[0]
    out_local = out_weight[0]
    count_utt = frames.shape[0]
    frames_count = frames.shape[1]
    width = gain.shape[0]
    qkv_cols = qkv_local.shape[1]
    heads_local = qkv_cols // (3 * HD)
    full_qkv, full_out = (
        lax.all_gather(qkv_local, "dp", axis=0, tiled=True),
        lax.all_gather(out_local, "dp", axis=1, tiled=True),
    )
    received = jnp.zeros((frames_count, width), jnp.bfloat16)
    pooled_rows = []
    frame_ids = jnp.arange(frames_count, dtype=jnp.int32)
    for step in range(count_utt + 1):
        first_mb = min(step, count_utt - 1)
        second_mb = max(step - 1, 0)
        projected_part = jnp.dot(
            frames[first_mb], feature_proj, preferred_element_type=jnp.float32
        ).astype(jnp.bfloat16)
        projected = lax.all_gather(projected_part, "mp", axis=1, tiled=True)
        first_section = section_index == 0
        layer_input = jnp.where(first_section, projected, received)
        length = jnp.where(first_section, lengths[first_mb], lengths[second_mb])
        normed = layer_norm(layer_input.astype(jnp.float32), gain).astype(jnp.bfloat16)
        qkv_sum = jnp.dot(normed, full_qkv, preferred_element_type=jnp.float32)
        qkv = qkv_sum.astype(jnp.bfloat16).reshape(frames_count, 3, heads_local, HD)
        query = qkv[:, 0]
        keys = qkv[:, 1]
        values = qkv[:, 2]
        scores = jnp.einsum(
            "qhd,khd->hqk", query, keys, preferred_element_type=jnp.float32
        ) / jnp.sqrt(jnp.float32(HD))
        attention_valid = jnp.arange(frames_count, dtype=jnp.int32) < length
        scores = jnp.where(attention_valid[None, None, :], scores, jnp.float32(-1e30))
        probs = jax.nn.softmax(scores, axis=-1).astype(jnp.bfloat16)
        context = jnp.einsum(
            "hqk,khd->qhd", probs, values, preferred_element_type=jnp.float32
        ).astype(jnp.bfloat16)
        context = context.reshape(frames_count, heads_local * HD)
        partial_out = jnp.dot(context, full_out, preferred_element_type=jnp.float32)
        attended = lax.psum(partial_out.astype(jnp.bfloat16), "mp").astype(jnp.float32)
        result = (layer_input.astype(jnp.float32) + attended).astype(jnp.bfloat16)
        if step >= 1:
            valid = frame_ids < lengths[step - 1]
            summed = jnp.sum(
                jnp.where(valid[:, None], result.astype(jnp.float32), jnp.float32(0.0)), axis=0
            )
            pooled_rows.append(summed / lengths[step - 1].astype(jnp.float32))
        if step < count_utt:
            received = passed_along(result, "section", 1)
    pooled = jnp.stack(pooled_rows, axis=0)
    pooled = broadcast(pooled, "section", 1)
    return jnp.dot(
        lax.all_gather(pooled, "dp", axis=0, tiled=True) - center,
        whitening,
        precision=lax.Precision.HIGHEST,
        preferred_element_type=jnp.float32,
    )


def slice_of(row, index, count, size):
    value = jnp.zeros((1, size), F32)
    for part in range(count):
        value += jnp.where(index == part, row[:, part * size : (part + 1) * size], 0.0)
    return value


def three_parts(value):
    high = value.astype(BF16).astype(F32)
    rest = value - high
    middle = rest.astype(BF16).astype(F32)
    return high, middle, rest - middle


def chunk_bounds(columns):
    size = -(-columns // (3 * 128)) * 128
    return [(start, min(start + size, columns)) for start in range(0, columns, size)]


def kernel(
    n,
    lengths_ref,
    frames_hbm,
    proj_hbm,
    gain_hbm,
    center_hbm,
    qkv_hbm,
    out_hbm,
    white_hbm,
    emb_ref,
    frames_ref,
    proj_ref,
    gain_ref,
    center_ref,
    wq,
    wo,
    wh,
    wh3,
    gsum,
    x0buf,
    xbuf,
    stat,
    normed,
    own,
    qkv,
    qsend0,
    qsend1,
    qsend2,
    qrecv0,
    qrecv1,
    qrecv2,
    ctx,
    psend,
    precv,
    xnew,
    pool,
    rows,
    load_sem,
    x_send,
    x_recv,
    stat_send,
    stat_recv,
    g_send,
    g_recv,
    q_send,
    q_recv,
    c_send,
    c_recv,
    p_send,
    p_recv,
    n_send,
    pool_send,
    pool_recv,
    row_send,
    row_recv,
):
    d = lax.axis_index("dp")
    s = lax.axis_index("section")
    m = lax.axis_index("mp")
    frames_count, wide = x0buf.shape
    full = n * wide

    pairs = (
        (frames_hbm, frames_ref),
        (proj_hbm, proj_ref),
        (gain_hbm, gain_ref),
        (qkv_hbm, wq),
        (out_hbm, wo),
        (center_hbm, center_ref),
        (white_hbm, wh),
    )
    loads = [pltpu.make_async_copy(src, dst, load_sem.at[i]) for i, (src, dst) in enumerate(pairs)]
    for load in loads:
        load.start()

    barrier = pltpu.get_barrier_semaphore()
    for dz in range(n):
        for dm in range(n):
            if dz or dm:
                pl.semaphore_signal(
                    barrier, inc=1, device_id=(lax.rem(d + dz, n), s, lax.rem(m + dm, n)), device_id_type=MESH
                )
    for dm in range(n):
        pl.semaphore_signal(barrier, inc=1, device_id=(d, 1 - s, lax.rem(m + dm, n)), device_id_type=MESH)

    loads[0].wait()
    loads[1].wait()

    @pl.when(s == 0)
    def _():
        x0buf[...] = lax.dot_general(
            frames_ref[0], proj_ref[...], (((1,), (1,)), ((), ())), preferred_element_type=F32
        ).astype(BF16)

    pl.semaphore_wait(barrier, n * n - 1 + n)

    def remote(src, dst, send, recv, target):
        return pltpu.make_async_remote_copy(
            src_ref=src, dst_ref=dst, send_sem=send, recv_sem=recv, device_id=target, device_id_type=MESH
        )

    def x0_copy(dm):
        return remote(
            x0buf, xbuf.at[d], x_send.at[dm], x_recv.at[d], (m, s, lax.rem(m + dm, n))
        )

    @pl.when(s == 0)
    def _():
        for dm in range(1, n):
            x0_copy(dm).start()

        @pl.when(d != m)
        def _():
            x0_copy(0).start()

        @pl.when(d == m)
        def _():
            xbuf[d] = x0buf[...]

    loads[2].wait()
    gain = slice_of(gain_ref, d, n, wide)
    lanes = lax.broadcasted_iota(jnp.int32, (frames_count, 128), 1)

    loads[3].wait()
    ids = lax.broadcasted_iota(jnp.int32, (16, wide), 0)
    gain_rows = jnp.zeros((16, wide), F32)
    for part, value in enumerate(three_parts(gain)):
        gain_rows = jnp.where(ids == part, value, gain_rows)
    products = jnp.dot(gain_rows.astype(BF16), wq[...], preferred_element_type=F32)
    gsum[0] = products[0:1] + products[1:2] + products[2:3]
    g_copies = []
    for k in range(1, n):
        copy = remote(gsum.at[0], gsum.at[k], g_send.at[k], g_recv.at[k], (lax.rem(d + k, n), s, m))
        copy.start()
        g_copies.append(copy)

    def split_whitening():
        loads[6].wait()
        for part in range(n):
            run = slice(part * wide, (part + 1) * wide)
            for i, value in enumerate(three_parts(wh[run])):
                wh3[i, run] = value.astype(BF16)

    @pl.when(s == 1)
    def _():
        split_whitening()

    table = jnp.zeros((frames_count, 128), F32)
    for u in range(n):
        @pl.when(jnp.logical_or(s == 1, jnp.logical_or(d != u, m != d)))
        def _():
            remote(x0buf, xbuf.at[u], x_send.at[0], x_recv.at[u], (d, s, m)).wait_recv()

        x = xbuf[u].astype(F32)
        mean = jnp.sum(x, axis=1, keepdims=True) * (1.0 / wide)
        centered = x - mean
        spread = jnp.sum(centered * centered, axis=1, keepdims=True)
        table = jnp.where(lanes == 2 * u, mean, table)
        table = jnp.where(lanes == 2 * u + 1, spread, table)
        normed[u * frames_count : (u + 1) * frames_count] = (centered * gain).astype(BF16)
    table = jnp.where(lanes == 2 * n, lengths_ref[0].astype(F32), table)

    third = n * HD
    bounds = chunk_bounds(3 * third)
    qsend, qrecv = (qsend0, qsend1, qsend2), (qrecv0, qrecv1, qrecv2)
    q_copies = []
    for c, (start, stop) in enumerate(bounds):
        partial = jnp.dot(normed[...], wq[:, start:stop], preferred_element_type=F32)
        for u in range(n):
            piece = partial[u * frames_count : (u + 1) * frames_count]
            qsend[c][u] = piece.astype(BF16)
            own[u, :, start:stop] = piece
        for k in (2, 1, 3):
            u = lax.rem(d + k, n)
            copy = remote(qsend[c].at[u], qrecv[c].at[k], q_send.at[c, k], q_recv.at[c, k], (u, s, m))
            copy.start()
            q_copies.append(copy)
        if c == 0:
            stat[0] = table.T[0:16]
            stat_copies = []
            for k in range(1, n):
                copy = remote(stat.at[0], stat.at[k], stat_send.at[k], stat_recv.at[k], (lax.rem(d + k, n), s, m))
                copy.start()
                stat_copies.append(copy)

    for copy in stat_copies + g_copies:
        copy.wait_recv()
    stat_ids = lax.broadcasted_iota(jnp.int32, (16, 128), 0)

    def stat_row(k, row):
        return jnp.sum(jnp.where(stat_ids == row, stat[k], 0.0), axis=0, keepdims=True)

    slice_means = [stat_row(k, 2 * d) for k in range(n)]
    mean = sum(slice_means) * (1.0 / n)
    deltas = [value - mean for value in slice_means]
    spread = sum(stat_row(k, 2 * d + 1) for k in range(n)) + wide * sum(value * value for value in deltas)
    rstd = lax.rsqrt(spread * (1.0 / full) + 1e-05)
    by_row = jnp.zeros((16, 128), F32)
    for k, value in enumerate(deltas + [rstd]):
        by_row = jnp.where(stat_ids == k, value, by_row)
    by_frame = jnp.concatenate([by_row, jnp.zeros((frames_count - 16, 128), F32)], axis=0).T

    def collect(c):
        start, stop = bounds[c]
        for copy in q_copies[c * (n - 1) : (c + 1) * (n - 1)]:
            copy.wait_recv()
        summed = own[d, :, start:stop]
        for k in range(1, n):
            summed = summed + qrecv[c][k].astype(F32)
        for k in range(n):
            summed = summed + by_frame[:, k : k + 1] * gsum[k, :, start:stop]
        qkv[:, start:stop] = (summed * by_frame[:, n : n + 1]).astype(BF16)

    collect(0)
    collect(1)
    query = qkv[:, 0:third]
    keys = qkv[:, third : 2 * third]
    columns = lax.broadcasted_iota(jnp.int32, (frames_count, third), 1)
    valid = lax.broadcasted_iota(jnp.int32, (frames_count, frames_count), 1) < lengths_ref[0]
    heads = []
    for h in range(n):
        in_head = jnp.logical_and(columns >= h * HD, columns < (h + 1) * HD)
        head_query = jnp.where(in_head, query, jnp.zeros_like(query))
        scores = lax.dot_general(
            head_query, keys, (((1,), (1,)), ((), ())), preferred_element_type=F32
        ) / jnp.sqrt(F32(HD))
        scores = jnp.where(valid, scores, F32(-1e30))
        weights = jnp.exp(scores - jnp.max(scores, axis=1, keepdims=True))
        heads.append((in_head, (weights / jnp.sum(weights, axis=1, keepdims=True)).astype(BF16)))
    collect(2)
    values = qkv[:, 2 * third : 3 * third]
    context = jnp.zeros((frames_count, third), F32)
    for in_head, probs in heads:
        head_values = jnp.where(in_head, values, jnp.zeros_like(values))
        context += jnp.dot(probs, head_values, preferred_element_type=F32)
    ctx[0] = context.astype(BF16)
    c_copies = []
    for k in (2, 1, 3):
        copy = remote(ctx.at[0], ctx.at[k], c_send.at[k], c_recv.at[k], (lax.rem(d + k, n), s, m))
        copy.start()
        c_copies.append(copy)
    loads[4].wait()

    def p_copy(k):
        u = lax.rem(d - k + n, n)
        slot = lax.rem(u - m + n, n)
        return remote(psend.at[k], precv.at[slot], p_send.at[k], p_recv.at[slot], (d, s, u))

    for k in (0, 1, 3, 2):
        if k:
            remote(ctx.at[0], ctx.at[k], c_send.at[k], c_recv.at[k], (d, s, m)).wait_recv()
        u = lax.rem(d - k + n, n)
        psend[k] = jnp.dot(ctx[k], wo[...], preferred_element_type=F32).astype(BF16)

        @pl.when(u != m)
        def _():
            p_copy(k).start()

        @pl.when(u == m)
        def _():
            precv[0] = psend[k]

    for j in range(1, n):
        remote(psend.at[0], precv.at[j], p_send.at[0], p_recv.at[j], (d, s, m)).wait_recv()
    attended = precv[0].astype(F32)
    for j in range(1, n):
        attended = attended + precv[j].astype(F32)
    xnew[...] = (xbuf[m].astype(F32) + attended).astype(BF16)

    def next_copy(dm):
        return remote(xnew, xbuf.at[m], n_send.at[dm], x_recv.at[m], (d, 1, lax.rem(m + dm, n)))

    @pl.when(s == 0)
    def _():
        for dm in range(n):
            next_copy(dm).start()
        split_whitening()

    def pool_copy(ds, dm):
        return remote(
            pool.at[m],
            pool.at[m],
            pool_send.at[ds, dm],
            pool_recv.at[m],
            (d, lax.rem(s + ds, 2), lax.rem(m + dm, n)),
        )

    hops = [(ds, dm) for ds in range(2) for dm in range(n) if ds or dm]

    @pl.when(s == 1)
    def _():
        length = stat[lax.rem(d - m + n, n), 2 * n : 2 * n + 1, :]
        inside = lax.broadcasted_iota(jnp.int32, (8, frames_count), 1).astype(F32) < length
        weights = jnp.where(inside, 1.0, 0.0).astype(BF16)
        total = jnp.dot(weights, xnew[...], preferred_element_type=F32)
        pool[m] = total / length[:, 0:1]
        for ds, dm in hops:
            pool_copy(ds, dm).start()

    for u in range(n):
        @pl.when(jnp.logical_or(s == 0, m != u))
        def _():
            remote(pool.at[u], pool.at[u], pool_send.at[0, 0], pool_recv.at[u], (d, s, m)).wait_recv()

    loads[5].wait()
    row_ids = lax.broadcasted_iota(jnp.int32, (8, wide), 0)
    gathered = jnp.zeros((8, wide), F32)
    for u in range(n):
        gathered = jnp.where(row_ids == u, pool[u], gathered)
    rows[d] = gathered - slice_of(center_ref[...].reshape(1, full), d, n, wide)
    row_copies = []
    for k in range(1, n):
        copy = remote(rows.at[d], rows.at[d], row_send.at[k], row_recv.at[k], (lax.rem(d + k, n), s, m))
        copy.start()
        row_copies.append(copy)
    for k in range(1, n):
        source = lax.rem(d - k + n, n)
        remote(rows.at[source], rows.at[source], row_send.at[k], row_recv.at[k], (source, s, m)).wait_recv()
    result = jnp.zeros((32, emb_ref.shape[1]), F32)
    for part in range(n):
        parts = jnp.concatenate(list(three_parts(rows[part])) + [jnp.zeros((8, wide), F32)], axis=0).astype(BF16)
        for i in range(3):
            result += jnp.dot(
                parts, wh3[i, part * wide : (part + 1) * wide, :], preferred_element_type=F32
            )
    result = result[0:8] + result[8:16] + result[16:24]
    emb_ref[...] = result[0:n]

    for copy in stat_copies + g_copies + q_copies + c_copies + row_copies:
        copy.wait_send()
    for k in range(n):
        @pl.when(lax.rem(d - k + n, n) != m)
        def _():
            p_copy(k).wait_send()

    @pl.when(s == 0)
    def _():
        for dm in range(1, n):
            x0_copy(dm).wait_send()

        @pl.when(d != m)
        def _():
            x0_copy(0).wait_send()

        for dm in range(n):
            next_copy(dm).wait_send()

    @pl.when(s == 1)
    def _():
        for ds, dm in hops:
            pool_copy(ds, dm).wait_send()


def fused(n, frames, lengths, feature_proj, norm_gain, qkv_weight, out_weight, center, whitening):
    frames_count = frames.shape[1]
    wide = feature_proj.shape[1]
    qkv_cols = qkv_weight.shape[2]
    head_rows = out_weight.shape[1]
    out_cols = whitening.shape[1]
    vmem = pl.BlockSpec(memory_space=pltpu.VMEM)
    anywhere = pl.BlockSpec(memory_space=pl.ANY)
    dma = pltpu.SemaphoreType.DMA
    return pl.pallas_call(
        functools.partial(kernel, n),
        out_shape=jax.ShapeDtypeStruct((n, out_cols), F32),
        in_specs=[pl.BlockSpec(memory_space=pltpu.SMEM)] + [anywhere] * 7,
        out_specs=vmem,
        scratch_shapes=[
            pltpu.VMEM(frames.shape, BF16),
            pltpu.VMEM(feature_proj.shape[::-1], BF16),
            pltpu.VMEM(norm_gain.shape, F32),
            pltpu.VMEM(center.shape, F32),
            pltpu.VMEM((wide, qkv_cols), BF16),
            pltpu.VMEM((head_rows, wide), BF16),
            pltpu.VMEM((n * wide, out_cols), F32),
            pltpu.VMEM((3, n * wide, out_cols), BF16),
            pltpu.VMEM((n, 1, qkv_cols), F32),
            pltpu.VMEM((frames_count, wide), BF16),
            pltpu.VMEM((n, frames_count, wide), BF16),
            pltpu.VMEM((n, 16, 128), F32),
            pltpu.VMEM((n * frames_count, wide), BF16),
            pltpu.VMEM((n, frames_count, qkv_cols), F32),
            pltpu.VMEM((frames_count, qkv_cols), BF16),
        ]
        + [pltpu.VMEM((n, frames_count, stop - start), BF16) for start, stop in chunk_bounds(qkv_cols)] * 2
        + [
            pltpu.VMEM((n, frames_count, head_rows), BF16),
            pltpu.VMEM((n, frames_count, wide), BF16),
            pltpu.VMEM((n, frames_count, wide), BF16),
            pltpu.VMEM((frames_count, wide), BF16),
            pltpu.VMEM((n, 8, wide), F32),
            pltpu.VMEM((n, 8, wide), F32),
            dma((7,)),
            dma((n,)), dma((n,)),
            dma((n,)), dma((n,)),
            dma((n,)), dma((n,)),
            dma((3, n)), dma((3, n)),
            dma((n,)), dma((n,)),
            dma((n,)), dma((n,)),
            dma((n,)),
            dma((2, n)), dma((n,)),
            dma((n,)), dma((n,)),
        ],
        compiler_params=pltpu.CompilerParams(
            collective_id=0, has_side_effects=True, vmem_limit_bytes=60 * 1024 * 1024
        ),
    )(
        lengths,
        frames,
        feature_proj.T,
        norm_gain,
        center,
        qkv_weight.reshape(qkv_weight.shape[1:]),
        out_weight.reshape(out_weight.shape[1:]),
        whitening,
    )


def solution(mesh):
    in_specs = (
        P("dp", None, None),
        P("dp"),
        P(None, "mp"),
        P("section", None),
        P("section", "dp", "mp"),
        P("section", "mp", "dp"),
        P(),
        P(None, "dp"),
    )
    out_specs = P(None, "dp")

    def step(frames, lengths, feature_proj, norm_gain, qkv_weight, out_weight, center, whitening):
        n = mesh.shape["mp"]
        square = mesh.shape["dp"] == n and mesh.shape["section"] == 2
        square = square and frames.shape[0] == 1 and frames.shape[1] == 128 and 2 * n < 16
        square = square and qkv_weight.shape[2] == 3 * n * HD and qkv_weight.shape[1] == feature_proj.shape[1]
        if square:
            return fused(
                n, frames, lengths, feature_proj, norm_gain, qkv_weight, out_weight, center, whitening
            )
        return body(frames, lengths, feature_proj, norm_gain, qkv_weight, out_weight, center, whitening)

    return jax.shard_map(step, mesh=mesh, in_specs=in_specs, out_specs=out_specs, check_vma=False)
```

```python
import functools

import jax
import jax.numpy as jnp
from jax import lax
from jax.experimental import pallas as pl
from jax.experimental.pallas import tpu as pltpu
from jax.sharding import PartitionSpec as P

MESH = pl.DeviceIdType.MESH
BF16 = jnp.bfloat16
F32 = jnp.float32

HD = 120


def passed_along(x, axis, by):
    count = lax.axis_size(axis)
    pairs = [(i, i + by) for i in range(count) if 0 <= i + by < count]
    return lax.ppermute(x, axis, pairs)


def broadcast(value, axis, source):
    kept = jnp.where(lax.axis_index(axis) == source, value, 0).astype(value.dtype)
    return lax.psum(kept, axis)


def layer_norm(values, gain):
    mean = jnp.mean(values, axis=-1, keepdims=True)
    centered = values - mean
    var = jnp.mean(centered * centered, axis=-1, keepdims=True)
    return centered * lax.rsqrt(var + 1e-05) * gain


def body(frames, lengths, feature_proj, norm_gain, qkv_weight, out_weight, center, whitening):
    section_index = lax.axis_index("section")
    gain = norm_gain[0]
    qkv_local = qkv_weight[0]
    out_local = out_weight[0]
    count_utt = frames.shape[0]
    frames_count = frames.shape[1]
    width = gain.shape[0]
    qkv_cols = qkv_local.shape[1]
    heads_local = qkv_cols // (3 * HD)
    full_qkv, full_out = (
        lax.all_gather(qkv_local, "dp", axis=0, tiled=True),
        lax.all_gather(out_local, "dp", axis=1, tiled=True),
    )
    received = jnp.zeros((frames_count, width), jnp.bfloat16)
    pooled_rows = []
    frame_ids = jnp.arange(frames_count, dtype=jnp.int32)
    for step in range(count_utt + 1):
        first_mb = min(step, count_utt - 1)
        second_mb = max(step - 1, 0)
        projected_part = jnp.dot(
            frames[first_mb], feature_proj, preferred_element_type=jnp.float32
        ).astype(jnp.bfloat16)
        projected = lax.all_gather(projected_part, "mp", axis=1, tiled=True)
        first_section = section_index == 0
        layer_input = jnp.where(first_section, projected, received)
        length = jnp.where(first_section, lengths[first_mb], lengths[second_mb])
        normed = layer_norm(layer_input.astype(jnp.float32), gain).astype(jnp.bfloat16)
        qkv_sum = jnp.dot(normed, full_qkv, preferred_element_type=jnp.float32)
        qkv = qkv_sum.astype(jnp.bfloat16).reshape(frames_count, 3, heads_local, HD)
        query = qkv[:, 0]
        keys = qkv[:, 1]
        values = qkv[:, 2]
        scores = jnp.einsum(
            "qhd,khd->hqk", query, keys, preferred_element_type=jnp.float32
        ) / jnp.sqrt(jnp.float32(HD))
        attention_valid = jnp.arange(frames_count, dtype=jnp.int32) < length
        scores = jnp.where(attention_valid[None, None, :], scores, jnp.float32(-1e30))
        probs = jax.nn.softmax(scores, axis=-1).astype(jnp.bfloat16)
        context = jnp.einsum(
            "hqk,khd->qhd", probs, values, preferred_element_type=jnp.float32
        ).astype(jnp.bfloat16)
        context = context.reshape(frames_count, heads_local * HD)
        partial_out = jnp.dot(context, full_out, preferred_element_type=jnp.float32)
        attended = lax.psum(partial_out.astype(jnp.bfloat16), "mp").astype(jnp.float32)
        result = (layer_input.astype(jnp.float32) + attended).astype(jnp.bfloat16)
        if step >= 1:
            valid = frame_ids < lengths[step - 1]
            summed = jnp.sum(
                jnp.where(valid[:, None], result.astype(jnp.float32), jnp.float32(0.0)), axis=0
            )
            pooled_rows.append(summed / lengths[step - 1].astype(jnp.float32))
        if step < count_utt:
            received = passed_along(result, "section", 1)
    pooled = jnp.stack(pooled_rows, axis=0)
    pooled = broadcast(pooled, "section", 1)
    return jnp.dot(
        lax.all_gather(pooled, "dp", axis=0, tiled=True) - center,
        whitening,
        precision=lax.Precision.HIGHEST,
        preferred_element_type=jnp.float32,
    )


def slice_of(row, index, count, size):
    value = jnp.zeros((1, size), F32)
    for part in range(count):
        value += jnp.where(index == part, row[:, part * size : (part + 1) * size], 0.0)
    return value


def three_parts(value):
    high = value.astype(BF16).astype(F32)
    rest = value - high
    middle = rest.astype(BF16).astype(F32)
    return high, middle, rest - middle


def kernel(
    n,
    lengths_ref,
    frames_hbm,
    proj_hbm,
    gain_hbm,
    center_hbm,
    qkv_hbm,
    out_hbm,
    white_hbm,
    emb_ref,
    frames_ref,
    proj_ref,
    gain_ref,
    center_ref,
    wq,
    wq2,
    wo,
    wh,
    wh3,
    gsend,
    gsum,
    x0buf,
    xbuf,
    stat,
    normed,
    qkv,
    qsend,
    qrecv,
    ctx,
    psend,
    precv,
    xnew,
    pool,
    rows,
    load_sem,
    x_send,
    x_recv,
    stat_send,
    stat_recv,
    g_send,
    g_recv,
    q_send,
    q_recv,
    c_send,
    c_recv,
    p_send,
    p_recv,
    n_send,
    pool_send,
    pool_recv,
    row_send,
    row_recv,
):
    d = lax.axis_index("dp")
    s = lax.axis_index("section")
    m = lax.axis_index("mp")
    pieces, part_rows, wide = xbuf.shape
    frames_count = 2 * part_rows
    full = n * wide
    half = n // 2 * HD
    groups = 2
    my_utt, my_half = d // 2, lax.rem(d, 2)
    pairs = (
        (frames_hbm, frames_ref),
        (proj_hbm, proj_ref),
        (gain_hbm, gain_ref),
        (qkv_hbm, wq),
        (out_hbm, wo),
        (center_hbm, center_ref),
        (white_hbm, wh),
    )
    loads = [pltpu.make_async_copy(src, dst, load_sem.at[i]) for i, (src, dst) in enumerate(pairs)]
    for load in loads:
        load.start()

    barrier = pltpu.get_barrier_semaphore()
    for dz in range(n):
        for dm in range(n):
            if dz or dm:
                pl.semaphore_signal(
                    barrier, inc=1, device_id=(lax.rem(d + dz, n), s, lax.rem(m + dm, n)), device_id_type=MESH
                )
    for dm in range(n):
        pl.semaphore_signal(barrier, inc=1, device_id=(d, 1 - s, lax.rem(m + dm, n)), device_id_type=MESH)

    loads[0].wait()
    loads[1].wait()

    @pl.when(s == 0)
    def _():
        projected = lax.dot_general(
            frames_ref[0], proj_ref[...], (((1,), (1,)), ((), ())), preferred_element_type=F32
        ).astype(BF16)
        x0buf[0] = projected[:part_rows]
        x0buf[1] = projected[part_rows:]

    pl.semaphore_wait(barrier, n * n - 1 + n)

    def remote(src, dst, send, recv, target):
        return pltpu.make_async_remote_copy(
            src_ref=src, dst_ref=dst, send_sem=send, recv_sem=recv, device_id=target, device_id_type=MESH
        )

    def arrived(dst, recv):
        remote(dst, dst, x_send.at[0], recv, (d, s, m)).wait_recv()

    def above(k):
        return lax.rem(d + k, n), s, m

    def below(k):
        return lax.rem(d - k + n, n)

    sent = []

    def x0_copy(dm):
        return remote(
            x0buf, xbuf.at[pl.ds(2 * d, 2)], x_send.at[dm], x_recv.at[2 * d], (m, s, lax.rem(m + dm, n))
        )

    @pl.when(s == 0)
    def _():
        for dm in range(1, n):
            x0_copy(dm).start()

        @pl.when(d != m)
        def _():
            x0_copy(0).start()

        @pl.when(d == m)
        def _():
            xbuf[pl.ds(2 * d, 2)] = x0buf[...]

    loads[2].wait()
    gain = slice_of(gain_ref, d, n, wide)
    ids = lax.broadcasted_iota(jnp.int32, (16, wide), 0)
    gain_rows = jnp.zeros((16, wide), F32)
    for part, value in enumerate(three_parts(gain)):
        gain_rows = jnp.where(ids == part, value, gain_rows)
    gain_rows = gain_rows.astype(BF16)
    loads[3].wait()
    for h in range(2):
        for t in range(3):
            start = (2 * t + h) * half
            wq2[h, :, t * half : (t + 1) * half] = wq[:, start : start + half]
        products = jnp.dot(gain_rows, wq2[h], preferred_element_type=F32)
        gsend[h] = products[0:1] + products[1:2] + products[2:3]
    gsum[d] = gsend[my_half]
    for k in range(1, n):
        copy = remote(gsend.at[lax.rem(d + k, 2)], gsum.at[d], g_send.at[k], g_recv.at[d], above(k))
        copy.start()
        sent.append(copy)

    def split_whitening():
        loads[6].wait()
        for part in range(n):
            run = slice(part * wide, (part + 1) * wide)
            for i, value in enumerate(three_parts(wh[run])):
                wh3[i, run] = value.astype(BF16)

    @pl.when(s == 1)
    def _():
        split_whitening()

    lanes = lax.broadcasted_iota(jnp.int32, (frames_count, 128), 1)
    length_row = 4

    def q_copy(g, to):
        return remote(qsend.at[g, to], qrecv.at[g, d], q_send.at[g, to], q_recv.at[g, d], (to, s, m))

    def stat_copy(g, k):
        return remote(stat.at[g, d], stat.at[g, d], stat_send.at[g, k], stat_recv.at[g, d], above(k))

    def project(g):
        for i in range(2):
            u = 2 * g + i

            @pl.when(jnp.logical_and(s == 0, jnp.logical_or(d != u, m != d)))
            def _():
                arrived(xbuf.at[pl.ds(2 * u, 2)], x_recv.at[2 * u])

            @pl.when(s == 1)
            def _():
                arrived(xbuf.at[2 * u], x_recv.at[2 * u])
                arrived(xbuf.at[2 * u + 1], x_recv.at[2 * u + 1])

        table = jnp.zeros((frames_count, 128), F32)
        for i in range(2):
            u = 2 * g + i
            x = jnp.concatenate([xbuf[2 * u], xbuf[2 * u + 1]], axis=0).astype(F32)
            mean = jnp.sum(x, axis=1, keepdims=True) * (1.0 / wide)
            centered = x - mean
            spread = jnp.sum(centered * centered, axis=1, keepdims=True)
            table = jnp.where(lanes == 2 * i, mean, table)
            table = jnp.where(lanes == 2 * i + 1, spread, table)
            normed[g, i * frames_count : (i + 1) * frames_count] = (centered * gain).astype(BF16)
        table = jnp.where(lanes == length_row, lengths_ref[0].astype(F32), table)
        for h in range(2):
            partial = jnp.dot(normed[g], wq2[h], preferred_element_type=F32).astype(BF16)
            for i in range(2):
                to = 2 * i + h
                qsend[g, to] = partial[i * frames_count : (i + 1) * frames_count]

                @pl.when(d != to)
                def _():
                    q_copy(g, to).start()

                @pl.when(d == to)
                def _():
                    qrecv[g, to] = qsend[g, to]

            if h == 0:
                stat[g, d] = table.T[0:8]
                for k in range(1, n):
                    stat_copy(g, k).start()

    stat_ids = lax.broadcasted_iota(jnp.int32, (8, 128), 0)
    columns = lax.broadcasted_iota(jnp.int32, (frames_count, half), 1)
    keys_ids = lax.broadcasted_iota(jnp.int32, (frames_count, frames_count), 1).astype(F32)

    def attend(g):
        for k in range(1, n):
            arrived(stat.at[g, below(k)], stat_recv.at[g, below(k)])
            if g == 0:
                arrived(gsum.at[below(k)], g_recv.at[below(k)])

        def stat_row(k, row):
            return jnp.sum(jnp.where(stat_ids == row, stat[g, k], 0.0), axis=0, keepdims=True)

        slice_means = [stat_row(k, 2 * my_utt) for k in range(n)]
        mean = sum(slice_means) * (1.0 / n)
        deltas = [value - mean for value in slice_means]
        spread = sum(stat_row(k, 2 * my_utt + 1) for k in range(n)) + wide * sum(value * value for value in deltas)
        rstd = lax.rsqrt(spread * (1.0 / full) + 1e-05)
        by_row = jnp.zeros((8, 128), F32)
        for k, value in enumerate(deltas + [rstd]):
            by_row = jnp.where(stat_ids == k, value, by_row)
        by_frame = jnp.concatenate([by_row, jnp.zeros((frames_count - 8, 128), F32)], axis=0).T
        length = stat[g, 2 * g + my_utt, length_row : length_row + 1, :]
        valid = keys_ids < length
        for k in range(1, n):
            arrived(qrecv.at[g, below(k)], q_recv.at[g, below(k)])
        summed = qrecv[g, 0].astype(F32) + by_frame[:, 0:1] * gsum[0]
        for k in range(1, n):
            summed = summed + qrecv[g, k].astype(F32) + by_frame[:, k : k + 1] * gsum[k]
        qkv[g] = (summed * by_frame[:, n : n + 1]).astype(BF16)
        query = qkv[g, :, 0:half]
        keys = qkv[g, :, half : 2 * half]
        values = qkv[g, :, 2 * half : 3 * half]
        context = jnp.zeros((frames_count, half), F32)
        for h in range(half // HD):
            in_head = jnp.logical_and(columns >= h * HD, columns < (h + 1) * HD)
            head_query = jnp.where(in_head, query, jnp.zeros_like(query))
            head_values = jnp.where(in_head, values, jnp.zeros_like(values))
            scores = lax.dot_general(
                head_query, keys, (((1,), (1,)), ((), ())), preferred_element_type=F32
            ) / jnp.sqrt(F32(HD))
            scores = jnp.where(valid, scores, F32(-1e30))
            weights = jnp.exp(scores - jnp.max(scores, axis=1, keepdims=True))
            probs = (weights / jnp.sum(weights, axis=1, keepdims=True)).astype(BF16)
            context += jnp.dot(probs, head_values, preferred_element_type=F32)
        ctx[g, d] = context.astype(BF16)
        for k in (2, 1, 3):
            copy = remote(ctx.at[g, d], ctx.at[g, d], c_send.at[g, k], c_recv.at[g, d], above(k))
            copy.start()
            sent.append(copy)

    def p_copy(g, to):
        return remote(psend.at[g, to], precv.at[g, m], p_send.at[g, to], p_recv.at[g, m], (d, s, to))

    def put_out(g):
        if g == 0:
            loads[4].wait()
        for i in range(2):
            total = jnp.zeros((frames_count, wide), F32)
            for h in range(2):
                source = 2 * i + h

                @pl.when(d != source)
                def _():
                    arrived(ctx.at[g, source], c_recv.at[g, source])

                total += jnp.dot(ctx[g, source], wo[h * half : (h + 1) * half], preferred_element_type=F32)
            total = total.astype(BF16)
            for h in range(2):
                to = 2 * i + h
                psend[g, to] = total[h * part_rows : (h + 1) * part_rows]

                @pl.when(m != to)
                def _():
                    p_copy(g, to).start()

                @pl.when(m == to)
                def _():
                    precv[g, to] = psend[g, to]

    def next_copy(g, dm):
        return remote(
            xnew.at[g], xbuf.at[n * g + m], n_send.at[g, dm], x_recv.at[n * g + m], (d, 1, lax.rem(m + dm, n))
        )

    def pool_copy(g, ds, dm):
        return remote(
            pool.at[g, m],
            pool.at[g, m],
            pool_send.at[g, ds, dm],
            pool_recv.at[g, m],
            (d, lax.rem(s + ds, 2), lax.rem(m + dm, n)),
        )

    hops = [(ds, dm) for ds in range(2) for dm in range(n) if ds or dm]

    def finish(g):
        for k in range(1, n):
            source = lax.rem(m - k + n, n)
            arrived(precv.at[g, source], p_recv.at[g, source])
        attended = precv[g, 0].astype(F32)
        for k in range(1, n):
            attended = attended + precv[g, k].astype(F32)
        xnew[g] = (xbuf[n * g + m].astype(F32) + attended).astype(BF16)

        @pl.when(s == 0)
        def _():
            for dm in range(n):
                next_copy(g, dm).start()

        @pl.when(s == 1)
        def _():
            length = stat[g, 2 * g + m // 2, length_row : length_row + 1, :]
            frame = lax.broadcasted_iota(jnp.int32, (8, part_rows), 1) + part_rows * lax.rem(m, 2)
            weights = jnp.where(frame.astype(F32) < length[:, :part_rows], 1.0, 0.0).astype(BF16)
            pool[g, m] = jnp.dot(weights, xnew[g], preferred_element_type=F32)
            for ds, dm in hops:
                pool_copy(g, ds, dm).start()

    project(0)

    @pl.when(s == 0)
    def _():
        project(1)

    attend(0)

    @pl.when(s == 1)
    def _():
        project(1)

    put_out(0)
    finish(0)
    attend(1)
    put_out(1)
    finish(1)

    @pl.when(s == 0)
    def _():
        split_whitening()

    loads[5].wait()
    row_ids = lax.broadcasted_iota(jnp.int32, (8, wide), 0)
    gathered = jnp.zeros((8, wide), F32)
    for u in range(n):
        g, i = u // 2, u % 2
        for source in (2 * i, 2 * i + 1):
            @pl.when(jnp.logical_or(s == 0, m != source))
            def _():
                arrived(pool.at[g, source], pool_recv.at[g, source])

        total = pool[g, 2 * i] + pool[g, 2 * i + 1]
        length = stat[g, u, length_row : length_row + 1, 0:1]
        gathered = jnp.where(row_ids == u, total / length, gathered)
    rows[d] = gathered - slice_of(center_ref[...].reshape(1, full), d, n, wide)
    for k in range(1, n):
        copy = remote(rows.at[d], rows.at[d], row_send.at[k], row_recv.at[d], above(k))
        copy.start()
        sent.append(copy)
    for k in range(1, n):
        arrived(rows.at[below(k)], row_recv.at[below(k)])
    result = jnp.zeros((32, emb_ref.shape[1]), F32)
    for part in range(n):
        parts = jnp.concatenate(list(three_parts(rows[part])) + [jnp.zeros((8, wide), F32)], axis=0).astype(BF16)
        for i in range(3):
            result += jnp.dot(
                parts, wh3[i, part * wide : (part + 1) * wide, :], preferred_element_type=F32
            )
    result = result[0:8] + result[8:16] + result[16:24]
    emb_ref[...] = result[0:n]

    for copy in sent:
        copy.wait_send()
    for g in range(groups):
        for k in range(1, n):
            stat_copy(g, k).wait_send()
        for to in range(n):
            @pl.when(d != to)
            def _():
                q_copy(g, to).wait_send()

            @pl.when(m != to)
            def _():
                p_copy(g, to).wait_send()

    @pl.when(s == 0)
    def _():
        for dm in range(1, n):
            x0_copy(dm).wait_send()

        @pl.when(d != m)
        def _():
            x0_copy(0).wait_send()

        for g in range(groups):
            for dm in range(n):
                next_copy(g, dm).wait_send()

    @pl.when(s == 1)
    def _():
        for g in range(groups):
            for ds, dm in hops:
                pool_copy(g, ds, dm).wait_send()


def fused(n, frames, lengths, feature_proj, norm_gain, qkv_weight, out_weight, center, whitening):
    frames_count = frames.shape[1]
    wide = feature_proj.shape[1]
    qkv_cols = qkv_weight.shape[2]
    head_rows = out_weight.shape[1]
    out_cols = whitening.shape[1]
    rows, columns = frames_count // 2, qkv_cols // 2
    vmem = pl.BlockSpec(memory_space=pltpu.VMEM)
    anywhere = pl.BlockSpec(memory_space=pl.ANY)
    dma = pltpu.SemaphoreType.DMA
    return pl.pallas_call(
        functools.partial(kernel, n),
        out_shape=jax.ShapeDtypeStruct((n, out_cols), F32),
        in_specs=[pl.BlockSpec(memory_space=pltpu.SMEM)] + [anywhere] * 7,
        out_specs=vmem,
        scratch_shapes=[
            pltpu.VMEM(frames.shape, BF16),
            pltpu.VMEM(feature_proj.shape[::-1], BF16),
            pltpu.VMEM(norm_gain.shape, F32),
            pltpu.VMEM(center.shape, F32),
            pltpu.VMEM((wide, qkv_cols), BF16),
            pltpu.VMEM((2, wide, columns), BF16),
            pltpu.VMEM((head_rows, wide), BF16),
            pltpu.VMEM((n * wide, out_cols), F32),
            pltpu.VMEM((3, n * wide, out_cols), BF16),
            pltpu.VMEM((2, 1, columns), F32),
            pltpu.VMEM((n, 1, columns), F32),
            pltpu.VMEM((2, rows, wide), BF16),
            pltpu.VMEM((2 * n, rows, wide), BF16),
            pltpu.VMEM((2, n, 8, 128), F32),
            pltpu.VMEM((2, 2 * frames_count, wide), BF16),
            pltpu.VMEM((2, frames_count, columns), BF16),
            pltpu.VMEM((2, n, frames_count, columns), BF16),
            pltpu.VMEM((2, n, frames_count, columns), BF16),
            pltpu.VMEM((2, n, frames_count, head_rows // 2), BF16),
            pltpu.VMEM((2, n, rows, wide), BF16),
            pltpu.VMEM((2, n, rows, wide), BF16),
            pltpu.VMEM((2, rows, wide), BF16),
            pltpu.VMEM((2, n, 8, wide), F32),
            pltpu.VMEM((n, 8, wide), F32),
            dma((7,)),
            dma((n,)), dma((2 * n,)),
            dma((2, n)), dma((2, n)),
            dma((n,)), dma((n,)),
            dma((2, n)), dma((2, n)),
            dma((2, n)), dma((2, n)),
            dma((2, n)), dma((2, n)),
            dma((2, n)),
            dma((2, 2, n)), dma((2, n)),
            dma((n,)), dma((n,)),
        ],
        compiler_params=pltpu.CompilerParams(
            collective_id=0, has_side_effects=True, vmem_limit_bytes=60 * 1024 * 1024
        ),
    )(
        lengths,
        frames,
        feature_proj.T,
        norm_gain,
        center,
        qkv_weight.reshape(qkv_weight.shape[1:]),
        out_weight.reshape(out_weight.shape[1:]),
        whitening,
    )


def solution(mesh):
    in_specs = (
        P("dp", None, None),
        P("dp"),
        P(None, "mp"),
        P("section", None),
        P("section", "dp", "mp"),
        P("section", "mp", "dp"),
        P(),
        P(None, "dp"),
    )
    out_specs = P(None, "dp")

    def step(frames, lengths, feature_proj, norm_gain, qkv_weight, out_weight, center, whitening):
        n = mesh.shape["mp"]
        square = mesh.shape["dp"] == n and mesh.shape["section"] == 2
        square = square and n == 4 and frames.shape[0] == 1 and frames.shape[1] == 128
        square = square and qkv_weight.shape[2] == 3 * n * HD and qkv_weight.shape[1] == feature_proj.shape[1]
        if square:
            return fused(
                n, frames, lengths, feature_proj, norm_gain, qkv_weight, out_weight, center, whitening
            )
        return body(frames, lengths, feature_proj, norm_gain, qkv_weight, out_weight, center, whitening)

    return jax.shard_map(step, mesh=mesh, in_specs=in_specs, out_specs=out_specs, check_vma=False)
```

```python
import functools

import jax
import jax.numpy as jnp
from jax import lax
from jax.experimental import pallas as pl
from jax.experimental.pallas import tpu as pltpu
from jax.sharding import PartitionSpec as P

MESH = pl.DeviceIdType.MESH
BF16 = jnp.bfloat16
F32 = jnp.float32

HD = 120


def passed_along(x, axis, by):
    count = lax.axis_size(axis)
    pairs = [(i, i + by) for i in range(count) if 0 <= i + by < count]
    return lax.ppermute(x, axis, pairs)


def broadcast(value, axis, source):
    kept = jnp.where(lax.axis_index(axis) == source, value, 0).astype(value.dtype)
    return lax.psum(kept, axis)


def layer_norm(values, gain):
    mean = jnp.mean(values, axis=-1, keepdims=True)
    centered = values - mean
    var = jnp.mean(centered * centered, axis=-1, keepdims=True)
    return centered * lax.rsqrt(var + 1e-05) * gain


def body(frames, lengths, feature_proj, norm_gain, qkv_weight, out_weight, center, whitening):
    section_index = lax.axis_index("section")
    gain = norm_gain[0]
    qkv_local = qkv_weight[0]
    out_local = out_weight[0]
    count_utt = frames.shape[0]
    frames_count = frames.shape[1]
    width = gain.shape[0]
    qkv_cols = qkv_local.shape[1]
    heads_local = qkv_cols // (3 * HD)
    full_qkv, full_out = (
        lax.all_gather(qkv_local, "dp", axis=0, tiled=True),
        lax.all_gather(out_local, "dp", axis=1, tiled=True),
    )
    received = jnp.zeros((frames_count, width), jnp.bfloat16)
    pooled_rows = []
    frame_ids = jnp.arange(frames_count, dtype=jnp.int32)
    for step in range(count_utt + 1):
        first_mb = min(step, count_utt - 1)
        second_mb = max(step - 1, 0)
        projected_part = jnp.dot(
            frames[first_mb], feature_proj, preferred_element_type=jnp.float32
        ).astype(jnp.bfloat16)
        projected = lax.all_gather(projected_part, "mp", axis=1, tiled=True)
        first_section = section_index == 0
        layer_input = jnp.where(first_section, projected, received)
        length = jnp.where(first_section, lengths[first_mb], lengths[second_mb])
        normed = layer_norm(layer_input.astype(jnp.float32), gain).astype(jnp.bfloat16)
        qkv_sum = jnp.dot(normed, full_qkv, preferred_element_type=jnp.float32)
        qkv = qkv_sum.astype(jnp.bfloat16).reshape(frames_count, 3, heads_local, HD)
        query = qkv[:, 0]
        keys = qkv[:, 1]
        values = qkv[:, 2]
        scores = jnp.einsum(
            "qhd,khd->hqk", query, keys, preferred_element_type=jnp.float32
        ) / jnp.sqrt(jnp.float32(HD))
        attention_valid = jnp.arange(frames_count, dtype=jnp.int32) < length
        scores = jnp.where(attention_valid[None, None, :], scores, jnp.float32(-1e30))
        probs = jax.nn.softmax(scores, axis=-1).astype(jnp.bfloat16)
        context = jnp.einsum(
            "hqk,khd->qhd", probs, values, preferred_element_type=jnp.float32
        ).astype(jnp.bfloat16)
        context = context.reshape(frames_count, heads_local * HD)
        partial_out = jnp.dot(context, full_out, preferred_element_type=jnp.float32)
        attended = lax.psum(partial_out.astype(jnp.bfloat16), "mp").astype(jnp.float32)
        result = (layer_input.astype(jnp.float32) + attended).astype(jnp.bfloat16)
        if step >= 1:
            valid = frame_ids < lengths[step - 1]
            summed = jnp.sum(
                jnp.where(valid[:, None], result.astype(jnp.float32), jnp.float32(0.0)), axis=0
            )
            pooled_rows.append(summed / lengths[step - 1].astype(jnp.float32))
        if step < count_utt:
            received = passed_along(result, "section", 1)
    pooled = jnp.stack(pooled_rows, axis=0)
    pooled = broadcast(pooled, "section", 1)
    return jnp.dot(
        lax.all_gather(pooled, "dp", axis=0, tiled=True) - center,
        whitening,
        precision=lax.Precision.HIGHEST,
        preferred_element_type=jnp.float32,
    )


def slice_of(row, index, count, size):
    value = jnp.zeros((1, size), F32)
    for part in range(count):
        value += jnp.where(index == part, row[:, part * size : (part + 1) * size], 0.0)
    return value


def three_parts(value):
    high = value.astype(BF16).astype(F32)
    rest = value - high
    middle = rest.astype(BF16).astype(F32)
    return high, middle, rest - middle


def whole_lanes(columns):
    return -(-columns // 128) * 128


def kernel(
    n,
    lengths_ref,
    frames_hbm,
    proj_hbm,
    gain_hbm,
    center_hbm,
    qkv_hbm,
    out_hbm,
    white_hbm,
    emb_ref,
    frames_ref,
    proj_ref,
    gain_ref,
    center_ref,
    wq,
    wq2,
    wo,
    wo2,
    wh,
    wh3,
    gsend,
    gsum,
    x0buf,
    xbuf,
    stat,
    normed,
    qkv,
    qsend,
    qrecv,
    ctx,
    psend,
    precv,
    xnew,
    pool,
    rows,
    load_sem,
    x_send,
    x_recv,
    stat_send,
    stat_recv,
    g_send,
    g_recv,
    q_send,
    q_recv,
    c_send,
    c_recv,
    p_send,
    p_recv,
    n_send,
    pool_send,
    pool_recv,
    row_send,
    row_recv,
):
    d = lax.axis_index("dp")
    s = lax.axis_index("section")
    m = lax.axis_index("mp")
    pieces, part_rows, lanes_x = xbuf.shape
    wide = wo.shape[1]
    frames_count = 2 * part_rows
    full = n * wide
    half = n // 2 * HD
    lanes_h = ctx.shape[3]
    pad_x, pad_h = lanes_x - wide, lanes_h - half
    groups = 2
    my_utt, my_half = d // 2, lax.rem(d, 2)
    pairs = (
        (frames_hbm, frames_ref),
        (proj_hbm, proj_ref.at[pl.ds(0, wide)]),
        (gain_hbm, gain_ref),
        (qkv_hbm, wq),
        (out_hbm, wo),
        (center_hbm, center_ref),
        (white_hbm, wh),
    )
    loads = [pltpu.make_async_copy(src, dst, load_sem.at[i]) for i, (src, dst) in enumerate(pairs)]
    for load in loads:
        load.start()

    barrier = pltpu.get_barrier_semaphore()
    for dz in range(n):
        for dm in range(n):
            if dz or dm:
                pl.semaphore_signal(
                    barrier, inc=1, device_id=(lax.rem(d + dz, n), s, lax.rem(m + dm, n)), device_id_type=MESH
                )
    for dm in range(n):
        pl.semaphore_signal(barrier, inc=1, device_id=(d, 1 - s, lax.rem(m + dm, n)), device_id_type=MESH)

    proj_ref[wide:] = jnp.zeros((pad_x, proj_ref.shape[1]), BF16)
    wq2[...] = jnp.zeros(wq2.shape, BF16)
    wo2[...] = jnp.zeros(wo2.shape, BF16)
    loads[0].wait()
    loads[1].wait()

    @pl.when(s == 0)
    def _():
        projected = lax.dot_general(
            frames_ref[0], proj_ref[...], (((1,), (1,)), ((), ())), preferred_element_type=F32
        ).astype(BF16)
        x0buf[0] = projected[:part_rows]
        x0buf[1] = projected[part_rows:]

    pl.semaphore_wait(barrier, n * n - 1 + n)

    def remote(src, dst, send, recv, target):
        return pltpu.make_async_remote_copy(
            src_ref=src, dst_ref=dst, send_sem=send, recv_sem=recv, device_id=target, device_id_type=MESH
        )

    def arrived(dst, recv):
        remote(dst, dst, x_send.at[0], recv, (d, s, m)).wait_recv()

    def above(k):
        return lax.rem(d + k, n), s, m

    def below(k):
        return lax.rem(d - k + n, n)

    sent = []

    def x0_copy(dm):
        return remote(
            x0buf, xbuf.at[pl.ds(2 * d, 2)], x_send.at[dm], x_recv.at[2 * d], (m, s, lax.rem(m + dm, n))
        )

    @pl.when(s == 0)
    def _():
        for dm in range(1, n):
            x0_copy(dm).start()

        @pl.when(d != m)
        def _():
            x0_copy(0).start()

        @pl.when(d == m)
        def _():
            xbuf[pl.ds(2 * d, 2)] = x0buf[...]

    loads[2].wait()
    gain = jnp.concatenate([slice_of(gain_ref, d, n, wide), jnp.zeros((1, pad_x), F32)], axis=1)
    ids = lax.broadcasted_iota(jnp.int32, (16, lanes_x), 0)
    gain_rows = jnp.zeros((16, lanes_x), F32)
    for part, value in enumerate(three_parts(gain)):
        gain_rows = jnp.where(ids == part, value, gain_rows)
    gain_rows = gain_rows.astype(BF16)
    loads[3].wait()
    for h in range(2):
        for t in range(3):
            start = (2 * t + h) * half
            wq2[h, 0:wide, t * lanes_h : t * lanes_h + half] = wq[:, start : start + half]
        products = jnp.dot(gain_rows, wq2[h], preferred_element_type=F32)
        gsend[h] = products[0:1] + products[1:2] + products[2:3]
    gsum[d] = gsend[my_half]
    for k in range(1, n):
        copy = remote(gsend.at[lax.rem(d + k, 2)], gsum.at[d], g_send.at[k], g_recv.at[d], above(k))
        copy.start()
        sent.append(copy)

    loads[4].wait()
    for h in range(2):
        wo2[h, 0:half, 0:wide] = wo[h * half : (h + 1) * half]

    def split_whitening():
        loads[6].wait()
        for part in range(n):
            for i, value in enumerate(three_parts(wh[part * wide : (part + 1) * wide])):
                wh3[i, part, 0:wide] = value.astype(BF16)
                wh3[i, part, wide:] = jnp.zeros((pad_x, wh3.shape[3]), BF16)

    @pl.when(s == 1)
    def _():
        split_whitening()

    lanes = lax.broadcasted_iota(jnp.int32, (frames_count, 128), 1)
    length_row = 4
    real = lax.broadcasted_iota(jnp.int32, (frames_count, lanes_x), 1) < wide

    def q_copy(g, to):
        return remote(qsend.at[g, to], qrecv.at[g, d], q_send.at[g, to], q_recv.at[g, d], (to, s, m))

    def stat_copy(g, k):
        return remote(stat.at[g, d], stat.at[g, d], stat_send.at[g, k], stat_recv.at[g, d], above(k))

    def project(g):
        for i in range(2):
            u = 2 * g + i

            @pl.when(jnp.logical_and(s == 0, jnp.logical_or(d != u, m != d)))
            def _():
                arrived(xbuf.at[pl.ds(2 * u, 2)], x_recv.at[2 * u])

            @pl.when(s == 1)
            def _():
                arrived(xbuf.at[2 * u], x_recv.at[2 * u])
                arrived(xbuf.at[2 * u + 1], x_recv.at[2 * u + 1])

        table = jnp.zeros((frames_count, 128), F32)
        for i in range(2):
            u = 2 * g + i
            x = jnp.concatenate([xbuf[2 * u], xbuf[2 * u + 1]], axis=0).astype(F32)
            mean = jnp.sum(x, axis=1, keepdims=True) * (1.0 / wide)
            centered = jnp.where(real, x - mean, 0.0)
            spread = jnp.sum(centered * centered, axis=1, keepdims=True)
            table = jnp.where(lanes == 2 * i, mean, table)
            table = jnp.where(lanes == 2 * i + 1, spread, table)
            normed[g, i * frames_count : (i + 1) * frames_count] = (centered * gain).astype(BF16)
        table = jnp.where(lanes == length_row, lengths_ref[0].astype(F32), table)
        for h in range(2):
            partial = jnp.dot(normed[g], wq2[h], preferred_element_type=F32).astype(BF16)
            for i in range(2):
                to = 2 * i + h
                qsend[g, to] = partial[i * frames_count : (i + 1) * frames_count]

                @pl.when(d != to)
                def _():
                    q_copy(g, to).start()

                @pl.when(d == to)
                def _():
                    qrecv[g, to] = qsend[g, to]

            if h == 0:
                stat[g, d] = table.T[0:8]
                for k in range(1, n):
                    stat_copy(g, k).start()

    stat_ids = lax.broadcasted_iota(jnp.int32, (8, 128), 0)
    columns = lax.broadcasted_iota(jnp.int32, (frames_count, lanes_h), 1)
    keys_ids = lax.broadcasted_iota(jnp.int32, (frames_count, frames_count), 1).astype(F32)

    def attend(g):
        for k in range(1, n):
            arrived(stat.at[g, below(k)], stat_recv.at[g, below(k)])
            if g == 0:
                arrived(gsum.at[below(k)], g_recv.at[below(k)])

        def stat_row(k, row):
            return jnp.sum(jnp.where(stat_ids == row, stat[g, k], 0.0), axis=0, keepdims=True)

        slice_means = [stat_row(k, 2 * my_utt) for k in range(n)]
        mean = sum(slice_means) * (1.0 / n)
        deltas = [value - mean for value in slice_means]
        spread = sum(stat_row(k, 2 * my_utt + 1) for k in range(n)) + wide * sum(value * value for value in deltas)
        rstd = lax.rsqrt(spread * (1.0 / full) + 1e-05)
        by_row = jnp.zeros((8, 128), F32)
        for k, value in enumerate(deltas + [rstd]):
            by_row = jnp.where(stat_ids == k, value, by_row)
        by_frame = jnp.concatenate([by_row, jnp.zeros((frames_count - 8, 128), F32)], axis=0).T
        length = stat[g, 2 * g + my_utt, length_row : length_row + 1, :]
        valid = keys_ids < length
        for k in range(1, n):
            arrived(qrecv.at[g, below(k)], q_recv.at[g, below(k)])
        summed = qrecv[g, 0].astype(F32) + by_frame[:, 0:1] * gsum[0]
        for k in range(1, n):
            summed = summed + qrecv[g, k].astype(F32) + by_frame[:, k : k + 1] * gsum[k]
        qkv[g] = (summed * by_frame[:, n : n + 1]).astype(BF16)
        query = qkv[g, :, 0:lanes_h]
        keys = qkv[g, :, lanes_h : 2 * lanes_h]
        values = qkv[g, :, 2 * lanes_h : 3 * lanes_h]
        context = jnp.zeros((frames_count, lanes_h), F32)
        for h in range(half // HD):
            in_head = jnp.logical_and(columns >= h * HD, columns < (h + 1) * HD)
            head_query = jnp.where(in_head, query, jnp.zeros_like(query))
            head_values = jnp.where(in_head, values, jnp.zeros_like(values))
            scores = lax.dot_general(
                head_query, keys, (((1,), (1,)), ((), ())), preferred_element_type=F32
            ) / jnp.sqrt(F32(HD))
            scores = jnp.where(valid, scores, F32(-1e30))
            weights = jnp.exp(scores - jnp.max(scores, axis=1, keepdims=True))
            probs = (weights / jnp.sum(weights, axis=1, keepdims=True)).astype(BF16)
            context += jnp.dot(probs, head_values, preferred_element_type=F32)
        ctx[g, d] = context.astype(BF16)
        for k in (2, 1, 3):
            copy = remote(ctx.at[g, d], ctx.at[g, d], c_send.at[g, k], c_recv.at[g, d], above(k))
            copy.start()
            sent.append(copy)

    def p_copy(g, to):
        return remote(psend.at[g, to], precv.at[g, m], p_send.at[g, to], p_recv.at[g, m], (d, s, to))

    def put_out(g):
        for i in range(2):
            total = jnp.zeros((frames_count, lanes_x), F32)
            for h in range(2):
                source = 2 * i + h

                @pl.when(d != source)
                def _():
                    arrived(ctx.at[g, source], c_recv.at[g, source])

                total += jnp.dot(ctx[g, source], wo2[h], preferred_element_type=F32)
            total = total.astype(BF16)
            for h in range(2):
                to = 2 * i + h
                psend[g, to] = total[h * part_rows : (h + 1) * part_rows]

                @pl.when(m != to)
                def _():
                    p_copy(g, to).start()

                @pl.when(m == to)
                def _():
                    precv[g, to] = psend[g, to]

    def next_copy(g, dm):
        return remote(
            xnew.at[g], xbuf.at[n * g + m], n_send.at[g, dm], x_recv.at[n * g + m], (d, 1, lax.rem(m + dm, n))
        )

    def pool_copy(g, ds, dm):
        return remote(
            pool.at[g, m],
            pool.at[g, m],
            pool_send.at[g, ds, dm],
            pool_recv.at[g, m],
            (d, lax.rem(s + ds, 2), lax.rem(m + dm, n)),
        )

    hops = [(ds, dm) for ds in range(2) for dm in range(n) if ds or dm]

    def finish(g):
        for k in range(1, n):
            source = lax.rem(m - k + n, n)
            arrived(precv.at[g, source], p_recv.at[g, source])
        attended = precv[g, 0].astype(F32)
        for k in range(1, n):
            attended = attended + precv[g, k].astype(F32)
        xnew[g] = (xbuf[n * g + m].astype(F32) + attended).astype(BF16)

        @pl.when(s == 0)
        def _():
            for dm in range(n):
                next_copy(g, dm).start()

        @pl.when(s == 1)
        def _():
            length = stat[g, 2 * g + m // 2, length_row : length_row + 1, :]
            frame = lax.broadcasted_iota(jnp.int32, (8, part_rows), 1) + part_rows * lax.rem(m, 2)
            weights = jnp.where(frame.astype(F32) < length[:, :part_rows], 1.0, 0.0).astype(BF16)
            pool[g, m] = jnp.dot(weights, xnew[g], preferred_element_type=F32)
            for ds, dm in hops:
                pool_copy(g, ds, dm).start()

    project(0)

    @pl.when(s == 0)
    def _():
        project(1)

    attend(0)

    @pl.when(s == 1)
    def _():
        project(1)

    put_out(0)
    finish(0)
    attend(1)
    put_out(1)
    finish(1)

    @pl.when(s == 0)
    def _():
        split_whitening()

    loads[5].wait()
    row_ids = lax.broadcasted_iota(jnp.int32, (8, lanes_x), 0)
    gathered = jnp.zeros((8, lanes_x), F32)
    for u in range(n):
        g, i = u // 2, u % 2
        for source in (2 * i, 2 * i + 1):
            @pl.when(jnp.logical_or(s == 0, m != source))
            def _():
                arrived(pool.at[g, source], pool_recv.at[g, source])

        total = pool[g, 2 * i] + pool[g, 2 * i + 1]
        length = stat[g, u, length_row : length_row + 1, 0:1]
        gathered = jnp.where(row_ids == u, total / length, gathered)
    center = slice_of(center_ref[...].reshape(1, full), d, n, wide)
    rows[d] = gathered - jnp.concatenate([center, jnp.zeros((1, pad_x), F32)], axis=1)
    for k in range(1, n):
        copy = remote(rows.at[d], rows.at[d], row_send.at[k], row_recv.at[d], above(k))
        copy.start()
        sent.append(copy)
    for k in range(1, n):
        arrived(rows.at[below(k)], row_recv.at[below(k)])
    result = jnp.zeros((32, emb_ref.shape[1]), F32)
    for part in range(n):
        parts = jnp.concatenate(list(three_parts(rows[part])) + [jnp.zeros((8, lanes_x), F32)], axis=0).astype(BF16)
        for i in range(3):
            result += jnp.dot(
                parts, wh3[i, part], preferred_element_type=F32
            )
    result = result[0:8] + result[8:16] + result[16:24]
    emb_ref[...] = result[0:n]

    for copy in sent:
        copy.wait_send()
    for g in range(groups):
        for k in range(1, n):
            stat_copy(g, k).wait_send()
        for to in range(n):
            @pl.when(d != to)
            def _():
                q_copy(g, to).wait_send()

            @pl.when(m != to)
            def _():
                p_copy(g, to).wait_send()

    @pl.when(s == 0)
    def _():
        for dm in range(1, n):
            x0_copy(dm).wait_send()

        @pl.when(d != m)
        def _():
            x0_copy(0).wait_send()

        for g in range(groups):
            for dm in range(n):
                next_copy(g, dm).wait_send()

    @pl.when(s == 1)
    def _():
        for g in range(groups):
            for ds, dm in hops:
                pool_copy(g, ds, dm).wait_send()


def fused(n, frames, lengths, feature_proj, norm_gain, qkv_weight, out_weight, center, whitening):
    frames_count = frames.shape[1]
    wide = feature_proj.shape[1]
    qkv_cols = qkv_weight.shape[2]
    head_rows = out_weight.shape[1]
    out_cols = whitening.shape[1]
    rows, lanes_x, lanes_h = frames_count // 2, whole_lanes(wide), whole_lanes(head_rows // 2)
    columns = 3 * lanes_h
    vmem = pl.BlockSpec(memory_space=pltpu.VMEM)
    anywhere = pl.BlockSpec(memory_space=pl.ANY)
    dma = pltpu.SemaphoreType.DMA
    return pl.pallas_call(
        functools.partial(kernel, n),
        out_shape=jax.ShapeDtypeStruct((n, out_cols), F32),
        in_specs=[pl.BlockSpec(memory_space=pltpu.SMEM)] + [anywhere] * 7,
        out_specs=vmem,
        scratch_shapes=[
            pltpu.VMEM(frames.shape, BF16),
            pltpu.VMEM((lanes_x, feature_proj.shape[0]), BF16),
            pltpu.VMEM(norm_gain.shape, F32),
            pltpu.VMEM(center.shape, F32),
            pltpu.VMEM((wide, qkv_cols), BF16),
            pltpu.VMEM((2, lanes_x, columns), BF16),
            pltpu.VMEM((head_rows, wide), BF16),
            pltpu.VMEM((2, lanes_h, lanes_x), BF16),
            pltpu.VMEM((n * wide, out_cols), F32),
            pltpu.VMEM((3, n, lanes_x, out_cols), BF16),
            pltpu.VMEM((2, 1, columns), F32),
            pltpu.VMEM((n, 1, columns), F32),
            pltpu.VMEM((2, rows, lanes_x), BF16),
            pltpu.VMEM((2 * n, rows, lanes_x), BF16),
            pltpu.VMEM((2, n, 8, 128), F32),
            pltpu.VMEM((2, 2 * frames_count, lanes_x), BF16),
            pltpu.VMEM((2, frames_count, columns), BF16),
            pltpu.VMEM((2, n, frames_count, columns), BF16),
            pltpu.VMEM((2, n, frames_count, columns), BF16),
            pltpu.VMEM((2, n, frames_count, lanes_h), BF16),
            pltpu.VMEM((2, n, rows, lanes_x), BF16),
            pltpu.VMEM((2, n, rows, lanes_x), BF16),
            pltpu.VMEM((2, rows, lanes_x), BF16),
            pltpu.VMEM((2, n, 8, lanes_x), F32),
            pltpu.VMEM((n, 8, lanes_x), F32),
            dma((7,)),
            dma((n,)), dma((2 * n,)),
            dma((2, n)), dma((2, n)),
            dma((n,)), dma((n,)),
            dma((2, n)), dma((2, n)),
            dma((2, n)), dma((2, n)),
            dma((2, n)), dma((2, n)),
            dma((2, n)),
            dma((2, 2, n)), dma((2, n)),
            dma((n,)), dma((n,)),
        ],
        compiler_params=pltpu.CompilerParams(
            collective_id=0, has_side_effects=True, vmem_limit_bytes=60 * 1024 * 1024
        ),
    )(
        lengths,
        frames,
        feature_proj.T,
        norm_gain,
        center,
        qkv_weight.reshape(qkv_weight.shape[1:]),
        out_weight.reshape(out_weight.shape[1:]),
        whitening,
    )


def solution(mesh):
    in_specs = (
        P("dp", None, None),
        P("dp"),
        P(None, "mp"),
        P("section", None),
        P("section", "dp", "mp"),
        P("section", "mp", "dp"),
        P(),
        P(None, "dp"),
    )
    out_specs = P(None, "dp")

    def step(frames, lengths, feature_proj, norm_gain, qkv_weight, out_weight, center, whitening):
        n = mesh.shape["mp"]
        square = mesh.shape["dp"] == n and mesh.shape["section"] == 2
        square = square and n == 4 and frames.shape[0] == 1 and frames.shape[1] == 128
        square = square and qkv_weight.shape[2] == 3 * n * HD and qkv_weight.shape[1] == feature_proj.shape[1]
        if square:
            return fused(
                n, frames, lengths, feature_proj, norm_gain, qkv_weight, out_weight, center, whitening
            )
        return body(frames, lengths, feature_proj, norm_gain, qkv_weight, out_weight, center, whitening)

    return jax.shard_map(step, mesh=mesh, in_specs=in_specs, out_specs=out_specs, check_vma=False)
```

```python
import functools

import jax
import jax.numpy as jnp
from jax import lax
from jax.experimental import pallas as pl
from jax.experimental.pallas import tpu as pltpu
from jax.sharding import PartitionSpec as P

MESH = pl.DeviceIdType.MESH
BF16 = jnp.bfloat16
F32 = jnp.float32

HD = 120


def passed_along(x, axis, by):
    count = lax.axis_size(axis)
    pairs = [(i, i + by) for i in range(count) if 0 <= i + by < count]
    return lax.ppermute(x, axis, pairs)


def broadcast(value, axis, source):
    kept = jnp.where(lax.axis_index(axis) == source, value, 0).astype(value.dtype)
    return lax.psum(kept, axis)


def layer_norm(values, gain):
    mean = jnp.mean(values, axis=-1, keepdims=True)
    centered = values - mean
    var = jnp.mean(centered * centered, axis=-1, keepdims=True)
    return centered * lax.rsqrt(var + 1e-05) * gain


def body(frames, lengths, feature_proj, norm_gain, qkv_weight, out_weight, center, whitening):
    section_index = lax.axis_index("section")
    gain = norm_gain[0]
    qkv_local = qkv_weight[0]
    out_local = out_weight[0]
    count_utt = frames.shape[0]
    frames_count = frames.shape[1]
    width = gain.shape[0]
    qkv_cols = qkv_local.shape[1]
    heads_local = qkv_cols // (3 * HD)
    full_qkv, full_out = (
        lax.all_gather(qkv_local, "dp", axis=0, tiled=True),
        lax.all_gather(out_local, "dp", axis=1, tiled=True),
    )
    received = jnp.zeros((frames_count, width), jnp.bfloat16)
    pooled_rows = []
    frame_ids = jnp.arange(frames_count, dtype=jnp.int32)
    for step in range(count_utt + 1):
        first_mb = min(step, count_utt - 1)
        second_mb = max(step - 1, 0)
        projected_part = jnp.dot(
            frames[first_mb], feature_proj, preferred_element_type=jnp.float32
        ).astype(jnp.bfloat16)
        projected = lax.all_gather(projected_part, "mp", axis=1, tiled=True)
        first_section = section_index == 0
        layer_input = jnp.where(first_section, projected, received)
        length = jnp.where(first_section, lengths[first_mb], lengths[second_mb])
        normed = layer_norm(layer_input.astype(jnp.float32), gain).astype(jnp.bfloat16)
        qkv_sum = jnp.dot(normed, full_qkv, preferred_element_type=jnp.float32)
        qkv = qkv_sum.astype(jnp.bfloat16).reshape(frames_count, 3, heads_local, HD)
        query = qkv[:, 0]
        keys = qkv[:, 1]
        values = qkv[:, 2]
        scores = jnp.einsum(
            "qhd,khd->hqk", query, keys, preferred_element_type=jnp.float32
        ) / jnp.sqrt(jnp.float32(HD))
        attention_valid = jnp.arange(frames_count, dtype=jnp.int32) < length
        scores = jnp.where(attention_valid[None, None, :], scores, jnp.float32(-1e30))
        probs = jax.nn.softmax(scores, axis=-1).astype(jnp.bfloat16)
        context = jnp.einsum(
            "hqk,khd->qhd", probs, values, preferred_element_type=jnp.float32
        ).astype(jnp.bfloat16)
        context = context.reshape(frames_count, heads_local * HD)
        partial_out = jnp.dot(context, full_out, preferred_element_type=jnp.float32)
        attended = lax.psum(partial_out.astype(jnp.bfloat16), "mp").astype(jnp.float32)
        result = (layer_input.astype(jnp.float32) + attended).astype(jnp.bfloat16)
        if step >= 1:
            valid = frame_ids < lengths[step - 1]
            summed = jnp.sum(
                jnp.where(valid[:, None], result.astype(jnp.float32), jnp.float32(0.0)), axis=0
            )
            pooled_rows.append(summed / lengths[step - 1].astype(jnp.float32))
        if step < count_utt:
            received = passed_along(result, "section", 1)
    pooled = jnp.stack(pooled_rows, axis=0)
    pooled = broadcast(pooled, "section", 1)
    return jnp.dot(
        lax.all_gather(pooled, "dp", axis=0, tiled=True) - center,
        whitening,
        precision=lax.Precision.HIGHEST,
        preferred_element_type=jnp.float32,
    )


def slice_of(row, index, count, size):
    value = jnp.zeros((1, size), F32)
    for part in range(count):
        value += jnp.where(index == part, row[:, part * size : (part + 1) * size], 0.0)
    return value


def three_parts(value):
    high = value.astype(BF16).astype(F32)
    rest = value - high
    middle = rest.astype(BF16).astype(F32)
    return high, middle, rest - middle


def whole_lanes(columns):
    return -(-columns // 128) * 128


def kernel(
    n,
    lengths_ref,
    frames_hbm,
    proj_hbm,
    gain_hbm,
    center_hbm,
    qkv_hbm,
    out_hbm,
    white_hbm,
    emb_ref,
    frames_ref,
    proj_ref,
    gain_ref,
    center_ref,
    wq,
    wq2,
    wo,
    wo2,
    wh,
    wh3,
    gsend,
    gsum,
    x0buf,
    xbuf,
    stat,
    normed,
    qkv,
    qsend,
    qrecv,
    ctx,
    psend,
    precv,
    xnew,
    pool,
    rows,
    load_sem,
    x_send,
    x_recv,
    stat_send,
    stat_recv,
    g_send,
    g_recv,
    q_send,
    q_recv,
    c_send,
    c_recv,
    p_send,
    p_recv,
    n_send,
    pool_send,
    pool_recv,
    row_send,
    row_recv,
):
    d = lax.axis_index("dp")
    s = lax.axis_index("section")
    m = lax.axis_index("mp")
    pieces, part_rows, lanes_x = xbuf.shape
    wide = wo.shape[1]
    frames_count = 2 * part_rows
    full = n * wide
    half = n // 2 * HD
    lanes_h = ctx.shape[3]
    pad_x, pad_h = lanes_x - wide, lanes_h - half
    groups = 2
    my_utt, my_half = d // 2, lax.rem(d, 2)
    pairs = (
        (frames_hbm, frames_ref),
        (proj_hbm, proj_ref.at[pl.ds(0, wide)]),
        (gain_hbm, gain_ref),
        (qkv_hbm, wq),
        (out_hbm, wo),
        (center_hbm, center_ref),
        (white_hbm, wh),
    )
    loads = [pltpu.make_async_copy(src, dst, load_sem.at[i]) for i, (src, dst) in enumerate(pairs)]
    for load in loads:
        load.start()

    barrier = pltpu.get_barrier_semaphore()
    for dz in range(n):
        for dm in range(n):
            if dz or dm:
                pl.semaphore_signal(
                    barrier, inc=1, device_id=(lax.rem(d + dz, n), s, lax.rem(m + dm, n)), device_id_type=MESH
                )
    for dm in range(n):
        pl.semaphore_signal(barrier, inc=1, device_id=(d, 1 - s, lax.rem(m + dm, n)), device_id_type=MESH)

    proj_ref[wide:] = jnp.zeros((pad_x, proj_ref.shape[1]), BF16)
    wq2[...] = jnp.zeros(wq2.shape, BF16)
    wo2[...] = jnp.zeros(wo2.shape, BF16)
    loads[0].wait()
    loads[1].wait()

    @pl.when(s == 0)
    def _():
        projected = lax.dot_general(
            frames_ref[0], proj_ref[...], (((1,), (1,)), ((), ())), preferred_element_type=F32
        ).astype(BF16)
        x0buf[0] = projected[:part_rows]
        x0buf[1] = projected[part_rows:]

    pl.semaphore_wait(barrier, n * n - 1 + n)

    def remote(src, dst, send, recv, target):
        return pltpu.make_async_remote_copy(
            src_ref=src, dst_ref=dst, send_sem=send, recv_sem=recv, device_id=target, device_id_type=MESH
        )

    def arrived(dst, recv):
        remote(dst, dst, x_send.at[0], recv, (d, s, m)).wait_recv()

    def above(k):
        return lax.rem(d + k, n), s, m

    def below(k):
        return lax.rem(d - k + n, n)

    sent = []

    def x0_copy(dm):
        return remote(
            x0buf, xbuf.at[pl.ds(2 * d, 2)], x_send.at[dm], x_recv.at[2 * d], (m, s, lax.rem(m + dm, n))
        )

    @pl.when(s == 0)
    def _():
        for dm in range(1, n):
            x0_copy(dm).start()

        @pl.when(d != m)
        def _():
            x0_copy(0).start()

        @pl.when(d == m)
        def _():
            xbuf[pl.ds(2 * d, 2)] = x0buf[...]

    loads[2].wait()
    gain = jnp.concatenate([slice_of(gain_ref, d, n, wide), jnp.zeros((1, pad_x), F32)], axis=1)
    ids = lax.broadcasted_iota(jnp.int32, (16, lanes_x), 0)
    gain_rows = jnp.zeros((16, lanes_x), F32)
    for part, value in enumerate(three_parts(gain)):
        gain_rows = jnp.where(ids == part, value, gain_rows)
    gain_rows = gain_rows.astype(BF16)
    loads[3].wait()
    for h in range(2):
        for t in range(3):
            start = (2 * t + h) * half
            wq2[h, 0:wide, t * lanes_h : t * lanes_h + half] = wq[:, start : start + half]
        products = jnp.dot(gain_rows, wq2[h], preferred_element_type=F32)
        gsend[h] = products[0:1] + products[1:2] + products[2:3]
    gsum[d] = gsend[my_half]
    for k in range(1, n):
        copy = remote(gsend.at[lax.rem(d + k, 2)], gsum.at[d], g_send.at[k], g_recv.at[d], above(k))
        copy.start()
        sent.append(copy)

    loads[4].wait()
    for h in range(2):
        wo2[h, 0:half, 0:wide] = wo[h * half : (h + 1) * half]

    def split_whitening():
        loads[6].wait()
        for part in range(n):
            for i, value in enumerate(three_parts(wh[part * wide : (part + 1) * wide])):
                wh3[i, part, 0:wide] = value.astype(BF16)
                wh3[i, part, wide:] = jnp.zeros((pad_x, wh3.shape[3]), BF16)

    @pl.when(s == 1)
    def _():
        split_whitening()

    lanes = lax.broadcasted_iota(jnp.int32, (frames_count, 128), 1)
    length_row = 4
    real = lax.broadcasted_iota(jnp.int32, (frames_count, lanes_x), 1) < wide

    def q_copy(g, to):
        return remote(qsend.at[g, to], qrecv.at[g, d], q_send.at[g, to], q_recv.at[g, d], (to, s, m))

    def stat_copy(g, k):
        return remote(stat.at[g, d], stat.at[g, d], stat_send.at[g, k], stat_recv.at[g, d], above(k))

    def send_partials(g, tos):
        for to in tos:
            @pl.when(d != to)
            def _():
                q_copy(g, to).start()

    def project(g, send):
        for i in range(2):
            u = 2 * g + i

            @pl.when(jnp.logical_and(s == 0, jnp.logical_or(d != u, m != d)))
            def _():
                arrived(xbuf.at[pl.ds(2 * u, 2)], x_recv.at[2 * u])

            @pl.when(s == 1)
            def _():
                arrived(xbuf.at[2 * u], x_recv.at[2 * u])
                arrived(xbuf.at[2 * u + 1], x_recv.at[2 * u + 1])

        table = jnp.zeros((frames_count, 128), F32)
        for i in range(2):
            u = 2 * g + i
            x = jnp.concatenate([xbuf[2 * u], xbuf[2 * u + 1]], axis=0).astype(F32)
            mean = jnp.sum(x, axis=1, keepdims=True) * (1.0 / wide)
            centered = jnp.where(real, x - mean, 0.0)
            spread = jnp.sum(centered * centered, axis=1, keepdims=True)
            table = jnp.where(lanes == 2 * i, mean, table)
            table = jnp.where(lanes == 2 * i + 1, spread, table)
            normed[g, i * frames_count : (i + 1) * frames_count] = (centered * gain).astype(BF16)
        table = jnp.where(lanes == length_row, lengths_ref[0].astype(F32), table)
        for h in range(2):
            partial = jnp.dot(normed[g], wq2[h], preferred_element_type=F32).astype(BF16)
            for i in range(2):
                to = 2 * i + h
                qsend[g, to] = partial[i * frames_count : (i + 1) * frames_count]

                @pl.when(d == to)
                def _():
                    qrecv[g, to] = qsend[g, to]

            if send:
                send_partials(g, (h, 2 + h))
            if h == 0:
                stat[g, d] = table.T[0:8]
                for k in range(1, n):
                    stat_copy(g, k).start()

    stat_ids = lax.broadcasted_iota(jnp.int32, (8, 128), 0)
    columns = lax.broadcasted_iota(jnp.int32, (frames_count, lanes_h), 1)
    keys_ids = lax.broadcasted_iota(jnp.int32, (frames_count, frames_count), 1).astype(F32)

    def attend(g):
        for k in range(1, n):
            arrived(stat.at[g, below(k)], stat_recv.at[g, below(k)])
            if g == 0:
                arrived(gsum.at[below(k)], g_recv.at[below(k)])

        def stat_row(k, row):
            return jnp.sum(jnp.where(stat_ids == row, stat[g, k], 0.0), axis=0, keepdims=True)

        slice_means = [stat_row(k, 2 * my_utt) for k in range(n)]
        mean = sum(slice_means) * (1.0 / n)
        deltas = [value - mean for value in slice_means]
        spread = sum(stat_row(k, 2 * my_utt + 1) for k in range(n)) + wide * sum(value * value for value in deltas)
        rstd = lax.rsqrt(spread * (1.0 / full) + 1e-05)
        by_row = jnp.zeros((8, 128), F32)
        for k, value in enumerate(deltas + [rstd]):
            by_row = jnp.where(stat_ids == k, value, by_row)
        by_frame = jnp.concatenate([by_row, jnp.zeros((frames_count - 8, 128), F32)], axis=0).T
        length = stat[g, 2 * g + my_utt, length_row : length_row + 1, :]
        valid = keys_ids < length
        for k in range(1, n):
            arrived(qrecv.at[g, below(k)], q_recv.at[g, below(k)])
        if g == 0:
            @pl.when(s == 0)
            def _():
                send_partials(1, range(n))

        summed = qrecv[g, 0].astype(F32) + by_frame[:, 0:1] * gsum[0]
        for k in range(1, n):
            summed = summed + qrecv[g, k].astype(F32) + by_frame[:, k : k + 1] * gsum[k]
        qkv[g] = (summed * by_frame[:, n : n + 1]).astype(BF16)
        query = qkv[g, :, 0:lanes_h]
        keys = qkv[g, :, lanes_h : 2 * lanes_h]
        values = qkv[g, :, 2 * lanes_h : 3 * lanes_h]
        context = jnp.zeros((frames_count, lanes_h), F32)
        for h in range(half // HD):
            in_head = jnp.logical_and(columns >= h * HD, columns < (h + 1) * HD)
            head_query = jnp.where(in_head, query, jnp.zeros_like(query))
            head_values = jnp.where(in_head, values, jnp.zeros_like(values))
            scores = lax.dot_general(
                head_query, keys, (((1,), (1,)), ((), ())), preferred_element_type=F32
            ) / jnp.sqrt(F32(HD))
            scores = jnp.where(valid, scores, F32(-1e30))
            weights = jnp.exp(scores - jnp.max(scores, axis=1, keepdims=True))
            probs = (weights / jnp.sum(weights, axis=1, keepdims=True)).astype(BF16)
            context += jnp.dot(probs, head_values, preferred_element_type=F32)
        ctx[g, d] = context.astype(BF16)
        for k in (2, 1, 3):
            copy = remote(ctx.at[g, d], ctx.at[g, d], c_send.at[g, k], c_recv.at[g, d], above(k))
            copy.start()
            sent.append(copy)

    def p_copy(g, to):
        return remote(psend.at[g, to], precv.at[g, m], p_send.at[g, to], p_recv.at[g, m], (d, s, to))

    def put_out(g):
        for i in range(2):
            total = jnp.zeros((frames_count, lanes_x), F32)
            for h in range(2):
                source = 2 * i + h

                @pl.when(d != source)
                def _():
                    arrived(ctx.at[g, source], c_recv.at[g, source])

                total += jnp.dot(ctx[g, source], wo2[h], preferred_element_type=F32)
            total = total.astype(BF16)
            for h in range(2):
                to = 2 * i + h
                psend[g, to] = total[h * part_rows : (h + 1) * part_rows]

                @pl.when(m != to)
                def _():
                    p_copy(g, to).start()

                @pl.when(m == to)
                def _():
                    precv[g, to] = psend[g, to]

    def next_copy(g, dm):
        return remote(
            xnew.at[g], xbuf.at[n * g + m], n_send.at[g, dm], x_recv.at[n * g + m], (d, 1, lax.rem(m + dm, n))
        )

    def pool_copy(g, ds, dm):
        return remote(
            pool.at[g, m],
            pool.at[g, m],
            pool_send.at[g, ds, dm],
            pool_recv.at[g, m],
            (d, lax.rem(s + ds, 2), lax.rem(m + dm, n)),
        )

    hops = [(ds, dm) for ds in range(2) for dm in range(n) if ds or dm]

    def finish(g):
        for k in range(1, n):
            source = lax.rem(m - k + n, n)
            arrived(precv.at[g, source], p_recv.at[g, source])
        attended = precv[g, 0].astype(F32)
        for k in range(1, n):
            attended = attended + precv[g, k].astype(F32)
        xnew[g] = (xbuf[n * g + m].astype(F32) + attended).astype(BF16)

        @pl.when(s == 0)
        def _():
            for dm in range(n):
                next_copy(g, dm).start()

        @pl.when(s == 1)
        def _():
            length = stat[g, 2 * g + m // 2, length_row : length_row + 1, :]
            frame = lax.broadcasted_iota(jnp.int32, (8, part_rows), 1) + part_rows * lax.rem(m, 2)
            weights = jnp.where(frame.astype(F32) < length[:, :part_rows], 1.0, 0.0).astype(BF16)
            pool[g, m] = jnp.dot(weights, xnew[g], preferred_element_type=F32)
            for ds, dm in hops:
                pool_copy(g, ds, dm).start()

    project(0, True)

    @pl.when(s == 0)
    def _():
        project(1, False)

    attend(0)

    @pl.when(s == 1)
    def _():
        project(1, True)

    put_out(0)
    finish(0)
    attend(1)
    put_out(1)
    finish(1)

    @pl.when(s == 0)
    def _():
        split_whitening()

    loads[5].wait()
    row_ids = lax.broadcasted_iota(jnp.int32, (8, lanes_x), 0)
    gathered = jnp.zeros((8, lanes_x), F32)
    for u in range(n):
        g, i = u // 2, u % 2
        for source in (2 * i, 2 * i + 1):
            @pl.when(jnp.logical_or(s == 0, m != source))
            def _():
                arrived(pool.at[g, source], pool_recv.at[g, source])

        total = pool[g, 2 * i] + pool[g, 2 * i + 1]
        length = stat[g, u, length_row : length_row + 1, 0:1]
        gathered = jnp.where(row_ids == u, total / length, gathered)
    center = slice_of(center_ref[...].reshape(1, full), d, n, wide)
    rows[d] = gathered - jnp.concatenate([center, jnp.zeros((1, pad_x), F32)], axis=1)
    for k in range(1, n):
        copy = remote(rows.at[d], rows.at[d], row_send.at[k], row_recv.at[d], above(k))
        copy.start()
        sent.append(copy)
    for k in range(1, n):
        arrived(rows.at[below(k)], row_recv.at[below(k)])
    result = jnp.zeros((32, emb_ref.shape[1]), F32)
    for part in range(n):
        parts = jnp.concatenate(list(three_parts(rows[part])) + [jnp.zeros((8, lanes_x), F32)], axis=0).astype(BF16)
        for i in range(3):
            result += jnp.dot(
                parts, wh3[i, part], preferred_element_type=F32
            )
    result = result[0:8] + result[8:16] + result[16:24]
    emb_ref[...] = result[0:n]

    for copy in sent:
        copy.wait_send()
    for g in range(groups):
        for k in range(1, n):
            stat_copy(g, k).wait_send()
        for to in range(n):
            @pl.when(d != to)
            def _():
                q_copy(g, to).wait_send()

            @pl.when(m != to)
            def _():
                p_copy(g, to).wait_send()

    @pl.when(s == 0)
    def _():
        for dm in range(1, n):
            x0_copy(dm).wait_send()

        @pl.when(d != m)
        def _():
            x0_copy(0).wait_send()

        for g in range(groups):
            for dm in range(n):
                next_copy(g, dm).wait_send()

    @pl.when(s == 1)
    def _():
        for g in range(groups):
            for ds, dm in hops:
                pool_copy(g, ds, dm).wait_send()


def fused(n, frames, lengths, feature_proj, norm_gain, qkv_weight, out_weight, center, whitening):
    frames_count = frames.shape[1]
    wide = feature_proj.shape[1]
    qkv_cols = qkv_weight.shape[2]
    head_rows = out_weight.shape[1]
    out_cols = whitening.shape[1]
    rows, lanes_x, lanes_h = frames_count // 2, whole_lanes(wide), whole_lanes(head_rows // 2)
    columns = 3 * lanes_h
    vmem = pl.BlockSpec(memory_space=pltpu.VMEM)
    anywhere = pl.BlockSpec(memory_space=pl.ANY)
    dma = pltpu.SemaphoreType.DMA
    return pl.pallas_call(
        functools.partial(kernel, n),
        out_shape=jax.ShapeDtypeStruct((n, out_cols), F32),
        in_specs=[pl.BlockSpec(memory_space=pltpu.SMEM)] + [anywhere] * 7,
        out_specs=vmem,
        scratch_shapes=[
            pltpu.VMEM(frames.shape, BF16),
            pltpu.VMEM((lanes_x, feature_proj.shape[0]), BF16),
            pltpu.VMEM(norm_gain.shape, F32),
            pltpu.VMEM(center.shape, F32),
            pltpu.VMEM((wide, qkv_cols), BF16),
            pltpu.VMEM((2, lanes_x, columns), BF16),
            pltpu.VMEM((head_rows, wide), BF16),
            pltpu.VMEM((2, lanes_h, lanes_x), BF16),
            pltpu.VMEM((n * wide, out_cols), F32),
            pltpu.VMEM((3, n, lanes_x, out_cols), BF16),
            pltpu.VMEM((2, 1, columns), F32),
            pltpu.VMEM((n, 1, columns), F32),
            pltpu.VMEM((2, rows, lanes_x), BF16),
            pltpu.VMEM((2 * n, rows, lanes_x), BF16),
            pltpu.VMEM((2, n, 8, 128), F32),
            pltpu.VMEM((2, 2 * frames_count, lanes_x), BF16),
            pltpu.VMEM((2, frames_count, columns), BF16),
            pltpu.VMEM((2, n, frames_count, columns), BF16),
            pltpu.VMEM((2, n, frames_count, columns), BF16),
            pltpu.VMEM((2, n, frames_count, lanes_h), BF16),
            pltpu.VMEM((2, n, rows, lanes_x), BF16),
            pltpu.VMEM((2, n, rows, lanes_x), BF16),
            pltpu.VMEM((2, rows, lanes_x), BF16),
            pltpu.VMEM((2, n, 8, lanes_x), F32),
            pltpu.VMEM((n, 8, lanes_x), F32),
            dma((7,)),
            dma((n,)), dma((2 * n,)),
            dma((2, n)), dma((2, n)),
            dma((n,)), dma((n,)),
            dma((2, n)), dma((2, n)),
            dma((2, n)), dma((2, n)),
            dma((2, n)), dma((2, n)),
            dma((2, n)),
            dma((2, 2, n)), dma((2, n)),
            dma((n,)), dma((n,)),
        ],
        compiler_params=pltpu.CompilerParams(
            collective_id=0, has_side_effects=True, vmem_limit_bytes=60 * 1024 * 1024
        ),
    )(
        lengths,
        frames,
        feature_proj.T,
        norm_gain,
        center,
        qkv_weight.reshape(qkv_weight.shape[1:]),
        out_weight.reshape(out_weight.shape[1:]),
        whitening,
    )


def solution(mesh):
    in_specs = (
        P("dp", None, None),
        P("dp"),
        P(None, "mp"),
        P("section", None),
        P("section", "dp", "mp"),
        P("section", "mp", "dp"),
        P(),
        P(None, "dp"),
    )
    out_specs = P(None, "dp")

    def step(frames, lengths, feature_proj, norm_gain, qkv_weight, out_weight, center, whitening):
        n = mesh.shape["mp"]
        square = mesh.shape["dp"] == n and mesh.shape["section"] == 2
        square = square and n == 4 and frames.shape[0] == 1 and frames.shape[1] == 128
        square = square and qkv_weight.shape[2] == 3 * n * HD and qkv_weight.shape[1] == feature_proj.shape[1]
        if square:
            return fused(
                n, frames, lengths, feature_proj, norm_gain, qkv_weight, out_weight, center, whitening
            )
        return body(frames, lengths, feature_proj, norm_gain, qkv_weight, out_weight, center, whitening)

    return jax.shard_map(step, mesh=mesh, in_specs=in_specs, out_specs=out_specs, check_vma=False)
```

```python
import functools

import jax
import jax.numpy as jnp
from jax import lax
from jax.experimental import pallas as pl
from jax.experimental.pallas import tpu as pltpu
from jax.sharding import PartitionSpec as P

MESH = pl.DeviceIdType.MESH
BF16 = jnp.bfloat16
F32 = jnp.float32

HD = 120


def passed_along(x, axis, by):
    count = lax.axis_size(axis)
    pairs = [(i, i + by) for i in range(count) if 0 <= i + by < count]
    return lax.ppermute(x, axis, pairs)


def broadcast(value, axis, source):
    kept = jnp.where(lax.axis_index(axis) == source, value, 0).astype(value.dtype)
    return lax.psum(kept, axis)


def layer_norm(values, gain):
    mean = jnp.mean(values, axis=-1, keepdims=True)
    centered = values - mean
    var = jnp.mean(centered * centered, axis=-1, keepdims=True)
    return centered * lax.rsqrt(var + 1e-05) * gain


def body(frames, lengths, feature_proj, norm_gain, qkv_weight, out_weight, center, whitening):
    section_index = lax.axis_index("section")
    gain = norm_gain[0]
    qkv_local = qkv_weight[0]
    out_local = out_weight[0]
    count_utt = frames.shape[0]
    frames_count = frames.shape[1]
    width = gain.shape[0]
    qkv_cols = qkv_local.shape[1]
    heads_local = qkv_cols // (3 * HD)
    full_qkv, full_out = (
        lax.all_gather(qkv_local, "dp", axis=0, tiled=True),
        lax.all_gather(out_local, "dp", axis=1, tiled=True),
    )
    received = jnp.zeros((frames_count, width), jnp.bfloat16)
    pooled_rows = []
    frame_ids = jnp.arange(frames_count, dtype=jnp.int32)
    for step in range(count_utt + 1):
        first_mb = min(step, count_utt - 1)
        second_mb = max(step - 1, 0)
        projected_part = jnp.dot(
            frames[first_mb], feature_proj, preferred_element_type=jnp.float32
        ).astype(jnp.bfloat16)
        projected = lax.all_gather(projected_part, "mp", axis=1, tiled=True)
        first_section = section_index == 0
        layer_input = jnp.where(first_section, projected, received)
        length = jnp.where(first_section, lengths[first_mb], lengths[second_mb])
        normed = layer_norm(layer_input.astype(jnp.float32), gain).astype(jnp.bfloat16)
        qkv_sum = jnp.dot(normed, full_qkv, preferred_element_type=jnp.float32)
        qkv = qkv_sum.astype(jnp.bfloat16).reshape(frames_count, 3, heads_local, HD)
        query = qkv[:, 0]
        keys = qkv[:, 1]
        values = qkv[:, 2]
        scores = jnp.einsum(
            "qhd,khd->hqk", query, keys, preferred_element_type=jnp.float32
        ) / jnp.sqrt(jnp.float32(HD))
        attention_valid = jnp.arange(frames_count, dtype=jnp.int32) < length
        scores = jnp.where(attention_valid[None, None, :], scores, jnp.float32(-1e30))
        probs = jax.nn.softmax(scores, axis=-1).astype(jnp.bfloat16)
        context = jnp.einsum(
            "hqk,khd->qhd", probs, values, preferred_element_type=jnp.float32
        ).astype(jnp.bfloat16)
        context = context.reshape(frames_count, heads_local * HD)
        partial_out = jnp.dot(context, full_out, preferred_element_type=jnp.float32)
        attended = lax.psum(partial_out.astype(jnp.bfloat16), "mp").astype(jnp.float32)
        result = (layer_input.astype(jnp.float32) + attended).astype(jnp.bfloat16)
        if step >= 1:
            valid = frame_ids < lengths[step - 1]
            summed = jnp.sum(
                jnp.where(valid[:, None], result.astype(jnp.float32), jnp.float32(0.0)), axis=0
            )
            pooled_rows.append(summed / lengths[step - 1].astype(jnp.float32))
        if step < count_utt:
            received = passed_along(result, "section", 1)
    pooled = jnp.stack(pooled_rows, axis=0)
    pooled = broadcast(pooled, "section", 1)
    return jnp.dot(
        lax.all_gather(pooled, "dp", axis=0, tiled=True) - center,
        whitening,
        precision=lax.Precision.HIGHEST,
        preferred_element_type=jnp.float32,
    )


def slice_of(row, index, count, size):
    value = jnp.zeros((1, size), F32)
    for part in range(count):
        value += jnp.where(index == part, row[:, part * size : (part + 1) * size], 0.0)
    return value


def three_parts(value):
    high = value.astype(BF16).astype(F32)
    rest = value - high
    middle = rest.astype(BF16).astype(F32)
    return high, middle, rest - middle


def whole_lanes(columns):
    return -(-columns // 128) * 128


def kernel(
    n,
    lengths_ref,
    frames_hbm,
    proj_hbm,
    gain_hbm,
    center_hbm,
    qkv_hbm,
    out_hbm,
    white_hbm,
    emb_ref,
    frames_ref,
    proj_ref,
    gain_ref,
    center_ref,
    wq,
    wq2,
    wo,
    wo2,
    wh,
    wh3,
    gsend,
    gsum,
    x0buf,
    xbuf,
    stat,
    normed,
    qkv,
    own,
    qsend,
    qrecv,
    sumsend,
    sumrecv,
    ctx,
    psend,
    precv,
    xnew,
    pool,
    rows,
    load_sem,
    x_send,
    x_recv,
    stat_send,
    stat_recv,
    g_send,
    g_recv,
    q_send,
    q_recv,
    sum_send,
    sum_recv,
    c_send,
    c_recv,
    p_send,
    p_recv,
    n_send,
    pool_send,
    pool_recv,
    row_send,
    row_recv,
):
    d = lax.axis_index("dp")
    s = lax.axis_index("section")
    m = lax.axis_index("mp")
    pieces, part_rows, lanes_x = xbuf.shape
    wide = wo.shape[1]
    frames_count = 2 * part_rows
    full = n * wide
    half = n // 2 * HD
    lanes_h = ctx.shape[3]
    pad_x, pad_h = lanes_x - wide, lanes_h - half
    groups = 2
    my_utt, my_half = d // 2, lax.rem(d, 2)
    pairs = (
        (frames_hbm, frames_ref),
        (proj_hbm, proj_ref.at[pl.ds(0, wide)]),
        (gain_hbm, gain_ref),
        (qkv_hbm, wq),
        (out_hbm, wo),
        (center_hbm, center_ref),
        (white_hbm, wh),
    )
    loads = [pltpu.make_async_copy(src, dst, load_sem.at[i]) for i, (src, dst) in enumerate(pairs)]
    for load in loads:
        load.start()

    barrier = pltpu.get_barrier_semaphore()
    for dz in range(n):
        for dm in range(n):
            if dz or dm:
                pl.semaphore_signal(
                    barrier, inc=1, device_id=(lax.rem(d + dz, n), s, lax.rem(m + dm, n)), device_id_type=MESH
                )
    for dm in range(n):
        pl.semaphore_signal(barrier, inc=1, device_id=(d, 1 - s, lax.rem(m + dm, n)), device_id_type=MESH)

    proj_ref[wide:] = jnp.zeros((pad_x, proj_ref.shape[1]), BF16)
    wq2[...] = jnp.zeros(wq2.shape, BF16)
    wo2[...] = jnp.zeros(wo2.shape, BF16)
    loads[0].wait()
    loads[1].wait()

    @pl.when(s == 0)
    def _():
        projected = lax.dot_general(
            frames_ref[0], proj_ref[...], (((1,), (1,)), ((), ())), preferred_element_type=F32
        ).astype(BF16)
        x0buf[0] = projected[:part_rows]
        x0buf[1] = projected[part_rows:]

    pl.semaphore_wait(barrier, n * n - 1 + n)

    def remote(src, dst, send, recv, target):
        return pltpu.make_async_remote_copy(
            src_ref=src, dst_ref=dst, send_sem=send, recv_sem=recv, device_id=target, device_id_type=MESH
        )

    def arrived(dst, recv):
        remote(dst, dst, x_send.at[0], recv, (d, s, m)).wait_recv()

    def above(k):
        return lax.rem(d + k, n), s, m

    def below(k):
        return lax.rem(d - k + n, n)

    sent = []

    def x0_copy(dm):
        return remote(
            x0buf, xbuf.at[pl.ds(2 * d, 2)], x_send.at[dm], x_recv.at[2 * d], (m, s, lax.rem(m + dm, n))
        )

    @pl.when(s == 0)
    def _():
        for dm in range(1, n):
            x0_copy(dm).start()

        @pl.when(d != m)
        def _():
            x0_copy(0).start()

        @pl.when(d == m)
        def _():
            xbuf[pl.ds(2 * d, 2)] = x0buf[...]

    loads[2].wait()
    gain = jnp.concatenate([slice_of(gain_ref, d, n, wide), jnp.zeros((1, pad_x), F32)], axis=1)
    ids = lax.broadcasted_iota(jnp.int32, (16, lanes_x), 0)
    gain_rows = jnp.zeros((16, lanes_x), F32)
    for part, value in enumerate(three_parts(gain)):
        gain_rows = jnp.where(ids == part, value, gain_rows)
    gain_rows = gain_rows.astype(BF16)
    loads[3].wait()
    for h in range(2):
        for t in range(3):
            start = (2 * t + h) * half
            wq2[h, 0:wide, t * lanes_h : t * lanes_h + half] = wq[:, start : start + half]
        products = jnp.dot(gain_rows, wq2[h], preferred_element_type=F32)
        gsend[h] = products[0:1] + products[1:2] + products[2:3]
    gsum[d] = gsend[my_half]
    for k in range(1, n):
        copy = remote(gsend.at[lax.rem(d + k, 2)], gsum.at[d], g_send.at[k], g_recv.at[d], above(k))
        copy.start()
        sent.append(copy)

    loads[4].wait()
    for h in range(2):
        wo2[h, 0:half, 0:wide] = wo[h * half : (h + 1) * half]

    def split_whitening():
        loads[6].wait()
        for part in range(n):
            for i, value in enumerate(three_parts(wh[part * wide : (part + 1) * wide])):
                wh3[i, part, 0:wide] = value.astype(BF16)
                wh3[i, part, wide:] = jnp.zeros((pad_x, wh3.shape[3]), BF16)

    @pl.when(s == 1)
    def _():
        split_whitening()

    lanes = lax.broadcasted_iota(jnp.int32, (frames_count, 128), 1)
    length_row = 4
    real = lax.broadcasted_iota(jnp.int32, (frames_count, lanes_x), 1) < wide

    def q_copy(g):
        return remote(qsend.at[g], qrecv.at[g], q_send.at[g], q_recv.at[g], (d + 1 - 2 * my_half, s, m))

    def sum_copy(g):
        return remote(sumsend.at[g], sumrecv.at[g], sum_send.at[g], sum_recv.at[g], above(2))

    def stat_copy(g, k):
        return remote(stat.at[g, d], stat.at[g, d], stat_send.at[g, k], stat_recv.at[g, d], above(k))

    def project(g):
        for i in range(2):
            u = 2 * g + i

            @pl.when(jnp.logical_and(s == 0, jnp.logical_or(d != u, m != d)))
            def _():
                arrived(xbuf.at[pl.ds(2 * u, 2)], x_recv.at[2 * u])

            @pl.when(s == 1)
            def _():
                arrived(xbuf.at[2 * u], x_recv.at[2 * u])
                arrived(xbuf.at[2 * u + 1], x_recv.at[2 * u + 1])

        table = jnp.zeros((frames_count, 128), F32)
        for i in range(2):
            u = 2 * g + i
            x = jnp.concatenate([xbuf[2 * u], xbuf[2 * u + 1]], axis=0).astype(F32)
            mean = jnp.sum(x, axis=1, keepdims=True) * (1.0 / wide)
            centered = jnp.where(real, x - mean, 0.0)
            spread = jnp.sum(centered * centered, axis=1, keepdims=True)
            table = jnp.where(lanes == 2 * i, mean, table)
            table = jnp.where(lanes == 2 * i + 1, spread, table)
            normed[g, i * frames_count : (i + 1) * frames_count] = (centered * gain).astype(BF16)
        table = jnp.where(lanes == length_row, lengths_ref[0].astype(F32), table)
        partial = jnp.dot(normed[g], wq2[1 - my_half], preferred_element_type=F32).astype(BF16)
        for i in range(2):
            qsend[g, i] = partial[i * frames_count : (i + 1) * frames_count]
        q_copy(g).start()
        stat[g, d] = table.T[0:8]
        for k in range(1, n):
            stat_copy(g, k).start()
        kept = jnp.dot(normed[g], wq2[my_half], preferred_element_type=F32)
        for i in range(2):
            own[g, i] = kept[i * frames_count : (i + 1) * frames_count]

    def exchange(g):
        arrived(qrecv.at[g], q_recv.at[g])
        other = 1 - my_utt
        sumsend[g] = (own[g, other] + qrecv[g, other].astype(F32)).astype(BF16)
        sum_copy(g).start()
        own[g, my_utt] = own[g, my_utt] + qrecv[g, my_utt].astype(F32)

    stat_ids = lax.broadcasted_iota(jnp.int32, (8, 128), 0)
    columns = lax.broadcasted_iota(jnp.int32, (frames_count, lanes_h), 1)
    keys_ids = lax.broadcasted_iota(jnp.int32, (frames_count, frames_count), 1).astype(F32)

    def attend(g):
        for k in range(1, n):
            arrived(stat.at[g, below(k)], stat_recv.at[g, below(k)])
            if g == 0:
                arrived(gsum.at[below(k)], g_recv.at[below(k)])

        def stat_row(k, row):
            return jnp.sum(jnp.where(stat_ids == row, stat[g, k], 0.0), axis=0, keepdims=True)

        slice_means = [stat_row(k, 2 * my_utt) for k in range(n)]
        mean = sum(slice_means) * (1.0 / n)
        deltas = [value - mean for value in slice_means]
        spread = sum(stat_row(k, 2 * my_utt + 1) for k in range(n)) + wide * sum(value * value for value in deltas)
        rstd = lax.rsqrt(spread * (1.0 / full) + 1e-05)
        by_row = jnp.zeros((8, 128), F32)
        for k, value in enumerate(deltas + [rstd]):
            by_row = jnp.where(stat_ids == k, value, by_row)
        by_frame = jnp.concatenate([by_row, jnp.zeros((frames_count - 8, 128), F32)], axis=0).T
        length = stat[g, 2 * g + my_utt, length_row : length_row + 1, :]
        valid = keys_ids < length
        arrived(sumrecv.at[g], sum_recv.at[g])
        summed = own[g, my_utt] + sumrecv[g].astype(F32)
        for k in range(n):
            summed = summed + by_frame[:, k : k + 1] * gsum[k]
        qkv[g] = (summed * by_frame[:, n : n + 1]).astype(BF16)
        query = qkv[g, :, 0:lanes_h]
        keys = qkv[g, :, lanes_h : 2 * lanes_h]
        values = qkv[g, :, 2 * lanes_h : 3 * lanes_h]
        context = jnp.zeros((frames_count, lanes_h), F32)
        for h in range(half // HD):
            in_head = jnp.logical_and(columns >= h * HD, columns < (h + 1) * HD)
            head_query = jnp.where(in_head, query, jnp.zeros_like(query))
            head_values = jnp.where(in_head, values, jnp.zeros_like(values))
            scores = lax.dot_general(
                head_query, keys, (((1,), (1,)), ((), ())), preferred_element_type=F32
            ) / jnp.sqrt(F32(HD))
            scores = jnp.where(valid, scores, F32(-1e30))
            weights = jnp.exp(scores - jnp.max(scores, axis=1, keepdims=True))
            probs = (weights / jnp.sum(weights, axis=1, keepdims=True)).astype(BF16)
            context += jnp.dot(probs, head_values, preferred_element_type=F32)
        ctx[g, d] = context.astype(BF16)
        for k in (2, 1, 3):
            copy = remote(ctx.at[g, d], ctx.at[g, d], c_send.at[g, k], c_recv.at[g, d], above(k))
            copy.start()
            sent.append(copy)

    def p_copy(g, to):
        return remote(psend.at[g, to], precv.at[g, m], p_send.at[g, to], p_recv.at[g, m], (d, s, to))

    def put_out(g):
        for i in range(2):
            total = jnp.zeros((frames_count, lanes_x), F32)
            for h in range(2):
                source = 2 * i + h

                @pl.when(d != source)
                def _():
                    arrived(ctx.at[g, source], c_recv.at[g, source])

                total += jnp.dot(ctx[g, source], wo2[h], preferred_element_type=F32)
            total = total.astype(BF16)
            for h in range(2):
                to = 2 * i + h
                psend[g, to] = total[h * part_rows : (h + 1) * part_rows]

                @pl.when(m != to)
                def _():
                    p_copy(g, to).start()

                @pl.when(m == to)
                def _():
                    precv[g, to] = psend[g, to]

    def next_copy(g, dm):
        return remote(
            xnew.at[g], xbuf.at[n * g + m], n_send.at[g, dm], x_recv.at[n * g + m], (d, 1, lax.rem(m + dm, n))
        )

    def pool_copy(g, ds, dm):
        return remote(
            pool.at[g, m],
            pool.at[g, m],
            pool_send.at[g, ds, dm],
            pool_recv.at[g, m],
            (d, lax.rem(s + ds, 2), lax.rem(m + dm, n)),
        )

    hops = [(ds, dm) for ds in range(2) for dm in range(n) if ds or dm]

    def finish(g):
        for k in range(1, n):
            source = lax.rem(m - k + n, n)
            arrived(precv.at[g, source], p_recv.at[g, source])
        attended = precv[g, 0].astype(F32)
        for k in range(1, n):
            attended = attended + precv[g, k].astype(F32)
        xnew[g] = (xbuf[n * g + m].astype(F32) + attended).astype(BF16)

        @pl.when(s == 0)
        def _():
            for dm in range(n):
                next_copy(g, dm).start()

        @pl.when(s == 1)
        def _():
            length = stat[g, 2 * g + m // 2, length_row : length_row + 1, :]
            frame = lax.broadcasted_iota(jnp.int32, (8, part_rows), 1) + part_rows * lax.rem(m, 2)
            weights = jnp.where(frame.astype(F32) < length[:, :part_rows], 1.0, 0.0).astype(BF16)
            pool[g, m] = jnp.dot(weights, xnew[g], preferred_element_type=F32)
            for ds, dm in hops:
                pool_copy(g, ds, dm).start()

    project(0)

    @pl.when(s == 0)
    def _():
        project(1)

    exchange(0)
    attend(0)

    @pl.when(s == 0)
    def _():
        exchange(1)

    @pl.when(s == 1)
    def _():
        project(1)

    put_out(0)

    @pl.when(s == 1)
    def _():
        exchange(1)

    finish(0)
    attend(1)
    put_out(1)
    finish(1)

    @pl.when(s == 0)
    def _():
        split_whitening()

    loads[5].wait()
    row_ids = lax.broadcasted_iota(jnp.int32, (8, lanes_x), 0)
    gathered = jnp.zeros((8, lanes_x), F32)
    for u in range(n):
        g, i = u // 2, u % 2
        for source in (2 * i, 2 * i + 1):
            @pl.when(jnp.logical_or(s == 0, m != source))
            def _():
                arrived(pool.at[g, source], pool_recv.at[g, source])

        total = pool[g, 2 * i] + pool[g, 2 * i + 1]
        length = stat[g, u, length_row : length_row + 1, 0:1]
        gathered = jnp.where(row_ids == u, total / length, gathered)
    center = slice_of(center_ref[...].reshape(1, full), d, n, wide)
    rows[d] = gathered - jnp.concatenate([center, jnp.zeros((1, pad_x), F32)], axis=1)
    for k in range(1, n):
        copy = remote(rows.at[d], rows.at[d], row_send.at[k], row_recv.at[d], above(k))
        copy.start()
        sent.append(copy)
    for k in range(1, n):
        arrived(rows.at[below(k)], row_recv.at[below(k)])
    result = jnp.zeros((32, emb_ref.shape[1]), F32)
    for part in range(n):
        parts = jnp.concatenate(list(three_parts(rows[part])) + [jnp.zeros((8, lanes_x), F32)], axis=0).astype(BF16)
        for i in range(3):
            result += jnp.dot(
                parts, wh3[i, part], preferred_element_type=F32
            )
    result = result[0:8] + result[8:16] + result[16:24]
    emb_ref[...] = result[0:n]

    for copy in sent:
        copy.wait_send()
    for g in range(groups):
        for k in range(1, n):
            stat_copy(g, k).wait_send()
        q_copy(g).wait_send()
        sum_copy(g).wait_send()
        for to in range(n):
            @pl.when(m != to)
            def _():
                p_copy(g, to).wait_send()

    @pl.when(s == 0)
    def _():
        for dm in range(1, n):
            x0_copy(dm).wait_send()

        @pl.when(d != m)
        def _():
            x0_copy(0).wait_send()

        for g in range(groups):
            for dm in range(n):
                next_copy(g, dm).wait_send()

    @pl.when(s == 1)
    def _():
        for g in range(groups):
            for ds, dm in hops:
                pool_copy(g, ds, dm).wait_send()


def fused(n, frames, lengths, feature_proj, norm_gain, qkv_weight, out_weight, center, whitening):
    frames_count = frames.shape[1]
    wide = feature_proj.shape[1]
    qkv_cols = qkv_weight.shape[2]
    head_rows = out_weight.shape[1]
    out_cols = whitening.shape[1]
    rows, lanes_x, lanes_h = frames_count // 2, whole_lanes(wide), whole_lanes(head_rows // 2)
    columns = 3 * lanes_h
    vmem = pl.BlockSpec(memory_space=pltpu.VMEM)
    anywhere = pl.BlockSpec(memory_space=pl.ANY)
    dma = pltpu.SemaphoreType.DMA
    return pl.pallas_call(
        functools.partial(kernel, n),
        out_shape=jax.ShapeDtypeStruct((n, out_cols), F32),
        in_specs=[pl.BlockSpec(memory_space=pltpu.SMEM)] + [anywhere] * 7,
        out_specs=vmem,
        scratch_shapes=[
            pltpu.VMEM(frames.shape, BF16),
            pltpu.VMEM((lanes_x, feature_proj.shape[0]), BF16),
            pltpu.VMEM(norm_gain.shape, F32),
            pltpu.VMEM(center.shape, F32),
            pltpu.VMEM((wide, qkv_cols), BF16),
            pltpu.VMEM((2, lanes_x, columns), BF16),
            pltpu.VMEM((head_rows, wide), BF16),
            pltpu.VMEM((2, lanes_h, lanes_x), BF16),
            pltpu.VMEM((n * wide, out_cols), F32),
            pltpu.VMEM((3, n, lanes_x, out_cols), BF16),
            pltpu.VMEM((2, 1, columns), F32),
            pltpu.VMEM((n, 1, columns), F32),
            pltpu.VMEM((2, rows, lanes_x), BF16),
            pltpu.VMEM((2 * n, rows, lanes_x), BF16),
            pltpu.VMEM((2, n, 8, 128), F32),
            pltpu.VMEM((2, 2 * frames_count, lanes_x), BF16),
            pltpu.VMEM((2, frames_count, columns), BF16),
            pltpu.VMEM((2, 2, frames_count, columns), F32),
            pltpu.VMEM((2, 2, frames_count, columns), BF16),
            pltpu.VMEM((2, 2, frames_count, columns), BF16),
            pltpu.VMEM((2, frames_count, columns), BF16),
            pltpu.VMEM((2, frames_count, columns), BF16),
            pltpu.VMEM((2, n, frames_count, lanes_h), BF16),
            pltpu.VMEM((2, n, rows, lanes_x), BF16),
            pltpu.VMEM((2, n, rows, lanes_x), BF16),
            pltpu.VMEM((2, rows, lanes_x), BF16),
            pltpu.VMEM((2, n, 8, lanes_x), F32),
            pltpu.VMEM((n, 8, lanes_x), F32),
            dma((7,)),
            dma((n,)), dma((2 * n,)),
            dma((2, n)), dma((2, n)),
            dma((n,)), dma((n,)),
            dma((2,)), dma((2,)),
            dma((2,)), dma((2,)),
            dma((2, n)), dma((2, n)),
            dma((2, n)), dma((2, n)),
            dma((2, n)),
            dma((2, 2, n)), dma((2, n)),
            dma((n,)), dma((n,)),
        ],
        compiler_params=pltpu.CompilerParams(
            collective_id=0, has_side_effects=True, vmem_limit_bytes=60 * 1024 * 1024
        ),
    )(
        lengths,
        frames,
        feature_proj.T,
        norm_gain,
        center,
        qkv_weight.reshape(qkv_weight.shape[1:]),
        out_weight.reshape(out_weight.shape[1:]),
        whitening,
    )


def solution(mesh):
    in_specs = (
        P("dp", None, None),
        P("dp"),
        P(None, "mp"),
        P("section", None),
        P("section", "dp", "mp"),
        P("section", "mp", "dp"),
        P(),
        P(None, "dp"),
    )
    out_specs = P(None, "dp")

    def step(frames, lengths, feature_proj, norm_gain, qkv_weight, out_weight, center, whitening):
        n = mesh.shape["mp"]
        square = mesh.shape["dp"] == n and mesh.shape["section"] == 2
        square = square and n == 4 and frames.shape[0] == 1 and frames.shape[1] == 128
        square = square and qkv_weight.shape[2] == 3 * n * HD and qkv_weight.shape[1] == feature_proj.shape[1]
        if square:
            return fused(
                n, frames, lengths, feature_proj, norm_gain, qkv_weight, out_weight, center, whitening
            )
        return body(frames, lengths, feature_proj, norm_gain, qkv_weight, out_weight, center, whitening)

    return jax.shard_map(step, mesh=mesh, in_specs=in_specs, out_specs=out_specs, check_vma=False)
```

```python
import functools

import jax
import jax.numpy as jnp
from jax import lax
from jax.experimental import pallas as pl
from jax.experimental.pallas import tpu as pltpu
from jax.sharding import PartitionSpec as P

MESH = pl.DeviceIdType.MESH
BF16 = jnp.bfloat16
F32 = jnp.float32

HD = 120


def passed_along(x, axis, by):
    count = lax.axis_size(axis)
    pairs = [(i, i + by) for i in range(count) if 0 <= i + by < count]
    return lax.ppermute(x, axis, pairs)


def broadcast(value, axis, source):
    kept = jnp.where(lax.axis_index(axis) == source, value, 0).astype(value.dtype)
    return lax.psum(kept, axis)


def layer_norm(values, gain):
    mean = jnp.mean(values, axis=-1, keepdims=True)
    centered = values - mean
    var = jnp.mean(centered * centered, axis=-1, keepdims=True)
    return centered * lax.rsqrt(var + 1e-05) * gain


def body(frames, lengths, feature_proj, norm_gain, qkv_weight, out_weight, center, whitening):
    section_index = lax.axis_index("section")
    gain = norm_gain[0]
    qkv_local = qkv_weight[0]
    out_local = out_weight[0]
    count_utt = frames.shape[0]
    frames_count = frames.shape[1]
    width = gain.shape[0]
    qkv_cols = qkv_local.shape[1]
    heads_local = qkv_cols // (3 * HD)
    full_qkv, full_out = (
        lax.all_gather(qkv_local, "dp", axis=0, tiled=True),
        lax.all_gather(out_local, "dp", axis=1, tiled=True),
    )
    received = jnp.zeros((frames_count, width), jnp.bfloat16)
    pooled_rows = []
    frame_ids = jnp.arange(frames_count, dtype=jnp.int32)
    for step in range(count_utt + 1):
        first_mb = min(step, count_utt - 1)
        second_mb = max(step - 1, 0)
        projected_part = jnp.dot(
            frames[first_mb], feature_proj, preferred_element_type=jnp.float32
        ).astype(jnp.bfloat16)
        projected = lax.all_gather(projected_part, "mp", axis=1, tiled=True)
        first_section = section_index == 0
        layer_input = jnp.where(first_section, projected, received)
        length = jnp.where(first_section, lengths[first_mb], lengths[second_mb])
        normed = layer_norm(layer_input.astype(jnp.float32), gain).astype(jnp.bfloat16)
        qkv_sum = jnp.dot(normed, full_qkv, preferred_element_type=jnp.float32)
        qkv = qkv_sum.astype(jnp.bfloat16).reshape(frames_count, 3, heads_local, HD)
        query = qkv[:, 0]
        keys = qkv[:, 1]
        values = qkv[:, 2]
        scores = jnp.einsum(
            "qhd,khd->hqk", query, keys, preferred_element_type=jnp.float32
        ) / jnp.sqrt(jnp.float32(HD))
        attention_valid = jnp.arange(frames_count, dtype=jnp.int32) < length
        scores = jnp.where(attention_valid[None, None, :], scores, jnp.float32(-1e30))
        probs = jax.nn.softmax(scores, axis=-1).astype(jnp.bfloat16)
        context = jnp.einsum(
            "hqk,khd->qhd", probs, values, preferred_element_type=jnp.float32
        ).astype(jnp.bfloat16)
        context = context.reshape(frames_count, heads_local * HD)
        partial_out = jnp.dot(context, full_out, preferred_element_type=jnp.float32)
        attended = lax.psum(partial_out.astype(jnp.bfloat16), "mp").astype(jnp.float32)
        result = (layer_input.astype(jnp.float32) + attended).astype(jnp.bfloat16)
        if step >= 1:
            valid = frame_ids < lengths[step - 1]
            summed = jnp.sum(
                jnp.where(valid[:, None], result.astype(jnp.float32), jnp.float32(0.0)), axis=0
            )
            pooled_rows.append(summed / lengths[step - 1].astype(jnp.float32))
        if step < count_utt:
            received = passed_along(result, "section", 1)
    pooled = jnp.stack(pooled_rows, axis=0)
    pooled = broadcast(pooled, "section", 1)
    return jnp.dot(
        lax.all_gather(pooled, "dp", axis=0, tiled=True) - center,
        whitening,
        precision=lax.Precision.HIGHEST,
        preferred_element_type=jnp.float32,
    )


def slice_of(row, index, count, size):
    value = jnp.zeros((1, size), F32)
    for part in range(count):
        value += jnp.where(index == part, row[:, part * size : (part + 1) * size], 0.0)
    return value


def three_parts(value):
    high = value.astype(BF16).astype(F32)
    rest = value - high
    middle = rest.astype(BF16).astype(F32)
    return high, middle, rest - middle


def whole_lanes(columns):
    return -(-columns // 128) * 128


def kernel(
    n,
    lengths_ref,
    frames_hbm,
    proj_hbm,
    gain_hbm,
    center_hbm,
    qkv_hbm,
    out_hbm,
    white_hbm,
    emb_ref,
    frames_ref,
    proj_ref,
    gain_ref,
    center_ref,
    wq,
    wq2,
    wo,
    wo2,
    wh,
    wh3,
    gsend,
    gsum,
    x0buf,
    xbuf,
    stat,
    normed,
    qkv,
    own,
    qsend,
    qrecv,
    sumsend,
    sumrecv,
    ctx,
    psend,
    precv,
    xnew,
    pool,
    rows,
    load_sem,
    x_send,
    x_recv,
    stat_send,
    stat_recv,
    g_send,
    g_recv,
    q_send,
    q_recv,
    sum_send,
    sum_recv,
    c_send,
    c_recv,
    p_send,
    p_recv,
    n_send,
    pool_send,
    pool_recv,
    row_send,
    row_recv,
):
    d = lax.axis_index("dp")
    s = lax.axis_index("section")
    m = lax.axis_index("mp")
    pieces, part_rows, lanes_x = xbuf.shape
    wide = wo.shape[1]
    frames_count = 2 * part_rows
    full = n * wide
    half = n // 2 * HD
    lanes_h = ctx.shape[3]
    pad_x, pad_h = lanes_x - wide, lanes_h - half
    groups = 2
    my_utt, my_half = d // 2, lax.rem(d, 2)
    pairs = (
        (frames_hbm, frames_ref),
        (proj_hbm, proj_ref.at[pl.ds(0, wide)]),
        (gain_hbm, gain_ref),
        (qkv_hbm, wq),
        (out_hbm, wo),
        (center_hbm, center_ref),
        (white_hbm, wh),
    )
    loads = [pltpu.make_async_copy(src, dst, load_sem.at[i]) for i, (src, dst) in enumerate(pairs)]
    for load in loads:
        load.start()

    barrier = pltpu.get_barrier_semaphore()
    for dz in range(n):
        for dm in range(n):
            if dz or dm:
                pl.semaphore_signal(
                    barrier, inc=1, device_id=(lax.rem(d + dz, n), s, lax.rem(m + dm, n)), device_id_type=MESH
                )
    for dm in range(n):
        pl.semaphore_signal(barrier, inc=1, device_id=(d, 1 - s, lax.rem(m + dm, n)), device_id_type=MESH)

    proj_ref[wide:] = jnp.zeros((pad_x, proj_ref.shape[1]), BF16)
    wq2[...] = jnp.zeros(wq2.shape, BF16)
    wo2[...] = jnp.zeros(wo2.shape, BF16)
    loads[0].wait()
    loads[1].wait()

    @pl.when(s == 0)
    def _():
        projected = lax.dot_general(
            frames_ref[0], proj_ref[...], (((1,), (1,)), ((), ())), preferred_element_type=F32
        ).astype(BF16)
        x0buf[0] = projected[:part_rows]
        x0buf[1] = projected[part_rows:]

    pl.semaphore_wait(barrier, n * n - 1 + n)

    def remote(src, dst, send, recv, target):
        return pltpu.make_async_remote_copy(
            src_ref=src, dst_ref=dst, send_sem=send, recv_sem=recv, device_id=target, device_id_type=MESH
        )

    def arrived(dst, recv):
        remote(dst, dst, x_send.at[0], recv, (d, s, m)).wait_recv()

    def above(k):
        return lax.rem(d + k, n), s, m

    def below(k):
        return lax.rem(d - k + n, n)

    sent = []

    def x0_copy(dm):
        return remote(
            x0buf, xbuf.at[pl.ds(2 * d, 2)], x_send.at[dm], x_recv.at[2 * d], (m, s, lax.rem(m + dm, n))
        )

    @pl.when(s == 0)
    def _():
        for dm in range(1, n):
            x0_copy(dm).start()

        @pl.when(d != m)
        def _():
            x0_copy(0).start()

        @pl.when(d == m)
        def _():
            xbuf[pl.ds(2 * d, 2)] = x0buf[...]

    loads[2].wait()
    gain = jnp.concatenate([slice_of(gain_ref, d, n, wide), jnp.zeros((1, pad_x), F32)], axis=1)
    ids = lax.broadcasted_iota(jnp.int32, (16, lanes_x), 0)
    gain_rows = jnp.zeros((16, lanes_x), F32)
    for part, value in enumerate(three_parts(gain)):
        gain_rows = jnp.where(ids == part, value, gain_rows)
    gain_rows = gain_rows.astype(BF16)
    loads[3].wait()

    @pl.loop(0, wide // 32)
    def _(step):
        run = pl.ds(pl.multiple_of(step * 32, 32), 32)
        for h in range(2):
            for t in range(3):
                start = (2 * t + h) * half
                wq2[h, run, t * lanes_h : t * lanes_h + half] = wq[run, start : start + half]

    @pl.loop(0, 2)
    def _(h):
        products = jnp.dot(gain_rows, wq2[h], preferred_element_type=F32)
        gsend[h] = products[0:1] + products[1:2] + products[2:3]
    gsum[d] = gsend[my_half]
    for k in range(1, n):
        copy = remote(gsend.at[lax.rem(d + k, 2)], gsum.at[d], g_send.at[k], g_recv.at[d], above(k))
        copy.start()
        sent.append(copy)

    loads[4].wait()
    for h in range(2):
        wo2[h, 0:half, 0:wide] = wo[h * half : (h + 1) * half]

    def split_whitening():
        loads[6].wait()
        for part in range(n):
            for i in range(3):
                wh3[i, part, wide:] = jnp.zeros((pad_x, wh3.shape[3]), BF16)

            @pl.loop(0, wide // 32)
            def _(step):
                source = pl.ds(pl.multiple_of(part * wide + step * 32, 32), 32)
                target = pl.ds(pl.multiple_of(step * 32, 32), 32)
                for i, value in enumerate(three_parts(wh[source])):
                    wh3[i, part, target] = value.astype(BF16)

    @pl.when(s == 1)
    def _():
        split_whitening()

    lanes = lax.broadcasted_iota(jnp.int32, (frames_count, 128), 1)
    length_row = 4
    real = lax.broadcasted_iota(jnp.int32, (frames_count, lanes_x), 1) < wide

    def q_copy(g):
        return remote(qsend.at[g], qrecv.at[g], q_send.at[g], q_recv.at[g], (d + 1 - 2 * my_half, s, m))

    def sum_copy(g):
        return remote(sumsend.at[g], sumrecv.at[g], sum_send.at[g], sum_recv.at[g], above(2))

    def stat_copy(g, k):
        return remote(stat.at[g, d], stat.at[g, d], stat_send.at[g, k], stat_recv.at[g, d], above(k))

    def project(g):
        for i in range(2):
            u = 2 * g + i

            @pl.when(jnp.logical_and(s == 0, jnp.logical_or(d != u, m != d)))
            def _():
                arrived(xbuf.at[pl.ds(2 * u, 2)], x_recv.at[2 * u])

            @pl.when(s == 1)
            def _():
                arrived(xbuf.at[2 * u], x_recv.at[2 * u])
                arrived(xbuf.at[2 * u + 1], x_recv.at[2 * u + 1])

        table = jnp.zeros((frames_count, 128), F32)
        for i in range(2):
            u = 2 * g + i
            x = jnp.concatenate([xbuf[2 * u], xbuf[2 * u + 1]], axis=0).astype(F32)
            mean = jnp.sum(x, axis=1, keepdims=True) * (1.0 / wide)
            centered = jnp.where(real, x - mean, 0.0)
            spread = jnp.sum(centered * centered, axis=1, keepdims=True)
            table = jnp.where(lanes == 2 * i, mean, table)
            table = jnp.where(lanes == 2 * i + 1, spread, table)
            normed[g, i * frames_count : (i + 1) * frames_count] = (centered * gain).astype(BF16)
        table = jnp.where(lanes == length_row, lengths_ref[0].astype(F32), table)
        partial = jnp.dot(normed[g], wq2[1 - my_half], preferred_element_type=F32).astype(BF16)
        for i in range(2):
            qsend[g, i] = partial[i * frames_count : (i + 1) * frames_count]
        q_copy(g).start()
        stat[g, d] = table.T[0:8]
        for k in range(1, n):
            stat_copy(g, k).start()
        kept = jnp.dot(normed[g], wq2[my_half], preferred_element_type=F32)
        for i in range(2):
            own[g, i] = kept[i * frames_count : (i + 1) * frames_count]

    def exchange(g):
        arrived(qrecv.at[g], q_recv.at[g])
        other = 1 - my_utt
        sumsend[g] = (own[g, other] + qrecv[g, other].astype(F32)).astype(BF16)
        sum_copy(g).start()
        own[g, my_utt] = own[g, my_utt] + qrecv[g, my_utt].astype(F32)

    stat_ids = lax.broadcasted_iota(jnp.int32, (8, 128), 0)
    columns = lax.broadcasted_iota(jnp.int32, (frames_count, lanes_h), 1)
    keys_ids = lax.broadcasted_iota(jnp.int32, (frames_count, frames_count), 1).astype(F32)

    def ctx_copy(g, k):
        return remote(ctx.at[g, d], ctx.at[g, d], c_send.at[g, k], c_recv.at[g, d], above(k))

    def attend(g):
        for k in range(1, n):
            arrived(stat.at[g, below(k)], stat_recv.at[g, below(k)])

        def stat_row(k, row):
            return jnp.sum(jnp.where(stat_ids == row, stat[g, k], 0.0), axis=0, keepdims=True)

        slice_means = [stat_row(k, 2 * my_utt) for k in range(n)]
        mean = sum(slice_means) * (1.0 / n)
        deltas = [value - mean for value in slice_means]
        spread = sum(stat_row(k, 2 * my_utt + 1) for k in range(n)) + wide * sum(value * value for value in deltas)
        rstd = lax.rsqrt(spread * (1.0 / full) + 1e-05)
        by_row = jnp.zeros((8, 128), F32)
        for k, value in enumerate(deltas + [rstd]):
            by_row = jnp.where(stat_ids == k, value, by_row)
        by_frame = jnp.concatenate([by_row, jnp.zeros((frames_count - 8, 128), F32)], axis=0).T
        length = stat[g, 2 * g + my_utt, length_row : length_row + 1, :]
        valid = keys_ids < length
        arrived(sumrecv.at[g], sum_recv.at[g])
        summed = own[g, my_utt] + sumrecv[g].astype(F32)
        for k in range(n):
            summed = summed + by_frame[:, k : k + 1] * gsum[k]
        qkv[g] = (summed * by_frame[:, n : n + 1]).astype(BF16)
        query = qkv[g, :, 0:lanes_h]
        keys = qkv[g, :, lanes_h : 2 * lanes_h]
        values = qkv[g, :, 2 * lanes_h : 3 * lanes_h]
        context = jnp.zeros((frames_count, lanes_h), F32)
        for h in range(half // HD):
            in_head = jnp.logical_and(columns >= h * HD, columns < (h + 1) * HD)
            head_query = jnp.where(in_head, query, jnp.zeros_like(query))
            head_values = jnp.where(in_head, values, jnp.zeros_like(values))
            scores = lax.dot_general(
                head_query, keys, (((1,), (1,)), ((), ())), preferred_element_type=F32
            ) / jnp.sqrt(F32(HD))
            scores = jnp.where(valid, scores, F32(-1e30))
            weights = jnp.exp(scores - jnp.max(scores, axis=1, keepdims=True))
            probs = (weights / jnp.sum(weights, axis=1, keepdims=True)).astype(BF16)
            context += jnp.dot(probs, head_values, preferred_element_type=F32)
        ctx[g, d] = context.astype(BF16)
        for k in (2, 1, 3):
            ctx_copy(g, k).start()

    def p_copy(g, to):
        return remote(psend.at[g, to], precv.at[g, m], p_send.at[g, to], p_recv.at[g, m], (d, s, to))

    def put_out(g):
        for i in range(2):
            total = jnp.zeros((frames_count, lanes_x), F32)
            for h in range(2):
                source = 2 * i + h

                @pl.when(d != source)
                def _():
                    arrived(ctx.at[g, source], c_recv.at[g, source])

                total += jnp.dot(ctx[g, source], wo2[h], preferred_element_type=F32)
            total = total.astype(BF16)
            for h in range(2):
                to = 2 * i + h
                psend[g, to] = total[h * part_rows : (h + 1) * part_rows]

                @pl.when(m != to)
                def _():
                    p_copy(g, to).start()

                @pl.when(m == to)
                def _():
                    precv[g, to] = psend[g, to]

    def next_copy(g, dm):
        return remote(
            xnew.at[g], xbuf.at[n * g + m], n_send.at[g, dm], x_recv.at[n * g + m], (d, 1, lax.rem(m + dm, n))
        )

    def pool_copy(g, ds, dm):
        return remote(
            pool.at[g, m],
            pool.at[g, m],
            pool_send.at[g, ds, dm],
            pool_recv.at[g, m],
            (d, lax.rem(s + ds, 2), lax.rem(m + dm, n)),
        )

    hops = [(ds, dm) for ds in range(2) for dm in range(n) if ds or dm]

    def finish(g):
        for k in range(1, n):
            source = lax.rem(m - k + n, n)
            arrived(precv.at[g, source], p_recv.at[g, source])
        attended = precv[g, 0].astype(F32)
        for k in range(1, n):
            attended = attended + precv[g, k].astype(F32)
        xnew[g] = (xbuf[n * g + m].astype(F32) + attended).astype(BF16)

        @pl.when(s == 0)
        def _():
            for dm in range(n):
                next_copy(g, dm).start()

        @pl.when(s == 1)
        def _():
            length = stat[g, 2 * g + m // 2, length_row : length_row + 1, :]
            frame = lax.broadcasted_iota(jnp.int32, (8, part_rows), 1) + part_rows * lax.rem(m, 2)
            weights = jnp.where(frame.astype(F32) < length[:, :part_rows], 1.0, 0.0).astype(BF16)
            pool[g, m] = jnp.dot(weights, xnew[g], preferred_element_type=F32)
            for ds, dm in hops:
                pool_copy(g, ds, dm).start()

    @pl.loop(0, groups + 1)
    def _(step):
        @pl.when(step > 0)
        def _():
            exchange(step - 1)
            attend(step - 1)

        @pl.when(step < groups)
        def _():
            project(step)

        @pl.when(step == 0)
        def _():
            for k in range(1, n):
                arrived(gsum.at[below(k)], g_recv.at[below(k)])

        @pl.when(step > 0)
        def _():
            put_out(step - 1)
            finish(step - 1)

    @pl.when(s == 0)
    def _():
        split_whitening()

    loads[5].wait()
    row_ids = lax.broadcasted_iota(jnp.int32, (8, lanes_x), 0)
    gathered = jnp.zeros((8, lanes_x), F32)
    for u in range(n):
        g, i = u // 2, u % 2
        for source in (2 * i, 2 * i + 1):
            @pl.when(jnp.logical_or(s == 0, m != source))
            def _():
                arrived(pool.at[g, source], pool_recv.at[g, source])

        total = pool[g, 2 * i] + pool[g, 2 * i + 1]
        length = stat[g, u, length_row : length_row + 1, 0:1]
        gathered = jnp.where(row_ids == u, total / length, gathered)
    center = slice_of(center_ref[...].reshape(1, full), d, n, wide)
    rows[d] = gathered - jnp.concatenate([center, jnp.zeros((1, pad_x), F32)], axis=1)
    for k in range(1, n):
        copy = remote(rows.at[d], rows.at[d], row_send.at[k], row_recv.at[d], above(k))
        copy.start()
        sent.append(copy)
    for k in range(1, n):
        arrived(rows.at[below(k)], row_recv.at[below(k)])
    result = jnp.zeros((32, emb_ref.shape[1]), F32)
    for part in range(n):
        parts = jnp.concatenate(list(three_parts(rows[part])) + [jnp.zeros((8, lanes_x), F32)], axis=0).astype(BF16)
        for i in range(3):
            result += jnp.dot(
                parts, wh3[i, part], preferred_element_type=F32
            )
    result = result[0:8] + result[8:16] + result[16:24]
    emb_ref[...] = result[0:n]

    for copy in sent:
        copy.wait_send()
    for g in range(groups):
        for k in range(1, n):
            stat_copy(g, k).wait_send()
            ctx_copy(g, k).wait_send()
        q_copy(g).wait_send()
        sum_copy(g).wait_send()
        for to in range(n):
            @pl.when(m != to)
            def _():
                p_copy(g, to).wait_send()

    @pl.when(s == 0)
    def _():
        for dm in range(1, n):
            x0_copy(dm).wait_send()

        @pl.when(d != m)
        def _():
            x0_copy(0).wait_send()

        for g in range(groups):
            for dm in range(n):
                next_copy(g, dm).wait_send()

    @pl.when(s == 1)
    def _():
        for g in range(groups):
            for ds, dm in hops:
                pool_copy(g, ds, dm).wait_send()


def fused(n, frames, lengths, feature_proj, norm_gain, qkv_weight, out_weight, center, whitening):
    frames_count = frames.shape[1]
    wide = feature_proj.shape[1]
    qkv_cols = qkv_weight.shape[2]
    head_rows = out_weight.shape[1]
    out_cols = whitening.shape[1]
    rows, lanes_x, lanes_h = frames_count // 2, whole_lanes(wide), whole_lanes(head_rows // 2)
    columns = 3 * lanes_h
    vmem = pl.BlockSpec(memory_space=pltpu.VMEM)
    anywhere = pl.BlockSpec(memory_space=pl.ANY)
    dma = pltpu.SemaphoreType.DMA
    return pl.pallas_call(
        functools.partial(kernel, n),
        out_shape=jax.ShapeDtypeStruct((n, out_cols), F32),
        in_specs=[pl.BlockSpec(memory_space=pltpu.SMEM)] + [anywhere] * 7,
        out_specs=vmem,
        scratch_shapes=[
            pltpu.VMEM(frames.shape, BF16),
            pltpu.VMEM((lanes_x, feature_proj.shape[0]), BF16),
            pltpu.VMEM(norm_gain.shape, F32),
            pltpu.VMEM(center.shape, F32),
            pltpu.VMEM((wide, qkv_cols), BF16),
            pltpu.VMEM((2, lanes_x, columns), BF16),
            pltpu.VMEM((head_rows, wide), BF16),
            pltpu.VMEM((2, lanes_h, lanes_x), BF16),
            pltpu.VMEM((n * wide, out_cols), F32),
            pltpu.VMEM((3, n, lanes_x, out_cols), BF16),
            pltpu.VMEM((2, 1, columns), F32),
            pltpu.VMEM((n, 1, columns), F32),
            pltpu.VMEM((2, rows, lanes_x), BF16),
            pltpu.VMEM((2 * n, rows, lanes_x), BF16),
            pltpu.VMEM((2, n, 8, 128), F32),
            pltpu.VMEM((2, 2 * frames_count, lanes_x), BF16),
            pltpu.VMEM((2, frames_count, columns), BF16),
            pltpu.VMEM((2, 2, frames_count, columns), F32),
            pltpu.VMEM((2, 2, frames_count, columns), BF16),
            pltpu.VMEM((2, 2, frames_count, columns), BF16),
            pltpu.VMEM((2, frames_count, columns), BF16),
            pltpu.VMEM((2, frames_count, columns), BF16),
            pltpu.VMEM((2, n, frames_count, lanes_h), BF16),
            pltpu.VMEM((2, n, rows, lanes_x), BF16),
            pltpu.VMEM((2, n, rows, lanes_x), BF16),
            pltpu.VMEM((2, rows, lanes_x), BF16),
            pltpu.VMEM((2, n, 8, lanes_x), F32),
            pltpu.VMEM((n, 8, lanes_x), F32),
            dma((7,)),
            dma((n,)), dma((2 * n,)),
            dma((2, n)), dma((2, n)),
            dma((n,)), dma((n,)),
            dma((2,)), dma((2,)),
            dma((2,)), dma((2,)),
            dma((2, n)), dma((2, n)),
            dma((2, n)), dma((2, n)),
            dma((2, n)),
            dma((2, 2, n)), dma((2, n)),
            dma((n,)), dma((n,)),
        ],
        compiler_params=pltpu.CompilerParams(
            collective_id=0, has_side_effects=True, vmem_limit_bytes=60 * 1024 * 1024
        ),
    )(
        lengths,
        frames,
        feature_proj.T,
        norm_gain,
        center,
        qkv_weight.reshape(qkv_weight.shape[1:]),
        out_weight.reshape(out_weight.shape[1:]),
        whitening,
    )


def solution(mesh):
    in_specs = (
        P("dp", None, None),
        P("dp"),
        P(None, "mp"),
        P("section", None),
        P("section", "dp", "mp"),
        P("section", "mp", "dp"),
        P(),
        P(None, "dp"),
    )
    out_specs = P(None, "dp")

    def step(frames, lengths, feature_proj, norm_gain, qkv_weight, out_weight, center, whitening):
        n = mesh.shape["mp"]
        square = mesh.shape["dp"] == n and mesh.shape["section"] == 2
        square = square and n == 4 and frames.shape[0] == 1 and frames.shape[1] == 128
        square = square and qkv_weight.shape[2] == 3 * n * HD and qkv_weight.shape[1] == feature_proj.shape[1]
        if square:
            return fused(
                n, frames, lengths, feature_proj, norm_gain, qkv_weight, out_weight, center, whitening
            )
        return body(frames, lengths, feature_proj, norm_gain, qkv_weight, out_weight, center, whitening)

    return jax.shard_map(step, mesh=mesh, in_specs=in_specs, out_specs=out_specs, check_vma=False)
```

```python
import functools

import jax
import jax.numpy as jnp
from jax import lax
from jax.experimental import pallas as pl
from jax.experimental.pallas import tpu as pltpu
from jax.sharding import PartitionSpec as P

MESH = pl.DeviceIdType.MESH
BF16 = jnp.bfloat16
F32 = jnp.float32

HD = 120


def passed_along(x, axis, by):
    count = lax.axis_size(axis)
    pairs = [(i, i + by) for i in range(count) if 0 <= i + by < count]
    return lax.ppermute(x, axis, pairs)


def broadcast(value, axis, source):
    kept = jnp.where(lax.axis_index(axis) == source, value, 0).astype(value.dtype)
    return lax.psum(kept, axis)


def layer_norm(values, gain):
    mean = jnp.mean(values, axis=-1, keepdims=True)
    centered = values - mean
    var = jnp.mean(centered * centered, axis=-1, keepdims=True)
    return centered * lax.rsqrt(var + 1e-05) * gain


def body(frames, lengths, feature_proj, norm_gain, qkv_weight, out_weight, center, whitening):
    section_index = lax.axis_index("section")
    gain = norm_gain[0]
    qkv_local = qkv_weight[0]
    out_local = out_weight[0]
    count_utt = frames.shape[0]
    frames_count = frames.shape[1]
    width = gain.shape[0]
    qkv_cols = qkv_local.shape[1]
    heads_local = qkv_cols // (3 * HD)
    full_qkv, full_out = (
        lax.all_gather(qkv_local, "dp", axis=0, tiled=True),
        lax.all_gather(out_local, "dp", axis=1, tiled=True),
    )
    received = jnp.zeros((frames_count, width), jnp.bfloat16)
    pooled_rows = []
    frame_ids = jnp.arange(frames_count, dtype=jnp.int32)
    for step in range(count_utt + 1):
        first_mb = min(step, count_utt - 1)
        second_mb = max(step - 1, 0)
        projected_part = jnp.dot(
            frames[first_mb], feature_proj, preferred_element_type=jnp.float32
        ).astype(jnp.bfloat16)
        projected = lax.all_gather(projected_part, "mp", axis=1, tiled=True)
        first_section = section_index == 0
        layer_input = jnp.where(first_section, projected, received)
        length = jnp.where(first_section, lengths[first_mb], lengths[second_mb])
        normed = layer_norm(layer_input.astype(jnp.float32), gain).astype(jnp.bfloat16)
        qkv_sum = jnp.dot(normed, full_qkv, preferred_element_type=jnp.float32)
        qkv = qkv_sum.astype(jnp.bfloat16).reshape(frames_count, 3, heads_local, HD)
        query = qkv[:, 0]
        keys = qkv[:, 1]
        values = qkv[:, 2]
        scores = jnp.einsum(
            "qhd,khd->hqk", query, keys, preferred_element_type=jnp.float32
        ) / jnp.sqrt(jnp.float32(HD))
        attention_valid = jnp.arange(frames_count, dtype=jnp.int32) < length
        scores = jnp.where(attention_valid[None, None, :], scores, jnp.float32(-1e30))
        probs = jax.nn.softmax(scores, axis=-1).astype(jnp.bfloat16)
        context = jnp.einsum(
            "hqk,khd->qhd", probs, values, preferred_element_type=jnp.float32
        ).astype(jnp.bfloat16)
        context = context.reshape(frames_count, heads_local * HD)
        partial_out = jnp.dot(context, full_out, preferred_element_type=jnp.float32)
        attended = lax.psum(partial_out.astype(jnp.bfloat16), "mp").astype(jnp.float32)
        result = (layer_input.astype(jnp.float32) + attended).astype(jnp.bfloat16)
        if step >= 1:
            valid = frame_ids < lengths[step - 1]
            summed = jnp.sum(
                jnp.where(valid[:, None], result.astype(jnp.float32), jnp.float32(0.0)), axis=0
            )
            pooled_rows.append(summed / lengths[step - 1].astype(jnp.float32))
        if step < count_utt:
            received = passed_along(result, "section", 1)
    pooled = jnp.stack(pooled_rows, axis=0)
    pooled = broadcast(pooled, "section", 1)
    return jnp.dot(
        lax.all_gather(pooled, "dp", axis=0, tiled=True) - center,
        whitening,
        precision=lax.Precision.HIGHEST,
        preferred_element_type=jnp.float32,
    )


def slice_of(row, index, count, size):
    value = jnp.zeros((1, size), F32)
    for part in range(count):
        value += jnp.where(index == part, row[:, part * size : (part + 1) * size], 0.0)
    return value


def three_parts(value):
    high = value.astype(BF16).astype(F32)
    rest = value - high
    middle = rest.astype(BF16).astype(F32)
    return high, middle, rest - middle


def whole_lanes(columns):
    return -(-columns // 128) * 128


def kernel(
    n,
    lengths_ref,
    frames_hbm,
    proj_hbm,
    gain_hbm,
    center_hbm,
    qkv_hbm,
    out_hbm,
    white_hbm,
    emb_ref,
    frames_ref,
    proj_ref,
    gain_ref,
    center_ref,
    wq,
    wq2,
    wo,
    wo2,
    wh,
    wh3,
    gsend,
    gsum,
    x0buf,
    xbuf,
    stat,
    normed,
    qkv,
    own,
    qsend,
    qrecv,
    sumsend,
    sumrecv,
    ctx,
    psend,
    precv,
    xnew,
    pool,
    rows,
    load_sem,
    x_send,
    x_recv,
    stat_send,
    stat_recv,
    g_send,
    g_recv,
    q_send,
    q_recv,
    sum_send,
    sum_recv,
    c_send,
    c_recv,
    p_send,
    p_recv,
    n_send,
    pool_send,
    pool_recv,
    row_send,
    row_recv,
):
    d = lax.axis_index("dp")
    s = lax.axis_index("section")
    m = lax.axis_index("mp")
    pieces, part_rows, lanes_x = xbuf.shape
    wide = wo.shape[1]
    frames_count = 2 * part_rows
    full = n * wide
    half = n // 2 * HD
    lanes_h = ctx.shape[3]
    pad_x, pad_h = lanes_x - wide, lanes_h - half
    groups = 2
    my_utt, my_half = d // 2, lax.rem(d, 2)
    pairs = (
        (frames_hbm, frames_ref),
        (proj_hbm, proj_ref.at[pl.ds(0, wide)]),
        (gain_hbm, gain_ref),
        (qkv_hbm, wq),
        (out_hbm, wo),
        (center_hbm, center_ref),
        (white_hbm, wh),
    )
    loads = [pltpu.make_async_copy(src, dst, load_sem.at[i]) for i, (src, dst) in enumerate(pairs)]
    for load in loads:
        load.start()

    barrier = pltpu.get_barrier_semaphore()
    for dz in range(n):
        for dm in range(n):
            if dz or dm:
                pl.semaphore_signal(
                    barrier, inc=1, device_id=(lax.rem(d + dz, n), s, lax.rem(m + dm, n)), device_id_type=MESH
                )
    for dm in range(n):
        pl.semaphore_signal(barrier, inc=1, device_id=(d, 1 - s, lax.rem(m + dm, n)), device_id_type=MESH)

    proj_ref[wide:] = jnp.zeros((pad_x, proj_ref.shape[1]), BF16)
    wq2[...] = jnp.zeros(wq2.shape, BF16)
    wo2[...] = jnp.zeros(wo2.shape, BF16)
    loads[0].wait()
    loads[1].wait()

    @pl.when(s == 0)
    def _():
        projected = lax.dot_general(
            frames_ref[0], proj_ref[...], (((1,), (1,)), ((), ())), preferred_element_type=F32
        ).astype(BF16)
        x0buf[0] = projected[:part_rows]
        x0buf[1] = projected[part_rows:]

    pl.semaphore_wait(barrier, n * n - 1 + n)

    def remote(src, dst, send, recv, target):
        return pltpu.make_async_remote_copy(
            src_ref=src, dst_ref=dst, send_sem=send, recv_sem=recv, device_id=target, device_id_type=MESH
        )

    def arrived(dst, recv):
        remote(dst, dst, x_send.at[0], recv, (d, s, m)).wait_recv()

    def above(k):
        return lax.rem(d + k, n), s, m

    def below(k):
        return lax.rem(d - k + n, n)

    sent = []

    def x0_copy(dm):
        return remote(
            x0buf, xbuf.at[pl.ds(2 * d, 2)], x_send.at[dm], x_recv.at[2 * d], (m, s, lax.rem(m + dm, n))
        )

    @pl.when(s == 0)
    def _():
        for dm in range(1, n):
            x0_copy(dm).start()

        @pl.when(d != m)
        def _():
            x0_copy(0).start()

        @pl.when(d == m)
        def _():
            xbuf[pl.ds(2 * d, 2)] = x0buf[...]

    loads[2].wait()
    gain = jnp.concatenate([slice_of(gain_ref, d, n, wide), jnp.zeros((1, pad_x), F32)], axis=1)
    ids = lax.broadcasted_iota(jnp.int32, (16, lanes_x), 0)
    gain_rows = jnp.zeros((16, lanes_x), F32)
    for part, value in enumerate(three_parts(gain)):
        gain_rows = jnp.where(ids == part, value, gain_rows)
    gain_rows = gain_rows.astype(BF16)
    loads[3].wait()

    @pl.loop(0, wide // 32)
    def _(step):
        run = pl.ds(pl.multiple_of(step * 32, 32), 32)
        for h in range(2):
            for t in range(3):
                start = (2 * t + h) * half
                wq2[h, run, t * lanes_h : t * lanes_h + half] = wq[run, start : start + half]

    @pl.loop(0, 2)
    def _(h):
        products = jnp.dot(gain_rows, wq2[h], preferred_element_type=F32)
        gsend[h] = products[0:1] + products[1:2] + products[2:3]
    gsum[d] = gsend[my_half]
    for k in range(1, n):
        copy = remote(gsend.at[lax.rem(d + k, 2)], gsum.at[d], g_send.at[k], g_recv.at[d], above(k))
        copy.start()
        sent.append(copy)

    loads[4].wait()
    for h in range(2):
        wo2[h, 0:half, 0:wide] = wo[h * half : (h + 1) * half]

    def split_whitening():
        loads[6].wait()
        for part in range(n):
            for i in range(3):
                wh3[i, part, wide:] = jnp.zeros((pad_x, wh3.shape[3]), BF16)

            @pl.loop(0, wide // 32)
            def _(step):
                source = pl.ds(pl.multiple_of(part * wide + step * 32, 32), 32)
                target = pl.ds(pl.multiple_of(step * 32, 32), 32)
                for i, value in enumerate(three_parts(wh[source])):
                    wh3[i, part, target] = value.astype(BF16)

    @pl.when(s == 1)
    def _():
        split_whitening()

    lanes = lax.broadcasted_iota(jnp.int32, (frames_count, 128), 1)
    length_row = 4
    real = lax.broadcasted_iota(jnp.int32, (frames_count, lanes_x), 1) < wide

    def q_copy(g):
        return remote(qsend.at[g], qrecv.at[g], q_send.at[g], q_recv.at[g], (d + 1 - 2 * my_half, s, m))

    def sum_copy(g):
        return remote(sumsend.at[g], sumrecv.at[g], sum_send.at[g], sum_recv.at[g], above(2))

    def stat_copy(g, k):
        return remote(stat.at[g, d], stat.at[g, d], stat_send.at[g, k], stat_recv.at[g, d], above(k))

    def project(g):
        for i in range(2):
            u = 2 * g + i

            @pl.when(jnp.logical_and(s == 0, jnp.logical_or(d != u, m != d)))
            def _():
                arrived(xbuf.at[pl.ds(2 * u, 2)], x_recv.at[2 * u])

            @pl.when(s == 1)
            def _():
                arrived(xbuf.at[2 * u], x_recv.at[2 * u])
                arrived(xbuf.at[2 * u + 1], x_recv.at[2 * u + 1])

        table = jnp.zeros((frames_count, 128), F32)
        for i in range(2):
            u = 2 * g + i
            x = jnp.concatenate([xbuf[2 * u], xbuf[2 * u + 1]], axis=0).astype(F32)
            mean = jnp.sum(x, axis=1, keepdims=True) * (1.0 / wide)
            centered = jnp.where(real, x - mean, 0.0)
            spread = jnp.sum(centered * centered, axis=1, keepdims=True)
            table = jnp.where(lanes == 2 * i, mean, table)
            table = jnp.where(lanes == 2 * i + 1, spread, table)
            normed[g, i * frames_count : (i + 1) * frames_count] = (centered * gain).astype(BF16)
        table = jnp.where(lanes == length_row, lengths_ref[0].astype(F32), table)
        partial = jnp.dot(normed[g], wq2[1 - my_half], preferred_element_type=F32).astype(BF16)
        for i in range(2):
            qsend[g, i] = partial[i * frames_count : (i + 1) * frames_count]
        q_copy(g).start()
        stat[g, d] = table.T[0:8]
        for k in range(1, n):
            stat_copy(g, k).start()
        kept = jnp.dot(normed[g], wq2[my_half], preferred_element_type=F32)
        for i in range(2):
            own[g, i] = kept[i * frames_count : (i + 1) * frames_count]

    def exchange(g):
        arrived(qrecv.at[g], q_recv.at[g])
        other = 1 - my_utt
        sumsend[g] = (own[g, other] + qrecv[g, other].astype(F32)).astype(BF16)
        sum_copy(g).start()
        own[g, my_utt] = own[g, my_utt] + qrecv[g, my_utt].astype(F32)

    stat_ids = lax.broadcasted_iota(jnp.int32, (8, 128), 0)
    columns = lax.broadcasted_iota(jnp.int32, (frames_count, lanes_h), 1)
    keys_ids = lax.broadcasted_iota(jnp.int32, (frames_count, frames_count), 1).astype(F32)

    def ctx_copy(g, k):
        return remote(ctx.at[g, d], ctx.at[g, d], c_send.at[g, k], c_recv.at[g, d], above(k))

    def attend(g):
        for k in range(1, n):
            arrived(stat.at[g, below(k)], stat_recv.at[g, below(k)])

        def stat_row(k, row):
            return jnp.sum(jnp.where(stat_ids == row, stat[g, k], 0.0), axis=0, keepdims=True)

        slice_means = [stat_row(k, 2 * my_utt) for k in range(n)]
        mean = sum(slice_means) * (1.0 / n)
        deltas = [value - mean for value in slice_means]
        spread = sum(stat_row(k, 2 * my_utt + 1) for k in range(n)) + wide * sum(value * value for value in deltas)
        rstd = lax.rsqrt(spread * (1.0 / full) + 1e-05)
        by_row = jnp.zeros((8, 128), F32)
        for k, value in enumerate(deltas + [rstd]):
            by_row = jnp.where(stat_ids == k, value, by_row)
        by_frame = jnp.concatenate([by_row, jnp.zeros((frames_count - 8, 128), F32)], axis=0).T
        length = stat[g, 2 * g + my_utt, length_row : length_row + 1, :]
        valid = keys_ids < length
        arrived(sumrecv.at[g], sum_recv.at[g])
        summed = own[g, my_utt] + sumrecv[g].astype(F32)
        for k in range(n):
            summed = summed + by_frame[:, k : k + 1] * gsum[k]
        qkv[g] = (summed * by_frame[:, n : n + 1]).astype(BF16)
        query = qkv[g, :, 0:lanes_h]
        keys = qkv[g, :, lanes_h : 2 * lanes_h]
        values = qkv[g, :, 2 * lanes_h : 3 * lanes_h]
        context = jnp.zeros((frames_count, lanes_h), F32)
        for h in range(half // HD):
            in_head = jnp.logical_and(columns >= h * HD, columns < (h + 1) * HD)
            head_query = jnp.where(in_head, query, jnp.zeros_like(query))
            head_values = jnp.where(in_head, values, jnp.zeros_like(values))
            scores = lax.dot_general(
                head_query, keys, (((1,), (1,)), ((), ())), preferred_element_type=F32
            ) / jnp.sqrt(F32(HD))
            scores = jnp.where(valid, scores, F32(-1e30))
            weights = jnp.exp(scores - jnp.max(scores, axis=1, keepdims=True))
            probs = (weights / jnp.sum(weights, axis=1, keepdims=True)).astype(BF16)
            context += jnp.dot(probs, head_values, preferred_element_type=F32)
        ctx[g, d] = context.astype(BF16)
        for k in (2, 1, 3):
            ctx_copy(g, k).start()

    def p_copy(g, to):
        return remote(psend.at[g, to], precv.at[g, m], p_send.at[g, to], p_recv.at[g, m], (d, s, to))

    def put_out(g):
        for i in range(2):
            total = jnp.zeros((frames_count, lanes_x), F32)
            for h in range(2):
                source = 2 * i + h

                @pl.when(d != source)
                def _():
                    arrived(ctx.at[g, source], c_recv.at[g, source])

                total += jnp.dot(ctx[g, source], wo2[h], preferred_element_type=F32)
            total = total.astype(BF16)
            for h in range(2):
                to = 2 * i + h
                psend[g, to] = total[h * part_rows : (h + 1) * part_rows]

                @pl.when(m != to)
                def _():
                    p_copy(g, to).start()

                @pl.when(m == to)
                def _():
                    precv[g, to] = psend[g, to]

    def next_copy(g, dm):
        return remote(
            xnew.at[g], xbuf.at[n * g + m], n_send.at[g, dm], x_recv.at[n * g + m], (d, 1, lax.rem(m + dm, n))
        )

    def pool_copy(g, ds, dm):
        return remote(
            pool.at[g, m],
            pool.at[g, m],
            pool_send.at[g, ds, dm],
            pool_recv.at[g, m],
            (d, lax.rem(s + ds, 2), lax.rem(m + dm, n)),
        )

    hops = [(ds, dm) for ds in range(2) for dm in range(n) if ds or dm]

    def finish(g):
        for k in range(1, n):
            source = lax.rem(m - k + n, n)
            arrived(precv.at[g, source], p_recv.at[g, source])
        attended = precv[g, 0].astype(F32)
        for k in range(1, n):
            attended = attended + precv[g, k].astype(F32)
        xnew[g] = (xbuf[n * g + m].astype(F32) + attended).astype(BF16)

        @pl.when(s == 0)
        def _():
            for dm in range(n):
                next_copy(g, dm).start()

        @pl.when(s == 1)
        def _():
            length = stat[g, 2 * g + m // 2, length_row : length_row + 1, :]
            frame = lax.broadcasted_iota(jnp.int32, (8, part_rows), 1) + part_rows * lax.rem(m, 2)
            weights = jnp.where(frame.astype(F32) < length[:, :part_rows], 1.0, 0.0).astype(BF16)
            pool[g, m] = jnp.dot(weights, xnew[g], preferred_element_type=F32)
            for ds, dm in hops:
                pool_copy(g, ds, dm).start()

    @pl.loop(0, groups + 1)
    def _(step):
        @pl.when(jnp.logical_and(step > 0, s == 1))
        def _():
            attend(step - 1)

        @pl.when(step < groups)
        def _():
            project(step)

        @pl.when(step == 0)
        def _():
            for k in range(1, n):
                arrived(gsum.at[below(k)], g_recv.at[below(k)])

        @pl.when(jnp.logical_and(step > 0, s == 0))
        def _():
            attend(step - 1)

        @pl.when(step < groups)
        def _():
            exchange(step)

        @pl.when(step > 0)
        def _():
            put_out(step - 1)
            finish(step - 1)

    @pl.when(s == 0)
    def _():
        split_whitening()

    loads[5].wait()
    row_ids = lax.broadcasted_iota(jnp.int32, (8, lanes_x), 0)
    gathered = jnp.zeros((8, lanes_x), F32)
    for u in range(n):
        g, i = u // 2, u % 2
        for source in (2 * i, 2 * i + 1):
            @pl.when(jnp.logical_or(s == 0, m != source))
            def _():
                arrived(pool.at[g, source], pool_recv.at[g, source])

        total = pool[g, 2 * i] + pool[g, 2 * i + 1]
        length = stat[g, u, length_row : length_row + 1, 0:1]
        gathered = jnp.where(row_ids == u, total / length, gathered)
    center = slice_of(center_ref[...].reshape(1, full), d, n, wide)
    rows[d] = gathered - jnp.concatenate([center, jnp.zeros((1, pad_x), F32)], axis=1)
    for k in range(1, n):
        copy = remote(rows.at[d], rows.at[d], row_send.at[k], row_recv.at[d], above(k))
        copy.start()
        sent.append(copy)
    for k in range(1, n):
        arrived(rows.at[below(k)], row_recv.at[below(k)])
    result = jnp.zeros((32, emb_ref.shape[1]), F32)
    for part in range(n):
        parts = jnp.concatenate(list(three_parts(rows[part])) + [jnp.zeros((8, lanes_x), F32)], axis=0).astype(BF16)
        for i in range(3):
            result += jnp.dot(
                parts, wh3[i, part], preferred_element_type=F32
            )
    result = result[0:8] + result[8:16] + result[16:24]
    emb_ref[...] = result[0:n]

    for copy in sent:
        copy.wait_send()
    for g in range(groups):
        for k in range(1, n):
            stat_copy(g, k).wait_send()
            ctx_copy(g, k).wait_send()
        q_copy(g).wait_send()
        sum_copy(g).wait_send()
        for to in range(n):
            @pl.when(m != to)
            def _():
                p_copy(g, to).wait_send()

    @pl.when(s == 0)
    def _():
        for dm in range(1, n):
            x0_copy(dm).wait_send()

        @pl.when(d != m)
        def _():
            x0_copy(0).wait_send()

        for g in range(groups):
            for dm in range(n):
                next_copy(g, dm).wait_send()

    @pl.when(s == 1)
    def _():
        for g in range(groups):
            for ds, dm in hops:
                pool_copy(g, ds, dm).wait_send()


def fused(n, frames, lengths, feature_proj, norm_gain, qkv_weight, out_weight, center, whitening):
    frames_count = frames.shape[1]
    wide = feature_proj.shape[1]
    qkv_cols = qkv_weight.shape[2]
    head_rows = out_weight.shape[1]
    out_cols = whitening.shape[1]
    rows, lanes_x, lanes_h = frames_count // 2, whole_lanes(wide), whole_lanes(head_rows // 2)
    columns = 3 * lanes_h
    vmem = pl.BlockSpec(memory_space=pltpu.VMEM)
    anywhere = pl.BlockSpec(memory_space=pl.ANY)
    dma = pltpu.SemaphoreType.DMA
    return pl.pallas_call(
        functools.partial(kernel, n),
        out_shape=jax.ShapeDtypeStruct((n, out_cols), F32),
        in_specs=[pl.BlockSpec(memory_space=pltpu.SMEM)] + [anywhere] * 7,
        out_specs=vmem,
        scratch_shapes=[
            pltpu.VMEM(frames.shape, BF16),
            pltpu.VMEM((lanes_x, feature_proj.shape[0]), BF16),
            pltpu.VMEM(norm_gain.shape, F32),
            pltpu.VMEM(center.shape, F32),
            pltpu.VMEM((wide, qkv_cols), BF16),
            pltpu.VMEM((2, lanes_x, columns), BF16),
            pltpu.VMEM((head_rows, wide), BF16),
            pltpu.VMEM((2, lanes_h, lanes_x), BF16),
            pltpu.VMEM((n * wide, out_cols), F32),
            pltpu.VMEM((3, n, lanes_x, out_cols), BF16),
            pltpu.VMEM((2, 1, columns), F32),
            pltpu.VMEM((n, 1, columns), F32),
            pltpu.VMEM((2, rows, lanes_x), BF16),
            pltpu.VMEM((2 * n, rows, lanes_x), BF16),
            pltpu.VMEM((2, n, 8, 128), F32),
            pltpu.VMEM((2, 2 * frames_count, lanes_x), BF16),
            pltpu.VMEM((2, frames_count, columns), BF16),
            pltpu.VMEM((2, 2, frames_count, columns), F32),
            pltpu.VMEM((2, 2, frames_count, columns), BF16),
            pltpu.VMEM((2, 2, frames_count, columns), BF16),
            pltpu.VMEM((2, frames_count, columns), BF16),
            pltpu.VMEM((2, frames_count, columns), BF16),
            pltpu.VMEM((2, n, frames_count, lanes_h), BF16),
            pltpu.VMEM((2, n, rows, lanes_x), BF16),
            pltpu.VMEM((2, n, rows, lanes_x), BF16),
            pltpu.VMEM((2, rows, lanes_x), BF16),
            pltpu.VMEM((2, n, 8, lanes_x), F32),
            pltpu.VMEM((n, 8, lanes_x), F32),
            dma((7,)),
            dma((n,)), dma((2 * n,)),
            dma((2, n)), dma((2, n)),
            dma((n,)), dma((n,)),
            dma((2,)), dma((2,)),
            dma((2,)), dma((2,)),
            dma((2, n)), dma((2, n)),
            dma((2, n)), dma((2, n)),
            dma((2, n)),
            dma((2, 2, n)), dma((2, n)),
            dma((n,)), dma((n,)),
        ],
        compiler_params=pltpu.CompilerParams(
            collective_id=0, has_side_effects=True, vmem_limit_bytes=60 * 1024 * 1024
        ),
    )(
        lengths,
        frames,
        feature_proj.T,
        norm_gain,
        center,
        qkv_weight.reshape(qkv_weight.shape[1:]),
        out_weight.reshape(out_weight.shape[1:]),
        whitening,
    )


def solution(mesh):
    in_specs = (
        P("dp", None, None),
        P("dp"),
        P(None, "mp"),
        P("section", None),
        P("section", "dp", "mp"),
        P("section", "mp", "dp"),
        P(),
        P(None, "dp"),
    )
    out_specs = P(None, "dp")

    def step(frames, lengths, feature_proj, norm_gain, qkv_weight, out_weight, center, whitening):
        n = mesh.shape["mp"]
        square = mesh.shape["dp"] == n and mesh.shape["section"] == 2
        square = square and n == 4 and frames.shape[0] == 1 and frames.shape[1] == 128
        square = square and qkv_weight.shape[2] == 3 * n * HD and qkv_weight.shape[1] == feature_proj.shape[1]
        if square:
            return fused(
                n, frames, lengths, feature_proj, norm_gain, qkv_weight, out_weight, center, whitening
            )
        return body(frames, lengths, feature_proj, norm_gain, qkv_weight, out_weight, center, whitening)

    return jax.shard_map(step, mesh=mesh, in_specs=in_specs, out_specs=out_specs, check_vma=False)
```

```python
import functools

import jax
import jax.numpy as jnp
from jax import lax
from jax.experimental import pallas as pl
from jax.experimental.pallas import tpu as pltpu
from jax.sharding import PartitionSpec as P

MESH = pl.DeviceIdType.MESH
BF16 = jnp.bfloat16
F32 = jnp.float32

HD = 120


def passed_along(x, axis, by):
    count = lax.axis_size(axis)
    pairs = [(i, i + by) for i in range(count) if 0 <= i + by < count]
    return lax.ppermute(x, axis, pairs)


def broadcast(value, axis, source):
    kept = jnp.where(lax.axis_index(axis) == source, value, 0).astype(value.dtype)
    return lax.psum(kept, axis)


def layer_norm(values, gain):
    mean = jnp.mean(values, axis=-1, keepdims=True)
    centered = values - mean
    var = jnp.mean(centered * centered, axis=-1, keepdims=True)
    return centered * lax.rsqrt(var + 1e-05) * gain


def body(frames, lengths, feature_proj, norm_gain, qkv_weight, out_weight, center, whitening):
    section_index = lax.axis_index("section")
    gain = norm_gain[0]
    qkv_local = qkv_weight[0]
    out_local = out_weight[0]
    count_utt = frames.shape[0]
    frames_count = frames.shape[1]
    width = gain.shape[0]
    qkv_cols = qkv_local.shape[1]
    heads_local = qkv_cols // (3 * HD)
    full_qkv, full_out = (
        lax.all_gather(qkv_local, "dp", axis=0, tiled=True),
        lax.all_gather(out_local, "dp", axis=1, tiled=True),
    )
    received = jnp.zeros((frames_count, width), jnp.bfloat16)
    pooled_rows = []
    frame_ids = jnp.arange(frames_count, dtype=jnp.int32)
    for step in range(count_utt + 1):
        first_mb = min(step, count_utt - 1)
        second_mb = max(step - 1, 0)
        projected_part = jnp.dot(
            frames[first_mb], feature_proj, preferred_element_type=jnp.float32
        ).astype(jnp.bfloat16)
        projected = lax.all_gather(projected_part, "mp", axis=1, tiled=True)
        first_section = section_index == 0
        layer_input = jnp.where(first_section, projected, received)
        length = jnp.where(first_section, lengths[first_mb], lengths[second_mb])
        normed = layer_norm(layer_input.astype(jnp.float32), gain).astype(jnp.bfloat16)
        qkv_sum = jnp.dot(normed, full_qkv, preferred_element_type=jnp.float32)
        qkv = qkv_sum.astype(jnp.bfloat16).reshape(frames_count, 3, heads_local, HD)
        query = qkv[:, 0]
        keys = qkv[:, 1]
        values = qkv[:, 2]
        scores = jnp.einsum(
            "qhd,khd->hqk", query, keys, preferred_element_type=jnp.float32
        ) / jnp.sqrt(jnp.float32(HD))
        attention_valid = jnp.arange(frames_count, dtype=jnp.int32) < length
        scores = jnp.where(attention_valid[None, None, :], scores, jnp.float32(-1e30))
        probs = jax.nn.softmax(scores, axis=-1).astype(jnp.bfloat16)
        context = jnp.einsum(
            "hqk,khd->qhd", probs, values, preferred_element_type=jnp.float32
        ).astype(jnp.bfloat16)
        context = context.reshape(frames_count, heads_local * HD)
        partial_out = jnp.dot(context, full_out, preferred_element_type=jnp.float32)
        attended = lax.psum(partial_out.astype(jnp.bfloat16), "mp").astype(jnp.float32)
        result = (layer_input.astype(jnp.float32) + attended).astype(jnp.bfloat16)
        if step >= 1:
            valid = frame_ids < lengths[step - 1]
            summed = jnp.sum(
                jnp.where(valid[:, None], result.astype(jnp.float32), jnp.float32(0.0)), axis=0
            )
            pooled_rows.append(summed / lengths[step - 1].astype(jnp.float32))
        if step < count_utt:
            received = passed_along(result, "section", 1)
    pooled = jnp.stack(pooled_rows, axis=0)
    pooled = broadcast(pooled, "section", 1)
    return jnp.dot(
        lax.all_gather(pooled, "dp", axis=0, tiled=True) - center,
        whitening,
        precision=lax.Precision.HIGHEST,
        preferred_element_type=jnp.float32,
    )


def slice_of(row, index, count, size):
    value = jnp.zeros((1, size), F32)
    for part in range(count):
        value += jnp.where(index == part, row[:, part * size : (part + 1) * size], 0.0)
    return value


def three_parts(value):
    high = value.astype(BF16).astype(F32)
    rest = value - high
    middle = rest.astype(BF16).astype(F32)
    return high, middle, rest - middle


def whole_lanes(columns):
    return -(-columns // 128) * 128


def kernel(
    n,
    lengths_ref,
    frames_hbm,
    proj_hbm,
    gain_hbm,
    center_hbm,
    qkv_hbm,
    out_hbm,
    white_hbm,
    emb_ref,
    frames_ref,
    proj_ref,
    gain_ref,
    center_ref,
    wq,
    wq2,
    wo,
    wo2,
    wh,
    wh3,
    gsend,
    gsum,
    x0buf,
    xbuf,
    stat,
    normed,
    qkv,
    own,
    qsend,
    qrecv,
    sumsend,
    sumrecv,
    ctx,
    psend,
    precv,
    xnew,
    pool,
    rows,
    load_sem,
    x_send,
    x_recv,
    stat_send,
    stat_recv,
    g_send,
    g_recv,
    q_send,
    q_recv,
    sum_send,
    sum_recv,
    c_send,
    c_recv,
    p_send,
    p_recv,
    n_send,
    pool_send,
    pool_recv,
    row_send,
    row_recv,
):
    d = lax.axis_index("dp")
    s = lax.axis_index("section")
    m = lax.axis_index("mp")
    pieces, part_rows, lanes_x = xbuf.shape
    wide = wo.shape[1]
    frames_count = 2 * part_rows
    full = n * wide
    half = n // 2 * HD
    lanes_h = ctx.shape[3]
    pad_x, pad_h = lanes_x - wide, lanes_h - half
    groups = 2
    my_utt, my_half = d // 2, lax.rem(d, 2)
    pairs = (
        (frames_hbm, frames_ref),
        (proj_hbm, proj_ref.at[pl.ds(0, wide)]),
        (gain_hbm, gain_ref),
        (qkv_hbm, wq),
        (out_hbm, wo),
        (center_hbm, center_ref),
        (white_hbm, wh),
    )
    loads = [pltpu.make_async_copy(src, dst, load_sem.at[i]) for i, (src, dst) in enumerate(pairs)]
    for load in loads:
        load.start()

    barrier = pltpu.get_barrier_semaphore()
    for dz in range(n):
        for dm in range(n):
            if dz or dm:
                pl.semaphore_signal(
                    barrier, inc=1, device_id=(lax.rem(d + dz, n), s, lax.rem(m + dm, n)), device_id_type=MESH
                )
    for dm in range(n):
        pl.semaphore_signal(barrier, inc=1, device_id=(d, 1 - s, lax.rem(m + dm, n)), device_id_type=MESH)

    proj_ref[wide:] = jnp.zeros((pad_x, proj_ref.shape[1]), BF16)
    loads[0].wait()
    loads[1].wait()

    @pl.when(s == 0)
    def _():
        projected = lax.dot_general(
            frames_ref[0], proj_ref[...], (((1,), (1,)), ((), ())), preferred_element_type=F32
        ).astype(BF16)
        x0buf[0] = projected[:part_rows]
        x0buf[1] = projected[part_rows:]

    pl.semaphore_wait(barrier, n * n - 1 + n)

    def remote(src, dst, send, recv, target):
        return pltpu.make_async_remote_copy(
            src_ref=src, dst_ref=dst, send_sem=send, recv_sem=recv, device_id=target, device_id_type=MESH
        )

    def arrived(dst, recv):
        remote(dst, dst, x_send.at[0], recv, (d, s, m)).wait_recv()

    def above(k):
        return lax.rem(d + k, n), s, m

    def below(k):
        return lax.rem(d - k + n, n)

    sent = []

    def x0_copy(dm):
        return remote(
            x0buf, xbuf.at[pl.ds(2 * d, 2)], x_send.at[dm], x_recv.at[2 * d], (m, s, lax.rem(m + dm, n))
        )

    @pl.when(s == 0)
    def _():
        for dm in range(1, n):
            x0_copy(dm).start()

        @pl.when(d != m)
        def _():
            x0_copy(0).start()

        @pl.when(d == m)
        def _():
            xbuf[pl.ds(2 * d, 2)] = x0buf[...]

    wq2[...] = jnp.zeros(wq2.shape, BF16)
    wo2[...] = jnp.zeros(wo2.shape, BF16)
    loads[2].wait()
    gain = jnp.concatenate([slice_of(gain_ref, d, n, wide), jnp.zeros((1, pad_x), F32)], axis=1)
    ids = lax.broadcasted_iota(jnp.int32, (16, lanes_x), 0)
    gain_rows = jnp.zeros((16, lanes_x), F32)
    for part, value in enumerate(three_parts(gain)):
        gain_rows = jnp.where(ids == part, value, gain_rows)
    gain_rows = gain_rows.astype(BF16)
    loads[3].wait()

    @pl.loop(0, wide // 32)
    def _(step):
        run = pl.ds(pl.multiple_of(step * 32, 32), 32)
        for h in range(2):
            for t in range(3):
                start = (2 * t + h) * half
                wq2[h, run, t * lanes_h : t * lanes_h + half] = wq[run, start : start + half]

    @pl.loop(0, 2)
    def _(h):
        products = jnp.dot(gain_rows, wq2[h], preferred_element_type=F32)
        gsend[h] = products[0:1] + products[1:2] + products[2:3]
    gsum[d] = gsend[my_half]
    for k in range(1, n):
        copy = remote(gsend.at[lax.rem(d + k, 2)], gsum.at[d], g_send.at[k], g_recv.at[d], above(k))
        copy.start()
        sent.append(copy)

    loads[4].wait()
    for h in range(2):
        wo2[h, 0:half, 0:wide] = wo[h * half : (h + 1) * half]

    def split_whitening():
        loads[6].wait()
        for part in range(n):
            for i in range(3):
                wh3[i, part, wide:] = jnp.zeros((pad_x, wh3.shape[3]), BF16)

            @pl.loop(0, wide // 32)
            def _(step):
                source = pl.ds(pl.multiple_of(part * wide + step * 32, 32), 32)
                target = pl.ds(pl.multiple_of(step * 32, 32), 32)
                for i, value in enumerate(three_parts(wh[source])):
                    wh3[i, part, target] = value.astype(BF16)

    @pl.when(s == 1)
    def _():
        split_whitening()

    lanes = lax.broadcasted_iota(jnp.int32, (frames_count, 128), 1)
    length_row = 4
    real = lax.broadcasted_iota(jnp.int32, (frames_count, lanes_x), 1) < wide

    def q_copy(g):
        return remote(qsend.at[g], qrecv.at[g], q_send.at[g], q_recv.at[g], (d + 1 - 2 * my_half, s, m))

    def sum_copy(g):
        return remote(sumsend.at[g], sumrecv.at[g], sum_send.at[g], sum_recv.at[g], above(2))

    def stat_copy(g, k):
        return remote(stat.at[g, d], stat.at[g, d], stat_send.at[g, k], stat_recv.at[g, d], above(k))

    def project(g):
        for i in range(2):
            u = 2 * g + i

            @pl.when(jnp.logical_and(s == 0, jnp.logical_or(d != u, m != d)))
            def _():
                arrived(xbuf.at[pl.ds(2 * u, 2)], x_recv.at[2 * u])

            @pl.when(s == 1)
            def _():
                arrived(xbuf.at[2 * u], x_recv.at[2 * u])
                arrived(xbuf.at[2 * u + 1], x_recv.at[2 * u + 1])

        table = jnp.zeros((frames_count, 128), F32)
        for i in range(2):
            u = 2 * g + i
            x = jnp.concatenate([xbuf[2 * u], xbuf[2 * u + 1]], axis=0).astype(F32)
            mean = jnp.sum(x, axis=1, keepdims=True) * (1.0 / wide)
            centered = jnp.where(real, x - mean, 0.0)
            spread = jnp.sum(centered * centered, axis=1, keepdims=True)
            table = jnp.where(lanes == 2 * i, mean, table)
            table = jnp.where(lanes == 2 * i + 1, spread, table)
            normed[g, i * frames_count : (i + 1) * frames_count] = (centered * gain).astype(BF16)
        table = jnp.where(lanes == length_row, lengths_ref[0].astype(F32), table)
        partial = jnp.dot(normed[g], wq2[1 - my_half], preferred_element_type=F32).astype(BF16)
        for i in range(2):
            qsend[g, i] = partial[i * frames_count : (i + 1) * frames_count]
        q_copy(g).start()
        stat[g, d] = table.T[0:8]
        for k in range(1, n):
            stat_copy(g, k).start()
        kept = jnp.dot(normed[g], wq2[my_half], preferred_element_type=F32)
        for i in range(2):
            own[g, i] = kept[i * frames_count : (i + 1) * frames_count]

    def exchange(g):
        arrived(qrecv.at[g], q_recv.at[g])
        other = 1 - my_utt
        sumsend[g] = (own[g, other] + qrecv[g, other].astype(F32)).astype(BF16)
        sum_copy(g).start()
        own[g, my_utt] = own[g, my_utt] + qrecv[g, my_utt].astype(F32)

    stat_ids = lax.broadcasted_iota(jnp.int32, (8, 128), 0)
    columns = lax.broadcasted_iota(jnp.int32, (frames_count, lanes_h), 1)
    keys_ids = lax.broadcasted_iota(jnp.int32, (frames_count, frames_count), 1).astype(F32)

    def ctx_copy(g, k):
        return remote(ctx.at[g, d], ctx.at[g, d], c_send.at[g, k], c_recv.at[g, d], above(k))

    def attend(g):
        for k in range(1, n):
            arrived(stat.at[g, below(k)], stat_recv.at[g, below(k)])

        def stat_row(k, row):
            return jnp.sum(jnp.where(stat_ids == row, stat[g, k], 0.0), axis=0, keepdims=True)

        slice_means = [stat_row(k, 2 * my_utt) for k in range(n)]
        mean = sum(slice_means) * (1.0 / n)
        deltas = [value - mean for value in slice_means]
        spread = sum(stat_row(k, 2 * my_utt + 1) for k in range(n)) + wide * sum(value * value for value in deltas)
        rstd = lax.rsqrt(spread * (1.0 / full) + 1e-05)
        by_row = jnp.zeros((8, 128), F32)
        for k, value in enumerate(deltas + [rstd]):
            by_row = jnp.where(stat_ids == k, value, by_row)
        by_frame = jnp.concatenate([by_row, jnp.zeros((frames_count - 8, 128), F32)], axis=0).T
        length = stat[g, 2 * g + my_utt, length_row : length_row + 1, :]
        valid = keys_ids < length
        arrived(sumrecv.at[g], sum_recv.at[g])
        summed = own[g, my_utt] + sumrecv[g].astype(F32)
        for k in range(n):
            summed = summed + by_frame[:, k : k + 1] * gsum[k]
        qkv[g] = (summed * by_frame[:, n : n + 1]).astype(BF16)
        query = qkv[g, :, 0:lanes_h]
        keys = qkv[g, :, lanes_h : 2 * lanes_h]
        values = qkv[g, :, 2 * lanes_h : 3 * lanes_h]
        context = jnp.zeros((frames_count, lanes_h), F32)
        for h in range(half // HD):
            in_head = jnp.logical_and(columns >= h * HD, columns < (h + 1) * HD)
            head_query = jnp.where(in_head, query, jnp.zeros_like(query))
            head_values = jnp.where(in_head, values, jnp.zeros_like(values))
            scores = lax.dot_general(
                head_query, keys, (((1,), (1,)), ((), ())), preferred_element_type=F32
            ) / jnp.sqrt(F32(HD))
            scores = jnp.where(valid, scores, F32(-1e30))
            weights = jnp.exp(scores - jnp.max(scores, axis=1, keepdims=True))
            probs = (weights / jnp.sum(weights, axis=1, keepdims=True)).astype(BF16)
            context += jnp.dot(probs, head_values, preferred_element_type=F32)
        ctx[g, d] = context.astype(BF16)
        for k in (2, 1, 3):
            ctx_copy(g, k).start()

    def p_copy(g, to):
        return remote(psend.at[g, to], precv.at[g, m], p_send.at[g, to], p_recv.at[g, m], (d, s, to))

    def put_out(g):
        for i in range(2):
            total = jnp.zeros((frames_count, lanes_x), F32)
            for h in range(2):
                source = 2 * i + h

                @pl.when(d != source)
                def _():
                    arrived(ctx.at[g, source], c_recv.at[g, source])

                total += jnp.dot(ctx[g, source], wo2[h], preferred_element_type=F32)
            total = total.astype(BF16)
            for h in range(2):
                to = 2 * i + h
                psend[g, to] = total[h * part_rows : (h + 1) * part_rows]

                @pl.when(m != to)
                def _():
                    p_copy(g, to).start()

                @pl.when(m == to)
                def _():
                    precv[g, to] = psend[g, to]

    def next_copy(g, dm):
        return remote(
            xnew.at[g], xbuf.at[n * g + m], n_send.at[g, dm], x_recv.at[n * g + m], (d, 1, lax.rem(m + dm, n))
        )

    def pool_copy(g, ds, dm):
        return remote(
            pool.at[g, m],
            pool.at[g, m],
            pool_send.at[g, ds, dm],
            pool_recv.at[g, m],
            (d, lax.rem(s + ds, 2), lax.rem(m + dm, n)),
        )

    hops = [(ds, dm) for ds in range(2) for dm in range(n) if ds or dm]

    def finish(g):
        for k in range(1, n):
            source = lax.rem(m - k + n, n)
            arrived(precv.at[g, source], p_recv.at[g, source])
        attended = precv[g, 0].astype(F32)
        for k in range(1, n):
            attended = attended + precv[g, k].astype(F32)
        xnew[g] = (xbuf[n * g + m].astype(F32) + attended).astype(BF16)

        @pl.when(s == 0)
        def _():
            for dm in range(n):
                next_copy(g, dm).start()

        @pl.when(s == 1)
        def _():
            length = stat[g, 2 * g + m // 2, length_row : length_row + 1, :]
            frame = lax.broadcasted_iota(jnp.int32, (8, part_rows), 1) + part_rows * lax.rem(m, 2)
            weights = jnp.where(frame.astype(F32) < length[:, :part_rows], 1.0, 0.0).astype(BF16)
            pool[g, m] = jnp.dot(weights, xnew[g], preferred_element_type=F32)
            for ds, dm in hops:
                pool_copy(g, ds, dm).start()

    @pl.loop(0, groups + 1)
    def _(step):
        @pl.when(jnp.logical_and(step > 0, s == 1))
        def _():
            attend(step - 1)

        @pl.when(step < groups)
        def _():
            project(step)

        @pl.when(step == 0)
        def _():
            for k in range(1, n):
                arrived(gsum.at[below(k)], g_recv.at[below(k)])

        @pl.when(jnp.logical_and(step > 0, s == 0))
        def _():
            attend(step - 1)

        @pl.when(step < groups)
        def _():
            exchange(step)

        @pl.when(step > 0)
        def _():
            put_out(step - 1)
            finish(step - 1)

    @pl.when(s == 0)
    def _():
        split_whitening()

    loads[5].wait()
    row_ids = lax.broadcasted_iota(jnp.int32, (8, lanes_x), 0)
    gathered = jnp.zeros((8, lanes_x), F32)
    for u in range(n):
        g, i = u // 2, u % 2
        for source in (2 * i, 2 * i + 1):
            @pl.when(jnp.logical_or(s == 0, m != source))
            def _():
                arrived(pool.at[g, source], pool_recv.at[g, source])

        total = pool[g, 2 * i] + pool[g, 2 * i + 1]
        length = stat[g, u, length_row : length_row + 1, 0:1]
        gathered = jnp.where(row_ids == u, total / length, gathered)
    center = slice_of(center_ref[...].reshape(1, full), d, n, wide)
    rows[d] = gathered - jnp.concatenate([center, jnp.zeros((1, pad_x), F32)], axis=1)
    for k in range(1, n):
        copy = remote(rows.at[d], rows.at[d], row_send.at[k], row_recv.at[d], above(k))
        copy.start()
        sent.append(copy)
    for k in range(1, n):
        arrived(rows.at[below(k)], row_recv.at[below(k)])
    result = jnp.zeros((32, emb_ref.shape[1]), F32)
    for part in range(n):
        parts = jnp.concatenate(list(three_parts(rows[part])) + [jnp.zeros((8, lanes_x), F32)], axis=0).astype(BF16)
        for i in range(3):
            result += jnp.dot(
                parts, wh3[i, part], preferred_element_type=F32
            )
    result = result[0:8] + result[8:16] + result[16:24]
    emb_ref[...] = result[0:n]

    for copy in sent:
        copy.wait_send()
    for g in range(groups):
        for k in range(1, n):
            stat_copy(g, k).wait_send()
            ctx_copy(g, k).wait_send()
        q_copy(g).wait_send()
        sum_copy(g).wait_send()
        for to in range(n):
            @pl.when(m != to)
            def _():
                p_copy(g, to).wait_send()

    @pl.when(s == 0)
    def _():
        for dm in range(1, n):
            x0_copy(dm).wait_send()

        @pl.when(d != m)
        def _():
            x0_copy(0).wait_send()

        for g in range(groups):
            for dm in range(n):
                next_copy(g, dm).wait_send()

    @pl.when(s == 1)
    def _():
        for g in range(groups):
            for ds, dm in hops:
                pool_copy(g, ds, dm).wait_send()


def fused(n, frames, lengths, feature_proj, norm_gain, qkv_weight, out_weight, center, whitening):
    frames_count = frames.shape[1]
    wide = feature_proj.shape[1]
    qkv_cols = qkv_weight.shape[2]
    head_rows = out_weight.shape[1]
    out_cols = whitening.shape[1]
    rows, lanes_x, lanes_h = frames_count // 2, whole_lanes(wide), whole_lanes(head_rows // 2)
    columns = 3 * lanes_h
    vmem = pl.BlockSpec(memory_space=pltpu.VMEM)
    anywhere = pl.BlockSpec(memory_space=pl.ANY)
    dma = pltpu.SemaphoreType.DMA
    return pl.pallas_call(
        functools.partial(kernel, n),
        out_shape=jax.ShapeDtypeStruct((n, out_cols), F32),
        in_specs=[pl.BlockSpec(memory_space=pltpu.SMEM)] + [anywhere] * 7,
        out_specs=vmem,
        scratch_shapes=[
            pltpu.VMEM(frames.shape, BF16),
            pltpu.VMEM((lanes_x, feature_proj.shape[0]), BF16),
            pltpu.VMEM(norm_gain.shape, F32),
            pltpu.VMEM(center.shape, F32),
            pltpu.VMEM((wide, qkv_cols), BF16),
            pltpu.VMEM((2, lanes_x, columns), BF16),
            pltpu.VMEM((head_rows, wide), BF16),
            pltpu.VMEM((2, lanes_h, lanes_x), BF16),
            pltpu.VMEM((n * wide, out_cols), F32),
            pltpu.VMEM((3, n, lanes_x, out_cols), BF16),
            pltpu.VMEM((2, 1, columns), F32),
            pltpu.VMEM((n, 1, columns), F32),
            pltpu.VMEM((2, rows, lanes_x), BF16),
            pltpu.VMEM((2 * n, rows, lanes_x), BF16),
            pltpu.VMEM((2, n, 8, 128), F32),
            pltpu.VMEM((2, 2 * frames_count, lanes_x), BF16),
            pltpu.VMEM((2, frames_count, columns), BF16),
            pltpu.VMEM((2, 2, frames_count, columns), F32),
            pltpu.VMEM((2, 2, frames_count, columns), BF16),
            pltpu.VMEM((2, 2, frames_count, columns), BF16),
            pltpu.VMEM((2, frames_count, columns), BF16),
            pltpu.VMEM((2, frames_count, columns), BF16),
            pltpu.VMEM((2, n, frames_count, lanes_h), BF16),
            pltpu.VMEM((2, n, rows, lanes_x), BF16),
            pltpu.VMEM((2, n, rows, lanes_x), BF16),
            pltpu.VMEM((2, rows, lanes_x), BF16),
            pltpu.VMEM((2, n, 8, lanes_x), F32),
            pltpu.VMEM((n, 8, lanes_x), F32),
            dma((7,)),
            dma((n,)), dma((2 * n,)),
            dma((2, n)), dma((2, n)),
            dma((n,)), dma((n,)),
            dma((2,)), dma((2,)),
            dma((2,)), dma((2,)),
            dma((2, n)), dma((2, n)),
            dma((2, n)), dma((2, n)),
            dma((2, n)),
            dma((2, 2, n)), dma((2, n)),
            dma((n,)), dma((n,)),
        ],
        compiler_params=pltpu.CompilerParams(
            collective_id=0, has_side_effects=True, vmem_limit_bytes=60 * 1024 * 1024
        ),
    )(
        lengths,
        frames,
        feature_proj.T,
        norm_gain,
        center,
        qkv_weight.reshape(qkv_weight.shape[1:]),
        out_weight.reshape(out_weight.shape[1:]),
        whitening,
    )


def solution(mesh):
    in_specs = (
        P("dp", None, None),
        P("dp"),
        P(None, "mp"),
        P("section", None),
        P("section", "dp", "mp"),
        P("section", "mp", "dp"),
        P(),
        P(None, "dp"),
    )
    out_specs = P(None, "dp")

    def step(frames, lengths, feature_proj, norm_gain, qkv_weight, out_weight, center, whitening):
        n = mesh.shape["mp"]
        square = mesh.shape["dp"] == n and mesh.shape["section"] == 2
        square = square and n == 4 and frames.shape[0] == 1 and frames.shape[1] == 128
        square = square and qkv_weight.shape[2] == 3 * n * HD and qkv_weight.shape[1] == feature_proj.shape[1]
        if square:
            return fused(
                n, frames, lengths, feature_proj, norm_gain, qkv_weight, out_weight, center, whitening
            )
        return body(frames, lengths, feature_proj, norm_gain, qkv_weight, out_weight, center, whitening)

    return jax.shard_map(step, mesh=mesh, in_specs=in_specs, out_specs=out_specs, check_vma=False)
```
